128 devices in a mesh: row: 8 (over y, core), col: 16 (over x, z).
Axes of the slice: x: 4, y: 4, z: 4, core: 2. Of those that a mesh axis runs over, the one named last changes fastest.
Arguments:
- x_paper: bfloat16 [32768, 768], P(('row', 'col')), may hold values from -6 to 6
- x_author: bfloat16 [32768, 768], P(('row', 'col')), may hold values from -6 to 6
- cite_nbr: int32 [32768, 16], P(('row', 'col')), may hold values from -1 to 4095, as said below
- write_src: int32 [128, 128, 4], P(('row', 'col')), may hold values from -1 to 255, as said below
- write_dst: int32 [128, 128, 4], P(('row', 'col')), may hold values from -1 to 255, as said below
- w_self_paper: bfloat16 [768, 1024], replicated, may hold values from -0.21875 to 0.21875
- w_cite: bfloat16 [768, 1024], replicated, may hold values from -0.21875 to 0.21875
- w_write: bfloat16 [768, 1024], replicated, may hold values from -0.21875 to 0.21875
- w_self_author: bfloat16 [768, 1024], replicated, may hold values from -0.21875 to 0.21875
- w_written: bfloat16 [768, 1024], replicated, may hold values from -0.21875 to 0.21875
- grad_paper: bfloat16 [32768, 1024], P(('row', 'col')), may hold values from -24 to 24
- grad_author: bfloat16 [32768, 1024], P(('row', 'col')), may hold values from -24 to 24
Outputs:
- out_paper: bfloat16 [32768, 1024], P(('row', 'col'))
- out_author: bfloat16 [32768, 1024], P(('row', 'col'))
- dx_paper: bfloat16 [32768, 768], P(('row', 'col'))
- dx_author: bfloat16 [32768, 768], P(('row', 'col'))
- dweights: float32 [5, 768, 1024], P(None, 'row', 'col')
The draws below stay inside these ranges and needn't reach their ends.
Inputs may be any that keep to these rules, and one draw needn't show every extreme that they name: `cite_nbr`: entries of a row that are -1 stand for no citation and come after all others; a value e >= 0 names the paper at position e of the paper's own block row. Some paper has all 16 entries. write_src[s, d, j] is -1 (empty slot) exactly where write_dst[d, s, j] is -1; otherwise it is an author position on device s. Some device d has every slot from every device s filled. write_dst[d, s, j] is -1 exactly where write_src[s, d, j] is -1; otherwise it is a paper position on device d. A paper may have several edges, also from one author.
All inputs are finite; a program needn't handle non-finite values.
Results may differ from the reference program's by a relative error of at most 0.0054.
Values may be sent and summed in bfloat16 or wider, within the bound.
No kernel may reach another device: no remote copies, remote signals or barrier semaphores. Data moves between devices by JAX's collectives and lax.ppermute only.
A program may use at most 192 MiB of HBM per device.

```python
import jax
import jax.numpy as jnp
from jax import lax

D_IN = 768
D_OUT = 1024
P_DEV = 256
A_DEV = 256
CAP = 4
K_CITE = 16
PAPERS = 32768
AUTHORS = 32768
ROW_PAPERS = 4096
N_ROW = 8
DEVICES = 128


def write_common(key):
    keys = jax.random.split(key, 5)
    chance = jax.random.randint(keys[0], (DEVICES, 1, 1), 20, 96)
    roll = jax.random.randint(keys[1], (DEVICES, DEVICES, CAP), 0, 100)
    chosen = jax.random.randint(keys[2], (), 0, DEVICES)
    receiver = jnp.arange(DEVICES, dtype=jnp.int32)[:, None, None]
    sender = jnp.arange(DEVICES, dtype=jnp.int32)[None, :, None]
    position = jnp.arange(CAP, dtype=jnp.int32)[None, None, :]
    live = (roll < chance) | (receiver == chosen)
    corner = (receiver == chosen) & (sender == 0) & (position == 0)
    paper_pos = jax.random.randint(keys[3], (DEVICES, DEVICES, CAP), 0, P_DEV)
    author_pos = jax.random.randint(keys[4], (DEVICES, DEVICES, CAP), 0, A_DEV)
    paper_pos = jnp.where(corner, P_DEV - 1, paper_pos)
    author_pos = jnp.where(corner, A_DEV - 1, author_pos)
    return (live, paper_pos, author_pos)


def draw_write_dst(key, part):
    live, paper_pos, author_pos = write_common(key)
    return jnp.where(live, paper_pos, -1).astype(jnp.int32)


def draw_write_src(key, part):
    live, paper_pos, author_pos = write_common(key)
    return jnp.transpose(jnp.where(live, author_pos, -1), (1, 0, 2)).astype(jnp.int32)


def draw_cite_nbr(key, part):
    key = jax.random.fold_in(key, 11)
    keys = jax.random.split(key, 5)
    blocks = ROW_PAPERS // P_DEV
    rows = jnp.arange(PAPERS, dtype=jnp.int32)
    counts = jax.random.randint(keys[0], (PAPERS,), 0, K_CITE + 1)
    chosen = jax.random.randint(keys[1], (), 0, PAPERS)
    counts = jnp.where(rows == chosen, K_CITE, counts)
    own_block = rows // P_DEV % blocks
    stay = jax.random.randint(keys[2], (PAPERS, K_CITE), 0, 2)
    other = jax.random.randint(keys[3], (PAPERS, K_CITE), 0, blocks)
    block_id = jnp.where(stay == 0, own_block[:, None], other)
    offset = jax.random.randint(keys[4], (PAPERS, K_CITE), 0, P_DEV)
    entries = block_id * P_DEV + offset
    first = (rows[:, None] == chosen) & (jnp.arange(K_CITE, dtype=jnp.int32)[None, :] == 0)
    entries = jnp.where(first, ROW_PAPERS - 1, entries)
    valid = jnp.arange(K_CITE, dtype=jnp.int32)[None, :] < counts[:, None]
    return jnp.where(valid, entries, -1).astype(jnp.int32)


def spiked(values, own_key, source, target, shards_of, factor):
    def block_of(axis_at):
        return (jnp.arange(values.shape[axis_at]) // (values.shape[axis_at] // shards_of)).reshape((-1,) + (1,) * (values.ndim - 1 - axis_at))

    first = jax.random.permutation(own_key, shards_of)[block_of(target)]
    second = (block_of(target) + shards_of // 2) % shards_of
    return jnp.where((block_of(source) == first) | (block_of(source) == second), factor * values, values)


def steps_of(key, shape, shards, low, high):
    def one(axis_at, blocks):
        heights = jax.random.uniform(jax.random.fold_in(jax.random.fold_in(key, 6), axis_at), (blocks,), jnp.float32, low / len(shards), high / len(shards))
        return jnp.repeat(jnp.exp(heights), shape[axis_at] // blocks).reshape((-1,) + (1,) * (len(shape) - axis_at - 1))

    level = one(*shards[0])
    for cut in shards[1:]:
        level = level * one(*cut)
    return level


def normal_values(own_key, dims, width, bound, shards=(), kind=jnp.bfloat16):
    values = jax.random.normal(own_key, dims, jnp.float32) * width
    if len(shards) > 0:
        values = steps_of(own_key, dims, shards, -0.22, 0.18) * values
    return jnp.clip(values, min=-bound, max=bound).astype(kind)


def noise_with(stream_key, dims, width, limit, shards, heavy, kind=jnp.bfloat16):
    drawn = width * jax.random.normal(stream_key, dims, jnp.float32)
    if shards:
        drawn = drawn * steps_of(stream_key, dims, shards, -0.22, 0.18)
    return jnp.clip(spiked(drawn, jax.random.fold_in(stream_key, 3), *heavy), -limit, limit).astype(kind)


def setup_inputs(seed: int = 0) -> dict:
    key_of = jax.random.split(jax.random.key(seed), 13)
    return {
        "x_paper": normal_values(key_of[0], (PAPERS, D_IN), 1.0, 6.0, ((0, 128),)),
        "x_author": normal_values(key_of[1], (AUTHORS, D_IN), 1.0, 6.0, ((0, 128),)),
        "cite_nbr": draw_cite_nbr(jax.random.fold_in(key_of[12], 71), 0),
        "write_src": draw_write_src(jax.random.fold_in(key_of[12], 71), 0),
        "write_dst": draw_write_dst(jax.random.fold_in(key_of[12], 71), 0),
        "w_self_paper": normal_values(key_of[5], (D_IN, D_OUT), D_IN ** -0.5, 0.21875),
        "w_cite": normal_values(key_of[6], (D_IN, D_OUT), D_IN ** -0.5, 0.21875),
        "w_write": normal_values(key_of[7], (D_IN, D_OUT), D_IN ** -0.5, 0.21875),
        "w_self_author": normal_values(key_of[8], (D_IN, D_OUT), D_IN ** -0.5, 0.21875),
        "w_written": normal_values(key_of[9], (D_IN, D_OUT), D_IN ** -0.5, 0.21875),
        "grad_paper": noise_with(key_of[10], (PAPERS, D_OUT), 1.0, 24.0, ((0, 128),), (0, 1, 128, 5.5)),
        "grad_author": noise_with(key_of[11], (AUTHORS, D_OUT), 1.0, 24.0, ((0, 128),), (0, 1, 128, 5.5)),
    }


def authors_to_papers(values, write_src, write_dst):
    src_by_dst = jnp.transpose(write_src, (1, 0, 2))
    offsets = (jnp.arange(DEVICES, dtype=jnp.int32) * A_DEV)[:, None]

    def one_device(pair):
        src_row, dst_row = pair
        live = dst_row >= 0
        index = (offsets + jnp.maximum(src_row, 0)).reshape(-1)
        picked = values[index].astype(jnp.float32) * live.reshape(-1, 1).astype(jnp.float32)
        target = jnp.where(live, dst_row, P_DEV).reshape(-1)
        return jax.ops.segment_sum(picked, target, P_DEV + 1)[:P_DEV]

    result = lax.map(one_device, (src_by_dst, write_dst))
    return result.reshape(PAPERS, -1)


def papers_to_authors(values, write_src, write_dst):
    dst_by_src = jnp.transpose(write_dst, (1, 0, 2))
    offsets = (jnp.arange(DEVICES, dtype=jnp.int32) * P_DEV)[:, None]

    def one_device(pair):
        dst_row, src_row = pair
        live = src_row >= 0
        index = (offsets + jnp.maximum(dst_row, 0)).reshape(-1)
        picked = values[index].astype(jnp.float32) * live.reshape(-1, 1).astype(jnp.float32)
        target = jnp.where(live, src_row, A_DEV).reshape(-1)
        return jax.ops.segment_sum(picked, target, A_DEV + 1)[:A_DEV]

    result = lax.map(one_device, (dst_by_src, write_src))
    return result.reshape(AUTHORS, -1)


def cite_forward(values, cite_nbr):
    groups = values.reshape(N_ROW, ROW_PAPERS, -1)
    lists = cite_nbr.reshape(N_ROW, ROW_PAPERS, K_CITE)

    def one_group(pair):
        block, entries = pair
        live = (entries >= 0).astype(jnp.float32)
        where_from = jnp.maximum(entries, 0)
        accum = jnp.zeros((ROW_PAPERS, block.shape[1]), jnp.float32)
        for slot in range(K_CITE):
            accum = accum + block[where_from[:, slot]].astype(jnp.float32) * live[:, slot:slot + 1]
        return accum

    return lax.map(one_group, (groups, lists)).reshape(PAPERS, -1)


def cite_backward(values, cite_nbr):
    groups = values.reshape(N_ROW, ROW_PAPERS, -1)
    lists = cite_nbr.reshape(N_ROW, ROW_PAPERS, K_CITE)

    def one_group(pair):
        block, entries = pair
        live = (entries >= 0).astype(jnp.float32)
        where_to = jnp.maximum(entries, 0)
        accum = jnp.zeros((ROW_PAPERS, block.shape[1]), jnp.float32)
        for slot in range(K_CITE):
            accum = accum.at[where_to[:, slot]].add(block.astype(jnp.float32) * live[:, slot:slot + 1])
        return accum

    return lax.map(one_group, (groups, lists)).reshape(PAPERS, -1)


def silu_slope(value):
    sigma = jax.nn.sigmoid(value)
    return sigma * (1.0 + value * (1.0 - sigma))


def project_back(delta, weight):
    return jnp.dot(delta, weight.T, preferred_element_type=jnp.float32)


def contract_rows(left_side, right_side):
    return jnp.dot(left_side.T, right_side, preferred_element_type=jnp.float32)


def reference(x_paper, x_author, cite_nbr, write_src, write_dst, w_self_paper, w_cite, w_write, w_self_author, w_written, grad_paper, grad_author):
    cnt_cite = jnp.maximum(jnp.sum((cite_nbr >= 0).astype(jnp.float32), axis=1, keepdims=True), 1.0)
    cnt_write = jnp.maximum(authors_to_papers(jnp.ones((AUTHORS, 1), jnp.float32), write_src, write_dst), 1.0)
    cnt_written = jnp.maximum(papers_to_authors(jnp.ones((PAPERS, 1), jnp.float32), write_src, write_dst), 1.0)
    cited = (cite_forward(x_paper, cite_nbr) / cnt_cite).astype(jnp.bfloat16)
    written = (authors_to_papers(x_author, write_src, write_dst) / cnt_write).astype(jnp.bfloat16)
    authored = (papers_to_authors(x_paper, write_src, write_dst) / cnt_written).astype(jnp.bfloat16)
    pre_paper = (jnp.dot(x_paper, w_self_paper, preferred_element_type=jnp.float32)
                 + jnp.dot(cited, w_cite, preferred_element_type=jnp.float32)
                 + jnp.dot(written, w_write, preferred_element_type=jnp.float32))
    pre_author = (jnp.dot(x_author, w_self_author, preferred_element_type=jnp.float32)
                  + jnp.dot(authored, w_written, preferred_element_type=jnp.float32))
    out_paper = jax.nn.silu(pre_paper).astype(jnp.bfloat16)
    out_author = jax.nn.silu(pre_author).astype(jnp.bfloat16)
    dpre_paper = (grad_paper.astype(jnp.float32) * silu_slope(pre_paper)).astype(jnp.bfloat16)
    dpre_author = (grad_author.astype(jnp.float32) * silu_slope(pre_author)).astype(jnp.bfloat16)
    dz_cite = (project_back(dpre_paper, w_cite) / cnt_cite).astype(jnp.bfloat16)
    dz_write = (project_back(dpre_paper, w_write) / cnt_write).astype(jnp.bfloat16)
    dz_written = (project_back(dpre_author, w_written) / cnt_written).astype(jnp.bfloat16)
    dx_paper = (project_back(dpre_paper, w_self_paper) + cite_backward(dz_cite, cite_nbr)
                + authors_to_papers(dz_written, write_src, write_dst)).astype(jnp.bfloat16)
    dx_author = (project_back(dpre_author, w_self_author)
                 + papers_to_authors(dz_write, write_src, write_dst)).astype(jnp.bfloat16)
    paper_scale = float(PAPERS) ** -0.5
    author_scale = float(AUTHORS) ** -0.5
    dweights = jnp.stack([
        contract_rows(x_paper, dpre_paper) * paper_scale,
        contract_rows(cited, dpre_paper) * paper_scale,
        contract_rows(written, dpre_paper) * paper_scale,
        contract_rows(x_author, dpre_author) * author_scale,
        contract_rows(authored, dpre_author) * author_scale,
    ])
    return out_paper, out_author, dx_paper, dx_author, dweights
```

```python
import jax
import jax.numpy as jnp
from jax import lax
from jax.sharding import PartitionSpec as P

BF = jnp.bfloat16
F32 = jnp.float32
MASKS = (4, 1, 12, 3)
ORDERS = tuple(tuple(MASKS[(q + k) % 4] for k in range(4)) for q in range(4))


def dot(a, b, dims=((1,), (0,))):
    return lax.dot_general(a, b, (dims, ((), ())), preferred_element_type=F32)


def gather_col(block):
    rows = block.shape[0] // 4
    parts = [block[q * rows : (q + 1) * rows] for q in range(4)]
    last = [None] * 4
    for k in range(4):
        for q in range(4):
            mask = ORDERS[q][k]
            got = lax.ppermute(parts[q], "col", [(i, i ^ mask) for i in range(16)])
            if k < 3:
                parts[q] = jnp.concatenate([parts[q], got], axis=0)
            else:
                last[q] = got
    return parts, last


def source_masks():
    table = []
    for q in range(4):
        masks = []
        for m in range(16):
            value = 0
            for k in range(4):
                if (m >> k) & 1:
                    value ^= ORDERS[q][k]
            masks.append(value)
        table.append(masks)
    return table


def column_of(entries, col):
    diff = (entries >> 8) ^ col
    bits = {}
    for axis, (near, far) in enumerate(((4, 12), (1, 3))):
        d = (diff >> 2) if axis == 0 else (diff & 3)
        bits[far] = d >> 1
        bits[near] = (d & 1) ^ (d >> 1)
    quarter = (entries >> 6) & 3
    place = jnp.zeros_like(entries)
    for q in range(4):
        m = jnp.zeros_like(entries)
        for k in range(4):
            m = m + (bits[ORDERS[q][k]] << k)
        place = jnp.where(quarter == q, m, place)
    return jnp.where(entries >= 0, quarter * 1024 + place * 64 + (entries & 63), -1)


def edge_lists(write_src, write_dst):
    none = jnp.full_like(write_src, -1)
    pick = jnp.concatenate([write_src, jnp.where(write_dst >= 0, write_dst + 256, -1)], axis=1)
    into_paper = jnp.concatenate([write_dst, none], axis=1)
    into_author = jnp.concatenate([none, write_src], axis=1)
    return pick.reshape(-1), into_paper.reshape(-1), into_author.reshape(-1)


def exchange(rows):
    sent = rows.reshape(128, 8, rows.shape[-1])
    got = lax.all_to_all(sent, ("row", "col"), split_axis=0, concat_axis=0, tiled=True)
    return got.reshape(1024, rows.shape[-1])


def other_core(value):
    return lax.ppermute(value, "row", [(i, i ^ 1) for i in range(8)])


def over_y(parts):
    got = lax.all_to_all(
        parts, "row", split_axis=0, concat_axis=0, tiled=True,
        axis_index_groups=[[0, 2, 4, 6], [1, 3, 5, 7]],
    )
    return jnp.sum(got.astype(F32), axis=0)


def silu_and_slope(value):
    sigma = jax.nn.sigmoid(value)
    return (value * sigma).astype(BF), sigma * (1.0 + value * (1.0 - sigma))


def per_device(
    x_paper, x_author, cite_nbr, write_src, write_dst,
    w_self_paper, w_cite, w_write, w_self_author, w_written, grad_paper, grad_author,
):
    col = lax.axis_index("col")
    core = lax.axis_index("row") & 1

    pick, into_paper, into_author = edge_lists(write_src[0], write_dst[0])
    picker = (pick[:, None] == lax.iota(jnp.int32, 512)[None, :]).astype(BF)
    ids = lax.iota(jnp.int32, 256)[:, None]
    adder = jnp.concatenate(
        [(into_paper[None, :] == ids), (into_author[None, :] == ids)], axis=0
    ).astype(BF)
    both = jnp.concatenate([x_author, x_paper], axis=0)
    arrived = exchange(dot(picker, both).astype(BF))

    first, last = gather_col(x_paper)
    cnt_cite = jnp.maximum(jnp.sum((cite_nbr >= 0).astype(F32), axis=1, keepdims=True), 1.0)
    places = column_of(cite_nbr, col)
    columns = lax.iota(jnp.int32, 4096)
    table = jnp.zeros((256, 4096), F32)
    for slot in range(16):
        table = table + (places[:, slot : slot + 1] == columns[None, :]).astype(F32)
    table = lax.optimization_barrier(table.astype(BF))

    all_nbr = lax.all_gather(cite_nbr, "col", axis=0, tiled=True).reshape(16, 4, 64, 16)
    sources = jnp.array(source_masks(), jnp.int32) ^ col
    ordered = jnp.concatenate([all_nbr[:, q][sources[q]] for q in range(4)], axis=0)
    ordered = ordered.reshape(4096, 16).T
    own = ids + col * 256
    back_table = jnp.zeros((256, 4096), F32)
    for slot in range(16):
        back_table = back_table + (ordered[slot : slot + 1, :] == own).astype(F32)
    back_table = lax.optimization_barrier(back_table.astype(BF))

    lane = lax.iota(jnp.int32, 384)
    target = (lane // 96) * 192 + lane % 96
    rows768 = lax.iota(jnp.int32, 768)[:, None]
    mine = (rows768 == (target + core * 96)[None, :]).astype(BF)
    theirs = (rows768 == (target + (1 - core) * 96)[None, :]).astype(BF)

    cnt = jnp.maximum(jnp.sum(adder.astype(F32), axis=1, keepdims=True), 1.0)
    edge_mean = (dot(adder, arrived) / cnt).astype(BF)
    written, authored = edge_mean[:256], edge_mean[256:]

    pre_author = dot(x_author, w_self_author) + dot(authored, w_written)
    out_author, slope = silu_and_slope(pre_author)
    dpre_author = (grad_author.astype(F32) * slope).astype(BF)
    dz_written = (dot(dpre_author, w_written, ((1,), (1,))) / cnt[256:]).astype(BF)
    dx_author_own = dot(dpre_author, w_self_author, ((1,), (1,)))

    def weight_parts(lefts, dpre):
        left = jnp.concatenate(lefts, axis=0)
        kept = dot(left, mine).astype(BF)
        given = other_core(dot(left, theirs).astype(BF))
        dpre_other = other_core(dpre)
        right = jnp.concatenate([dpre, dpre_other], axis=0)
        outs = []
        for i in range(len(lefts)):
            pair = jnp.concatenate([kept[256 * i : 256 * i + 256], given[256 * i : 256 * i + 256]], axis=0)
            outs.append(dot(pair, right, ((0,), (0,))).astype(BF).reshape(4, 96, 1024))
        return over_y(jnp.stack(outs, axis=1))

    sums_author = weight_parts([x_author, authored], dpre_author)

    cite_total = jnp.zeros((256, 768), F32)
    for q in range(4):
        cite_total = cite_total + dot(table[:, q * 1024 : q * 1024 + 512], first[q])
        cite_total = cite_total + dot(table[:, q * 1024 + 512 : q * 1024 + 1024], last[q])
    cited = (cite_total / cnt_cite).astype(BF)
    pre_paper = dot(x_paper, w_self_paper) + dot(written, w_write) + dot(cited, w_cite)
    out_paper, slope = silu_and_slope(pre_paper)
    dpre_paper = (grad_paper.astype(F32) * slope).astype(BF)
    dz_cite = (dot(dpre_paper, w_cite, ((1,), (1,))) / cnt_cite).astype(BF)
    first, last = gather_col(dz_cite)
    dz_write = (dot(dpre_paper, w_write, ((1,), (1,))) / cnt[:256]).astype(BF)
    back = exchange(dot(picker, jnp.concatenate([dz_written, dz_write], axis=0)).astype(BF))
    dx_paper_own = dot(dpre_paper, w_self_paper, ((1,), (1,)))
    sums_paper = weight_parts([x_paper, cited, written], dpre_paper)

    sums = jnp.concatenate([sums_paper, sums_author], axis=0).reshape(480, 1024)
    cols = sums.T.astype(BF).reshape(16, 64, 480)
    got = lax.all_to_all(cols, "col", split_axis=0, concat_axis=0, tiled=True)
    total = jnp.sum(got.astype(F32), axis=0) * (32768.0 ** -0.5)
    dweights = total.reshape(64, 5, 96).transpose(1, 2, 0)

    edge_sum = dot(adder, back)
    dx_author = (dx_author_own + edge_sum[256:]).astype(BF)
    acc = dx_paper_own + edge_sum[:256]
    for q in range(4):
        acc = acc + dot(back_table[:, q * 1024 : q * 1024 + 512], first[q])
        acc = acc + dot(back_table[:, q * 1024 + 512 : q * 1024 + 1024], last[q])
    dx_paper = acc.astype(BF)
    return (out_paper, out_author, dx_paper, dx_author, dweights)


def solution(mesh):
    part = P(("row", "col"), None)
    part3 = P(("row", "col"), None, None)
    return jax.shard_map(
        per_device,
        mesh=mesh,
        in_specs=(part, part, part, part3, part3, P(), P(), P(), P(), P(), part, part),
        out_specs=(part, part, part, part, P(None, "row", "col")),
        check_vma=False,
    )
```

```python
import jax
import jax.numpy as jnp
from jax import lax
from jax.sharding import PartitionSpec as P

BF = jnp.bfloat16
F32 = jnp.float32
MASKS = (4, 1, 12, 3)
ORDERS = tuple(tuple(MASKS[(q + k) % 4] for k in range(4)) for q in range(4))


def dot(a, b, dims=((1,), (0,))):
    return lax.dot_general(a, b, (dims, ((), ())), preferred_element_type=F32)


def quarters(block):
    rows = block.shape[0] // 4
    return [block[q * rows : (q + 1) * rows] for q in range(4)]


def doubling(parts, k):
    done = []
    for q in range(4):
        mask = ORDERS[q][k]
        got = lax.ppermute(parts[q], "col", [(i, i ^ mask) for i in range(16)])
        done.append((parts[q], got) if k == 3 else jnp.concatenate([parts[q], got], axis=0))
    return done


def together(*values):
    return lax.optimization_barrier(values)


def source_masks():
    table = []
    for q in range(4):
        masks = []
        for m in range(16):
            value = 0
            for k in range(4):
                if (m >> k) & 1:
                    value ^= ORDERS[q][k]
            masks.append(value)
        table.append(masks)
    return table


def column_of(entries, col):
    diff = (entries >> 8) ^ col
    bits = {}
    for axis, (near, far) in enumerate(((4, 12), (1, 3))):
        d = (diff >> 2) if axis == 0 else (diff & 3)
        bits[far] = d >> 1
        bits[near] = (d & 1) ^ (d >> 1)
    quarter = (entries >> 6) & 3
    place = jnp.zeros_like(entries)
    for q in range(4):
        m = jnp.zeros_like(entries)
        for k in range(4):
            m = m + (bits[ORDERS[q][k]] << k)
        place = jnp.where(quarter == q, m, place)
    return jnp.where(entries >= 0, quarter * 1024 + place * 64 + (entries & 63), -1)


def edge_lists(write_src, write_dst):
    none = jnp.full_like(write_src, -1)
    pick = jnp.concatenate([write_src, jnp.where(write_dst >= 0, write_dst + 256, -1)], axis=1)
    into_paper = jnp.concatenate([write_dst, none], axis=1)
    into_author = jnp.concatenate([none, write_src], axis=1)
    return pick.reshape(-1), into_paper.reshape(-1), into_author.reshape(-1)


def exchange(rows):
    sent = rows.reshape(128, 8, rows.shape[-1])
    got = lax.all_to_all(sent, ("row", "col"), split_axis=0, concat_axis=0, tiled=True)
    return got.reshape(1024, rows.shape[-1])


def other_core(value):
    return lax.ppermute(value, "row", [(i, i ^ 1) for i in range(8)])


def over_y(parts):
    got = lax.all_to_all(
        parts, "row", split_axis=0, concat_axis=0, tiled=True,
        axis_index_groups=[[0, 2, 4, 6], [1, 3, 5, 7]],
    )
    return jnp.sum(got.astype(F32), axis=0)


def silu_and_slope(value):
    sigma = jax.nn.sigmoid(value)
    return (value * sigma).astype(BF), sigma * (1.0 + value * (1.0 - sigma))


def per_device(
    x_paper, x_author, cite_nbr, write_src, write_dst,
    w_self_paper, w_cite, w_write, w_self_author, w_written, grad_paper, grad_author,
):
    col = lax.axis_index("col")
    core = lax.axis_index("row") & 1
    ids = lax.iota(jnp.int32, 256)[:, None]
    all_nbr = lax.all_gather(cite_nbr.T.astype(F32), "col", axis=0)

    parts = doubling(quarters(x_paper), 0)
    pick, into_paper, into_author = edge_lists(write_src[0], write_dst[0])
    picker = (pick[:, None] == lax.iota(jnp.int32, 512)[None, :]).astype(BF)
    both = jnp.concatenate([x_author, x_paper], axis=0)
    rows = dot(picker, both).astype(BF)
    parts, rows = together(parts, rows)

    arrived = exchange(rows)
    parts = doubling(parts, 1)
    cnt_cite = jnp.maximum(jnp.sum((cite_nbr >= 0).astype(F32), axis=1, keepdims=True), 1.0)
    places = column_of(cite_nbr, col)
    columns = lax.iota(jnp.int32, 4096)
    table = jnp.zeros((256, 4096), F32)
    for slot in range(16):
        table = table + (places[:, slot : slot + 1] == columns[None, :]).astype(F32)
    table = table.astype(BF)
    parts, table = together(parts, table)

    parts = doubling(parts, 2)
    sources = jnp.array(source_masks(), jnp.int32) ^ col
    pieces = all_nbr.reshape(16, 16, 4, 64)
    ordered = jnp.concatenate(
        [pieces[:, :, q][sources[q]].transpose(1, 0, 2).reshape(16, 1024) for q in range(4)], axis=1
    )
    own = (ids + col * 256).astype(F32)
    back_table = jnp.zeros((256, 4096), F32)
    for slot in range(16):
        back_table = back_table + (ordered[slot : slot + 1, :] == own).astype(F32)
    back_table = back_table.astype(BF)
    parts, back_table = together(parts, back_table)

    halves = doubling(parts, 3)
    lane = lax.iota(jnp.int32, 384)
    target = (lane // 96) * 192 + lane % 96
    rows768 = lax.iota(jnp.int32, 768)[:, None]
    mine = (rows768 == (target + core * 96)[None, :]).astype(BF)
    theirs = (rows768 == (target + (1 - core) * 96)[None, :]).astype(BF)
    adder = jnp.concatenate(
        [(into_paper[None, :] == ids), (into_author[None, :] == ids)], axis=0
    ).astype(BF)
    cnt = jnp.maximum(jnp.sum(adder.astype(F32), axis=1, keepdims=True), 1.0)
    edge_mean = (dot(adder, arrived) / cnt).astype(BF)
    written, authored = edge_mean[:256], edge_mean[256:]
    pre_author = dot(x_author, w_self_author) + dot(authored, w_written)
    out_author, slope = silu_and_slope(pre_author)
    dpre_author = (grad_author.astype(F32) * slope).astype(BF)
    dz_written = (dot(dpre_author, w_written, ((1,), (1,))) / cnt[256:]).astype(BF)
    dx_author_own = dot(dpre_author, w_self_author, ((1,), (1,)))

    def weight_parts(lefts, dpre):
        left = jnp.concatenate(lefts, axis=0)
        kept = dot(left, mine).astype(BF)
        given = other_core(dot(left, theirs).astype(BF))
        dpre_other = other_core(dpre)
        right = jnp.concatenate([dpre, dpre_other], axis=0)
        outs = []
        for i in range(len(lefts)):
            pair = jnp.concatenate([kept[256 * i : 256 * i + 256], given[256 * i : 256 * i + 256]], axis=0)
            outs.append(dot(pair, right, ((0,), (0,))).astype(BF).reshape(4, 96, 1024))
        return jnp.stack(outs, axis=1)

    parts_author = weight_parts([x_author, authored], dpre_author)
    pre_paper = dot(x_paper, w_self_paper) + dot(written, w_write)
    cite_total = jnp.zeros((256, 768), F32)
    for q in range(4):
        cite_total = cite_total + dot(table[:, q * 1024 : q * 1024 + 512], halves[q][0])
    halves, cite_total, pre_paper, dz_written, parts_author = together(
        halves, cite_total, pre_paper, dz_written, parts_author
    )
    sums_author = over_y(parts_author)

    for q in range(4):
        cite_total = cite_total + dot(table[:, q * 1024 + 512 : q * 1024 + 1024], halves[q][1])
    cited = (cite_total / cnt_cite).astype(BF)
    pre_paper = pre_paper + dot(cited, w_cite)
    out_paper, slope = silu_and_slope(pre_paper)
    dpre_paper = (grad_paper.astype(F32) * slope).astype(BF)
    dz_cite = (dot(dpre_paper, w_cite, ((1,), (1,))) / cnt_cite).astype(BF)

    parts = doubling(quarters(dz_cite), 0)
    dz_write = (dot(dpre_paper, w_write, ((1,), (1,))) / cnt[:256]).astype(BF)
    rows = dot(picker, jnp.concatenate([dz_written, dz_write], axis=0)).astype(BF)
    parts, rows = together(parts, rows)

    back = exchange(rows)
    parts = doubling(parts, 1)
    parts_paper = weight_parts([x_paper, cited, written], dpre_paper)
    parts, parts_paper = together(parts, parts_paper)

    sums_paper = over_y(parts_paper)
    parts = doubling(parts, 2)
    acc = dot(dpre_paper, w_self_paper, ((1,), (1,)))
    parts, acc = together(parts, acc)
    halves = doubling(parts, 3)
    for q in range(4):
        acc = acc + dot(back_table[:, q * 1024 : q * 1024 + 512], halves[q][0])

    sums = jnp.concatenate([sums_paper, sums_author], axis=0).reshape(480, 1024)
    cols = sums.T.astype(BF).reshape(16, 64, 480)
    got = lax.all_to_all(cols, "col", split_axis=0, concat_axis=0, tiled=True)
    total = jnp.sum(got.astype(F32), axis=0) * (32768.0 ** -0.5)
    dweights = total.reshape(64, 5, 96).transpose(1, 2, 0)

    edge_sum = dot(adder, back)
    dx_author = (dx_author_own + edge_sum[256:]).astype(BF)
    acc = acc + edge_sum[:256]
    for q in range(4):
        acc = acc + dot(back_table[:, q * 1024 + 512 : q * 1024 + 1024], halves[q][1])
    dx_paper = acc.astype(BF)
    return (out_paper, out_author, dx_paper, dx_author, dweights)


def solution(mesh):
    part = P(("row", "col"), None)
    part3 = P(("row", "col"), None, None)
    return jax.shard_map(
        per_device,
        mesh=mesh,
        in_specs=(part, part, part, part3, part3, P(), P(), P(), P(), P(), part, part),
        out_specs=(part, part, part, part, P(None, "row", "col")),
        check_vma=False,
    )
```

```python
import functools

import jax
import jax.numpy as jnp
from jax import lax
from jax.experimental import pallas as pl
from jax.experimental.pallas import tpu as pltpu
from jax.sharding import PartitionSpec as P

BF = jnp.bfloat16
F32 = jnp.float32
I32 = jnp.int32
MIB = 1024 * 1024
MASKS = (4, 1, 12, 3)
ORDERS = tuple(tuple(MASKS[(q + k) % 4] for k in range(4)) for q in range(4))
IN_VMEM = pl.BlockSpec(memory_space=pltpu.VMEM)
ANYWHERE = pl.BlockSpec(memory_space=pl.ANY)
IN_SMEM = pl.BlockSpec(memory_space=pltpu.SMEM)


def dot(a, b, dims=((1,), (0,))):
    return lax.dot_general(a, b, (dims, ((), ())), preferred_element_type=F32)


def shape(dims, kind):
    return jax.ShapeDtypeStruct(dims, kind)


def params(mib):
    return pltpu.CompilerParams(vmem_limit_bytes=mib * MIB)


def join_kernel(*refs):
    n = (len(refs) - 1) // 3
    sems = refs[-1]
    copies = []
    for i in range(n):
        a, b, out = refs[2 * i], refs[2 * i + 1], refs[2 * n + i]
        rows = a.shape[0]
        copies.append(pltpu.make_async_copy(a, out.at[pl.ds(0, rows)], sems.at[2 * i]))
        copies.append(pltpu.make_async_copy(b, out.at[pl.ds(rows, rows)], sems.at[2 * i + 1]))
    for copy in copies:
        copy.start()
    for copy in copies:
        copy.wait()


def join(pairs):
    n = len(pairs)
    flat = [v for pair in pairs for v in pair]
    outs = [shape((2 * a.shape[0],) + a.shape[1:], a.dtype) for a, _ in pairs]
    return pl.pallas_call(
        join_kernel,
        out_shape=outs,
        in_specs=[ANYWHERE] * (2 * n),
        out_specs=[ANYWHERE] * n,
        scratch_shapes=[pltpu.SemaphoreType.DMA((2 * n,))],
        name="join",
    )(*flat)


def travel(parts, k):
    pairs = []
    for q, part in enumerate(parts):
        mask = ORDERS[q % 4][k]
        pairs.append((part, lax.ppermute(part, "col", [(i, i ^ mask) for i in range(16)])))
    return pairs


def source_mask(q, m):
    value = 0
    for k in range(4):
        if (m >> k) & 1:
            value ^= ORDERS[q][k]
    return value


def column_of(entries, col):
    diff = (entries >> 8) ^ col
    bits = {}
    for axis, (near, far) in enumerate(((4, 12), (1, 3))):
        d = (diff >> 2) if axis == 0 else (diff & 3)
        bits[far] = d >> 1
        bits[near] = (d & 1) ^ (d >> 1)
    quarter = (entries >> 6) & 3
    place = jnp.zeros_like(entries)
    for q in range(4):
        m = jnp.zeros_like(entries)
        for k in range(4):
            m = m + (bits[ORDERS[q][k]] << k)
        place = jnp.where(quarter == q, m, place)
    return jnp.where(entries >= 0, quarter * 1024 + place * 64 + (entries & 63), -1)


def table_kernel(col_ref, nbr_ref, token_ref, out_ref):
    places = column_of(nbr_ref[...], col_ref[0])

    @pl.loop(0, 16)
    def _(t):
        lanes = lax.broadcasted_iota(I32, (256, 256), 1) + t * 256
        acc = jnp.zeros((256, 256), F32)
        for slot in range(16):
            acc = acc + jnp.where(places[:, slot : slot + 1] == lanes, 1.0, 0.0)
        out_ref[:, pl.ds(pl.multiple_of(t * 256, 256), 256)] = acc.astype(BF)


def cite_table(col, nbr, token):
    return pl.pallas_call(
        table_kernel,
        out_shape=shape((256, 4096), BF),
        in_specs=[IN_SMEM, IN_VMEM, ANYWHERE],
        out_specs=IN_VMEM,
        compiler_params=params(16),
        cost_estimate=pl.CostEstimate(flops=10**9, bytes_accessed=3 * 10**6, transcendentals=0),
        name="cite_table",
    )(col, nbr, token)


def back_table_kernel(col_ref, a_ref, b_ref, out_ref):
    col = col_ref[0]
    own = lax.broadcasted_iota(I32, (256, 256), 0) + col * 256
    for m in range(16):
        half = a_ref if m < 8 else b_ref
        acc = jnp.zeros((256, 256), F32)
        for slot in range(16):
            acc = acc + jnp.where(half[m % 8, slot : slot + 1, :] == own, 1.0, 0.0)
        block = col ^ source_mask(0, m)
        out_ref[:, pl.ds(pl.multiple_of(block * 256, 256), 256)] = acc.astype(BF)


def cited_by_table(col, a, b):
    return pl.pallas_call(
        back_table_kernel,
        out_shape=shape((256, 4096), BF),
        in_specs=[IN_SMEM, IN_VMEM, IN_VMEM],
        out_specs=IN_VMEM,
        compiler_params=params(16),
        cost_estimate=pl.CostEstimate(flops=10**9, bytes_accessed=3 * 10**6, transcendentals=0),
        name="cited_by_table",
    )(col, a, b)


def edge_lists(write_src, write_dst):
    none = jnp.full_like(write_src, -1)
    pick = jnp.concatenate([write_src, jnp.where(write_dst >= 0, write_dst + 256, -1)], axis=1)
    into_paper = jnp.concatenate([write_dst, none], axis=1)
    into_author = jnp.concatenate([none, write_src], axis=1)
    return pick.reshape(-1), into_paper.reshape(1, -1), into_author.reshape(1, -1)


def exchange(rows):
    sent = rows.reshape(128, 8, rows.shape[-1])
    got = lax.all_to_all(sent, ("row", "col"), split_axis=0, concat_axis=0, tiled=True)
    return got.reshape(1024, rows.shape[-1])


def other_core(value):
    return lax.ppermute(value, "row", [(i, i ^ 1) for i in range(8)])


def over_y(parts):
    return lax.all_to_all(
        parts, "row", split_axis=0, concat_axis=0, tiled=True,
        axis_index_groups=[[0, 2, 4, 6], [1, 3, 5, 7]],
    )


def silu_and_slope(value):
    sigma = 1.0 / (1.0 + jnp.exp(-value))
    return (value * sigma).astype(BF), sigma * (1.0 + value * (1.0 - sigma))


def author_kernel(
    arrived_ref, into_paper_ref, into_author_ref, x_author_ref, x_paper_ref, grad_ref,
    w_sa_hbm, w_wn_hbm, w_sp_hbm, w_wr_hbm,
    out_ref, pack_ref, dz_ref, dx_ref, pre_ref, adder_ref, cnt_ref,
    w_sa, w_wn, w_sp, w_wr, sems,
):
    copies = []
    for i, (a, b) in enumerate(((w_sa_hbm, w_sa), (w_wn_hbm, w_wn), (w_sp_hbm, w_sp), (w_wr_hbm, w_wr))):
        copies.append(pltpu.make_async_copy(a, b, sems.at[i]))
        copies[-1].start()
    ids = lax.broadcasted_iota(I32, (256, 1024), 0)
    means = []
    for i, ref in enumerate((into_paper_ref, into_author_ref)):
        hit = jnp.where(ref[...] == ids, 1.0, 0.0)
        cnt = jnp.maximum(jnp.sum(hit, axis=1, keepdims=True), 1.0)
        cnt_ref[pl.ds(256 * i, 256), :] = jnp.broadcast_to(cnt, (256, 128))
        hit = hit.astype(BF)
        adder_ref[pl.ds(256 * i, 256), :] = hit
        means.append((dot(hit, arrived_ref[...]) / cnt).astype(BF))
    written, authored = means
    x_author, x_paper = x_author_ref[...], x_paper_ref[...]
    copies[0].wait()
    copies[1].wait()
    pre = dot(x_author, w_sa[...]) + dot(authored, w_wn[...])
    out, slope = silu_and_slope(pre)
    out_ref[...] = out
    dpre = (grad_ref[...].astype(F32) * slope).astype(BF)
    pack_ref[:, pl.ds(0, 768)] = x_author
    pack_ref[:, pl.ds(768, 768)] = authored
    pack_ref[:, pl.ds(1536, 768)] = x_paper
    pack_ref[:, pl.ds(2304, 768)] = written
    pack_ref[:, pl.ds(3072, 1024)] = dpre
    dz_ref[...] = (dot(dpre, w_wn[...], ((1,), (1,))) / cnt_ref[pl.ds(256, 256), pl.ds(0, 1)]).astype(BF)
    dx_ref[...] = dot(dpre, w_sa[...], ((1,), (1,)))
    copies[2].wait()
    copies[3].wait()
    pre_ref[...] = dot(x_paper, w_sp[...]) + dot(written, w_wr[...])


def author_step(arrived, into_paper, into_author, x_author, x_paper, grad, w_sa, w_wn, w_sp, w_wr):
    weight = pltpu.VMEM((768, 1024), BF)
    return pl.pallas_call(
        author_kernel,
        out_shape=[
            shape((256, 1024), BF), shape((256, 4096), BF), shape((256, 768), BF), shape((256, 768), F32),
            shape((256, 1024), F32), shape((512, 1024), BF), shape((512, 128), F32),
        ],
        in_specs=[IN_VMEM] * 6 + [ANYWHERE] * 4,
        out_specs=[IN_VMEM] * 7,
        scratch_shapes=[weight] * 4 + [pltpu.SemaphoreType.DMA((4,))],
        compiler_params=params(40),
        cost_estimate=pl.CostEstimate(flops=4 * 10**9, bytes_accessed=15 * 10**6, transcendentals=0),
        name="author_step",
    )(arrived, into_paper, into_author, x_author, x_paper, grad, w_sa, w_wn, w_sp, w_wr)


def half_kernel(offset, *refs):
    table_ref, blocks, out_ref = refs[0], refs[1:5], refs[5]
    acc = jnp.zeros((256, 768), F32)
    for q in range(4):
        acc = acc + dot(table_ref[:, pl.ds(q * 1024 + offset, 512)], blocks[q][...])
    out_ref[...] = acc


def first_half(table, blocks):
    return pl.pallas_call(
        functools.partial(half_kernel, 0),
        out_shape=shape((256, 768), F32),
        in_specs=[IN_VMEM] * 5,
        out_specs=IN_VMEM,
        compiler_params=params(24),
        cost_estimate=pl.CostEstimate(flops=2 * 10**9, bytes_accessed=5 * 10**6, transcendentals=0),
        name="first_half",
    )(table, *blocks)


def paper_kernel(
    table_ref, b0, b1, b2, b3, first_ref, nbr_ref, pre_ref, grad_ref, w_hbm,
    out_ref, pack_ref, dz_ref, w_ref, sem,
):
    copy = pltpu.make_async_copy(w_hbm, w_ref, sem)
    copy.start()
    total = first_ref[...]
    for q, block in enumerate((b0, b1, b2, b3)):
        total = total + dot(table_ref[:, pl.ds(q * 1024 + 512, 512)], block[...])
    cnt = jnp.sum(jnp.where(nbr_ref[...] >= 0, 1.0, 0.0), axis=1, keepdims=True)
    cnt = jnp.maximum(cnt, 1.0)
    cited = (total / cnt).astype(BF)
    pack_ref[:, pl.ds(0, 768)] = cited
    copy.wait()
    out, slope = silu_and_slope(pre_ref[...] + dot(cited, w_ref[...]))
    out_ref[...] = out
    dpre = (grad_ref[...].astype(F32) * slope).astype(BF)
    pack_ref[:, pl.ds(768, 1024)] = dpre
    dz_ref[...] = (dot(dpre, w_ref[...], ((1,), (1,))) / cnt).astype(BF)


def paper_step(table, blocks, first, nbr, pre, grad, w_cite):
    return pl.pallas_call(
        paper_kernel,
        out_shape=[shape((256, 1024), BF), shape((256, 1792), BF), shape((256, 768), BF)],
        in_specs=[IN_VMEM] * 9 + [ANYWHERE],
        out_specs=[IN_VMEM] * 3,
        scratch_shapes=[pltpu.VMEM((768, 1024), BF), pltpu.SemaphoreType.DMA],
        compiler_params=params(32),
        cost_estimate=pl.CostEstimate(flops=3 * 10**9, bytes_accessed=10 * 10**6, transcendentals=0),
        name="paper_step",
    )(table, *blocks, first, nbr, pre, grad, w_cite)


def edge_back_kernel(pack_ref, cnt_ref, w_wr_hbm, w_sp_hbm, dz_ref, dx_ref, w_wr, w_sp, sems):
    copies = [pltpu.make_async_copy(w_wr_hbm, w_wr, sems.at[0]), pltpu.make_async_copy(w_sp_hbm, w_sp, sems.at[1])]
    for copy in copies:
        copy.start()
    dpre = pack_ref[:, pl.ds(768, 1024)]
    copies[0].wait()
    dz_ref[...] = (dot(dpre, w_wr[...], ((1,), (1,))) / cnt_ref[pl.ds(0, 256), pl.ds(0, 1)]).astype(BF)
    copies[1].wait()
    dx_ref[...] = dot(dpre, w_sp[...], ((1,), (1,)))


def edge_back(pack, cnt, w_write, w_self):
    return pl.pallas_call(
        edge_back_kernel,
        out_shape=[shape((256, 768), BF), shape((256, 768), F32)],
        in_specs=[IN_VMEM, IN_VMEM, ANYWHERE, ANYWHERE],
        out_specs=[IN_VMEM] * 2,
        scratch_shapes=[pltpu.VMEM((768, 1024), BF)] * 2 + [pltpu.SemaphoreType.DMA((2,))],
        compiler_params=params(16),
        cost_estimate=pl.CostEstimate(flops=10**9, bytes_accessed=5 * 10**6, transcendentals=0),
        name="edge_back",
    )(pack, cnt, w_write, w_self)


def weight_kernel(lefts, right, core_ref, *refs):
    ins, out_ref, turned = refs[: -2], refs[-2], refs[-1]
    core = core_ref[0]
    own, other, lane = right
    dpre = jnp.concatenate([ins[own][:, pl.ds(lane, 1024)], ins[other][:, pl.ds(lane, 1024)]], axis=0)
    for i, (own, other, lane) in enumerate(lefts):
        for k, ref in enumerate((ins[own], ins[other])):
            turned[i, :, pl.ds(256 * k, 256)] = ref[:, pl.ds(lane, 768)].T
        rows = []
        for y in range(4):
            start = pl.multiple_of((2 * y + core) * 96, 32)
            rows.append(turned[i, pl.ds(start, 96), :])
        product = dot(jnp.concatenate(rows, axis=0), dpre).astype(BF)
        for y in range(4):
            out_ref[y, i] = product[96 * y : 96 * y + 96]


def weight_parts(core, arrays, lefts, right):
    n = len(lefts)
    return pl.pallas_call(
        functools.partial(weight_kernel, lefts, right),
        out_shape=shape((4, n, 96, 1024), BF),
        in_specs=[IN_SMEM] + [IN_VMEM] * len(arrays),
        out_specs=IN_VMEM,
        scratch_shapes=[pltpu.VMEM((n, 768, 512), BF)],
        compiler_params=params(32),
        cost_estimate=pl.CostEstimate(flops=2 * 10**9, bytes_accessed=8 * 10**6, transcendentals=0),
        name="weight_parts",
    )(core, *arrays)


def y_sum_kernel(paper_ref, author_ref, out_ref, stack):
    for m in range(5):
        ref, i = (paper_ref, m) if m < 3 else (author_ref, m - 3)
        total = ref[0, i].astype(F32)
        for y in range(1, 4):
            total = total + ref[y, i].astype(F32)
        stack[pl.ds(96 * m, 96), :] = total
    stack[pl.ds(480, 32), :] = jnp.zeros((32, 1024), F32)
    for j in range(16):
        if j % 2 == 0:
            turned = stack[:, pl.ds(64 * j, 128)].T.astype(BF)
        out_ref[j] = turned[64 * (j % 2) : 64 * (j % 2) + 64]


def y_sum(paper, author):
    return pl.pallas_call(
        y_sum_kernel,
        out_shape=shape((16, 64, 512), BF),
        in_specs=[IN_VMEM] * 2,
        out_specs=IN_VMEM,
        scratch_shapes=[pltpu.VMEM((512, 1024), F32)],
        compiler_params=params(20),
        name="y_sum",
    )(paper, author)


def last_sum_kernel(got_ref, out_ref):
    total = got_ref[0].astype(F32)
    for j in range(1, 16):
        total = total + got_ref[j].astype(F32)
    total = total * (32768.0 ** -0.5)
    for m in range(5):
        out_ref[m] = total[:, 96 * m : 96 * m + 96]


def last_sum(got):
    return pl.pallas_call(
        last_sum_kernel,
        out_shape=shape((5, 64, 96), F32),
        in_specs=[IN_VMEM],
        out_specs=IN_VMEM,
        compiler_params=params(8),
        name="last_sum",
    )(got)


def per_device(
    x_paper, x_author, cite_nbr, write_src, write_dst,
    w_self_paper, w_cite, w_write, w_self_author, w_written, grad_paper, grad_author,
):
    col = lax.axis_index("col").astype(I32).reshape(1)
    core = (lax.axis_index("row") & 1).astype(I32).reshape(1)

    pick, into_paper, into_author = edge_lists(write_src[0], write_dst[0])
    picker = (pick[:, None] == lax.iota(I32, 512)[None, :]).astype(BF)
    rows = dot(picker, jnp.concatenate([x_author, x_paper], axis=0)).astype(BF)
    arrived = exchange(rows)

    parts = [x_paper[64 * q : 64 * q + 64] for q in range(4)] + [cite_nbr.T.reshape(1, 16, 256)]
    parts = join(travel(parts, 0))
    table = cite_table(col, cite_nbr, parts[0])
    parts = join(travel(parts, 1))
    parts = join(travel(parts, 2))
    pairs = travel(parts, 3)
    cite_first = first_half(table, [pair[0] for pair in pairs[:4]])

    out_author, pack_a, dz_written, dx_author_own, pre_paper, adder, cnt = author_step(
        arrived, into_paper, into_author, x_author, x_paper, grad_author,
        w_self_author, w_written, w_self_paper, w_write,
    )
    pack_a_other = other_core(pack_a)
    parts_author = weight_parts(core, [pack_a, pack_a_other], [(0, 1, 0), (0, 1, 768)], (0, 1, 3072))
    got_author = over_y(parts_author)

    out_paper, pack_p, dz_cite = paper_step(
        table, [pair[1] for pair in pairs[:4]], cite_first, cite_nbr, pre_paper, grad_paper, w_cite
    )
    gathered = lax.all_gather(dz_cite, "col", axis=0, tiled=True)
    pack_p_other = other_core(pack_p)
    dz_write, dx_paper_own = edge_back(pack_p, cnt, w_write, w_self_paper)
    rows = dot(picker, jnp.concatenate([dz_written, dz_write], axis=0)).astype(BF)
    parts_paper = weight_parts(
        core, [pack_a, pack_a_other, pack_p, pack_p_other],
        [(0, 1, 1536), (2, 3, 0), (0, 1, 2304)], (2, 3, 768),
    )
    got_paper = over_y(parts_paper)
    back = exchange(rows)
    back_table = cited_by_table(col, pairs[4][0], pairs[4][1])

    got = lax.all_to_all(y_sum(got_paper, got_author), "col", split_axis=0, concat_axis=0, tiled=True)
    dweights = last_sum(got).transpose(0, 2, 1)

    edge_sum = dot(adder, back)
    dx_author = (dx_author_own + edge_sum[256:]).astype(BF)
    dx_paper = (dot(back_table, gathered) + (dx_paper_own + edge_sum[:256])).astype(BF)
    return (out_paper, out_author, dx_paper, dx_author, dweights)


def solution(mesh):
    part = P(("row", "col"), None)
    part3 = P(("row", "col"), None, None)
    return jax.shard_map(
        per_device,
        mesh=mesh,
        in_specs=(part, part, part, part3, part3, P(), P(), P(), P(), P(), part, part),
        out_specs=(part, part, part, part, P(None, "row", "col")),
        check_vma=False,
    )
```

```python
import functools

import jax
import jax.numpy as jnp
from jax import lax
from jax.experimental import pallas as pl
from jax.experimental.pallas import tpu as pltpu
from jax.sharding import PartitionSpec as P

BF = jnp.bfloat16
F32 = jnp.float32
I32 = jnp.int32
MIB = 1024 * 1024
I16 = jnp.int16
CYCLE = (4, 1, 12, 3)
IN_VMEM = pl.BlockSpec(memory_space=pltpu.VMEM)
ANYWHERE = pl.BlockSpec(memory_space=pl.ANY)
IN_SMEM = pl.BlockSpec(memory_space=pltpu.SMEM)


def dot(a, b, dims=((1,), (0,))):
    return lax.dot_general(a, b, (dims, ((), ())), preferred_element_type=F32)


def shape(dims, kind):
    return jax.ShapeDtypeStruct(dims, kind)


def params(mib):
    return pltpu.CompilerParams(vmem_limit_bytes=mib * MIB)


def join_kernel(n, *refs):
    outs = refs[len(refs) - n :]
    for i in range(n):
        a, b, out = refs[2 * i], refs[2 * i + 1], outs[i]
        rows = a.shape[0]
        out[pl.ds(0, rows)] = a[...]
        out[pl.ds(rows, rows)] = b[...]


def join(pairs, tokens=()):
    n = len(pairs)
    flat = [v for pair in pairs for v in pair]
    outs = [shape((2 * a.shape[0],) + a.shape[1:], a.dtype) for a, _ in pairs]
    return pl.pallas_call(
        functools.partial(join_kernel, n),
        out_shape=outs,
        in_specs=[IN_VMEM] * (2 * n) + [ANYWHERE] * len(tokens),
        out_specs=[IN_VMEM] * n,
        compiler_params=params(16),
        name="join",
    )(*flat, *tokens)


def travel(parts, k):
    pairs = []
    for h, part in enumerate(parts):
        masks = [CYCLE[(k + 2 * (h & 1) + c) % 4] for c in range(2)]
        perm = [(r * 16 + c, r * 16 + (c ^ masks[r & 1])) for r in range(8) for c in range(16)]
        pairs.append((part, lax.ppermute(part, ("row", "col"), perm)))
    return pairs


def column_of(entries, col, core):
    diff = (entries >> 8) ^ col
    bits = {}
    for axis, (near, far) in enumerate(((4, 12), (1, 3))):
        d = ((diff >> 2) & 3) if axis == 0 else (diff & 3)
        bits[far] = d >> 1
        bits[near] = (d & 1) ^ (d >> 1)
    half = (entries >> 7) & 1
    turn = (2 * half + core) & 3
    place = jnp.zeros_like(entries)
    for s in range(4):
        m = jnp.zeros_like(entries)
        for k in range(4):
            m = m + (bits[CYCLE[(k + s) % 4]] << k)
        place = jnp.where(turn == s, m, place)
    return half * 2048 + place * 128 + (entries & 127)


def table_kernel(place_ref, nbr_ref, token_ref, out_ref, wide):
    nbr = nbr_ref[...]
    places = column_of(jnp.maximum(nbr, 0), place_ref[0], place_ref[1])
    live = nbr >= 0
    high = jnp.where(live, places & 4032, -64).astype(F32).astype(BF)
    low = jnp.where(live, places & 63, 0).astype(F32).astype(BF)
    slot = lax.broadcasted_iota(I32, (32, 2048), 0) & 15
    spread = jnp.where(slot == (lax.broadcasted_iota(I32, (32, 2048), 1) >> 7), 1.0, 0.0).astype(BF)
    wide[...] = dot(jnp.concatenate([high, low], axis=1), spread).astype(I32).astype(I16)
    base = lax.broadcasted_iota(I32, (256, 128), 1)
    one, zero = jnp.ones((), BF), jnp.zeros((), BF)

    @pl.loop(0, 32)
    def _(t):
        lanes = (base + t * 128).astype(I16)
        acc = jnp.zeros((256, 128), BF)
        for slot in range(16):
            acc = acc + jnp.where(wide[:, pl.ds(slot * 128, 128)] == lanes, one, zero)
        out_ref[:, pl.ds(pl.multiple_of(t * 128, 128), 128)] = acc


def cite_table(place, nbr, token):
    return pl.pallas_call(
        table_kernel,
        out_shape=shape((256, 4096), BF),
        in_specs=[IN_SMEM, IN_VMEM, ANYWHERE],
        out_specs=IN_VMEM,
        scratch_shapes=[pltpu.VMEM((256, 2048), I16)],
        compiler_params=params(16),
        cost_estimate=pl.CostEstimate(flops=10**9, bytes_accessed=3 * 10**6, transcendentals=0),
        name="cite_table",
    )(place, nbr, token)


def back_table_kernel(place_ref, a_ref, b_ref, token_ref, out_ref):
    own = (lax.broadcasted_iota(I32, (256, 128), 0) + place_ref[0] * 256).astype(I16)
    one, zero = jnp.ones((), BF), jnp.zeros((), BF)
    for m in range(16):
        lists = (a_ref if m < 8 else b_ref)[m % 8].astype(I16)
        for h in range(2):
            acc = jnp.zeros((256, 128), BF)
            for slot in range(16):
                acc = acc + jnp.where(lists[slot : slot + 1, 128 * h : 128 * h + 128] == own, one, zero)
            place = m if h == 0 else (m >> 2) | ((m & 3) << 2)
            out_ref[:, pl.ds(h * 2048 + place * 128, 128)] = acc


def cited_by_table(place, a, b, token):
    return pl.pallas_call(
        back_table_kernel,
        out_shape=shape((256, 4096), BF),
        in_specs=[IN_SMEM, IN_VMEM, IN_VMEM, ANYWHERE],
        out_specs=IN_VMEM,
        compiler_params=params(16),
        cost_estimate=pl.CostEstimate(flops=10**9, bytes_accessed=3 * 10**6, transcendentals=0),
        name="cited_by_table",
    )(place, a, b, token)


def edge_lists(write_src, write_dst):
    none = jnp.full_like(write_src, -1)
    pick = jnp.concatenate([write_src, jnp.where(write_dst >= 0, write_dst + 256, -1)], axis=1)
    into_paper = jnp.concatenate([write_dst, none], axis=1)
    into_author = jnp.concatenate([none, write_src], axis=1)
    return pick.reshape(-1), into_paper.reshape(1, -1), into_author.reshape(1, -1)


def exchange(rows):
    sent = rows.reshape(128, 8, rows.shape[-1])
    got = lax.all_to_all(sent, ("row", "col"), split_axis=0, concat_axis=0, tiled=True)
    return got.reshape(1024, rows.shape[-1])


def other_core(value):
    return lax.ppermute(value, "row", [(i, i ^ 1) for i in range(8)])


def over_y(parts):
    got = [parts[0]]
    for d in range(1, 4):
        perm = [(2 * y + c, 2 * ((y + d) % 4) + c) for y in range(4) for c in range(2)]
        got.append(lax.ppermute(parts[d], "row", perm))
    return got


def silu_and_slope(value):
    sigma = 1.0 / (1.0 + jnp.exp(-value))
    return (value * sigma).astype(BF), sigma * (1.0 + value * (1.0 - sigma))


def author_kernel(
    arrived_ref, into_paper_ref, into_author_ref, x_author_ref, x_paper_ref, grad_ref,
    w_sa_hbm, w_wn_hbm, w_sp_hbm, w_wr_hbm,
    out_ref, pack_ref, dz_ref, dx_ref, pre_ref, adder_ref, cnt_ref,
    w_sa, w_wn, w_sp, w_wr, sems,
):
    copies = []
    for i, (a, b) in enumerate(((w_sa_hbm, w_sa), (w_wn_hbm, w_wn), (w_sp_hbm, w_sp), (w_wr_hbm, w_wr))):
        copies.append(pltpu.make_async_copy(a, b, sems.at[i]))
        copies[-1].start()
    ids = lax.broadcasted_iota(I32, (256, 1024), 0)
    means = []
    for i, ref in enumerate((into_paper_ref, into_author_ref)):
        hit = jnp.where(ref[...] == ids, 1.0, 0.0)
        cnt = jnp.maximum(jnp.sum(hit, axis=1, keepdims=True), 1.0)
        cnt_ref[pl.ds(256 * i, 256), :] = jnp.broadcast_to(cnt, (256, 128))
        hit = hit.astype(BF)
        adder_ref[pl.ds(256 * i, 256), :] = hit
        means.append((dot(hit, arrived_ref[...]) / cnt).astype(BF))
    written, authored = means
    x_author, x_paper = x_author_ref[...], x_paper_ref[...]
    copies[0].wait()
    copies[1].wait()
    pre = dot(x_author, w_sa[...]) + dot(authored, w_wn[...])
    out, slope = silu_and_slope(pre)
    out_ref[...] = out
    dpre = (grad_ref[...].astype(F32) * slope).astype(BF)
    pack_ref[:, pl.ds(0, 768)] = x_author
    pack_ref[:, pl.ds(768, 768)] = authored
    pack_ref[:, pl.ds(1536, 768)] = x_paper
    pack_ref[:, pl.ds(2304, 768)] = written
    pack_ref[:, pl.ds(3072, 1024)] = dpre
    dz_ref[...] = (dot(dpre, w_wn[...], ((1,), (1,))) / cnt_ref[pl.ds(256, 256), pl.ds(0, 1)]).astype(BF)
    dx_ref[...] = dot(dpre, w_sa[...], ((1,), (1,)))
    copies[2].wait()
    copies[3].wait()
    pre_ref[...] = dot(x_paper, w_sp[...]) + dot(written, w_wr[...])


def author_step(arrived, into_paper, into_author, x_author, x_paper, grad, w_sa, w_wn, w_sp, w_wr):
    weight = pltpu.VMEM((768, 1024), BF)
    return pl.pallas_call(
        author_kernel,
        out_shape=[
            shape((256, 1024), BF), shape((256, 4096), BF), shape((256, 768), BF), shape((256, 768), F32),
            shape((256, 1024), F32), shape((512, 1024), BF), shape((512, 128), F32),
        ],
        in_specs=[IN_VMEM] * 6 + [ANYWHERE] * 4,
        out_specs=[IN_VMEM] * 7,
        scratch_shapes=[weight] * 4 + [pltpu.SemaphoreType.DMA((4,))],
        compiler_params=params(40),
        cost_estimate=pl.CostEstimate(flops=4 * 10**9, bytes_accessed=15 * 10**6, transcendentals=0),
        name="author_step",
    )(arrived, into_paper, into_author, x_author, x_paper, grad, w_sa, w_wn, w_sp, w_wr)


def first_kernel(table_ref, b0, b1, out_ref):
    acc = dot(table_ref[:, pl.ds(0, 1024)], b0[...]) + dot(table_ref[:, pl.ds(2048, 1024)], b1[...])
    out_ref[...] = acc


def first_half(table, blocks):
    return pl.pallas_call(
        first_kernel,
        out_shape=shape((256, 768), F32),
        in_specs=[IN_VMEM] * 3,
        out_specs=IN_VMEM,
        compiler_params=params(24),
        cost_estimate=pl.CostEstimate(flops=2 * 10**9, bytes_accessed=5 * 10**6, transcendentals=0),
        name="first_half",
    )(table, *blocks)


def last_kernel(table_ref, b0, b1, first_ref, own_ref, out_ref):
    acc = dot(table_ref[:, pl.ds(1024, 1024)], b0[...]) + dot(table_ref[:, pl.ds(3072, 1024)], b1[...])
    out_ref[...] = (acc + (first_ref[...] + own_ref[...])).astype(BF)


def last_half(table, blocks, first, own):
    return pl.pallas_call(
        last_kernel,
        out_shape=shape((256, 768), BF),
        in_specs=[IN_VMEM] * 5,
        out_specs=IN_VMEM,
        compiler_params=params(24),
        cost_estimate=pl.CostEstimate(flops=2 * 10**9, bytes_accessed=5 * 10**6, transcendentals=0),
        name="last_half",
    )(table, *blocks, first, own)


def edge_add_kernel(adder_ref, back_ref, author_ref, paper_ref, out_ref, sum_ref):
    back = back_ref[...]
    sum_ref[...] = paper_ref[...] + dot(adder_ref[pl.ds(0, 256), :], back)
    out_ref[...] = (author_ref[...] + dot(adder_ref[pl.ds(256, 256), :], back)).astype(BF)


def edge_add(adder, back, author, paper):
    return pl.pallas_call(
        edge_add_kernel,
        out_shape=[shape((256, 768), BF), shape((256, 768), F32)],
        in_specs=[IN_VMEM] * 4,
        out_specs=[IN_VMEM] * 2,
        compiler_params=params(16),
        cost_estimate=pl.CostEstimate(flops=10**9, bytes_accessed=5 * 10**6, transcendentals=0),
        name="edge_add",
    )(adder, back, author, paper)


def paper_kernel(
    table_ref, b0, b1, first_ref, nbr_ref, pre_ref, grad_ref, w_hbm, token_ref,
    out_ref, pack_ref, dz_ref, w_ref, sem,
):
    copy = pltpu.make_async_copy(w_hbm, w_ref, sem)
    copy.start()
    total = first_ref[...]
    for h, block in enumerate((b0, b1)):
        total = total + dot(table_ref[:, pl.ds(h * 2048 + 1024, 1024)], block[...])
    cnt = jnp.sum(jnp.where(nbr_ref[...] >= 0, 1.0, 0.0), axis=1, keepdims=True)
    cnt = jnp.maximum(cnt, 1.0)
    cited = (total / cnt).astype(BF)
    pack_ref[:, pl.ds(0, 768)] = cited
    copy.wait()
    out, slope = silu_and_slope(pre_ref[...] + dot(cited, w_ref[...]))
    out_ref[...] = out
    dpre = (grad_ref[...].astype(F32) * slope).astype(BF)
    pack_ref[:, pl.ds(768, 1024)] = dpre
    dz_ref[...] = (dot(dpre, w_ref[...], ((1,), (1,))) / cnt).astype(BF)


def paper_step(table, blocks, first, nbr, pre, grad, w_cite, token):
    return pl.pallas_call(
        paper_kernel,
        out_shape=[shape((256, 1024), BF), shape((256, 1792), BF), shape((256, 768), BF)],
        in_specs=[IN_VMEM] * 7 + [ANYWHERE] * 2,
        out_specs=[IN_VMEM] * 3,
        scratch_shapes=[pltpu.VMEM((768, 1024), BF), pltpu.SemaphoreType.DMA],
        compiler_params=params(32),
        cost_estimate=pl.CostEstimate(flops=3 * 10**9, bytes_accessed=10 * 10**6, transcendentals=0),
        name="paper_step",
    )(table, *blocks, first, nbr, pre, grad, w_cite, token)


def edge_back_kernel(pack_ref, cnt_ref, w_wr_hbm, w_sp_hbm, dz_ref, dx_ref, w_wr, w_sp, sems):
    copies = [pltpu.make_async_copy(w_wr_hbm, w_wr, sems.at[0]), pltpu.make_async_copy(w_sp_hbm, w_sp, sems.at[1])]
    for copy in copies:
        copy.start()
    dpre = pack_ref[:, pl.ds(768, 1024)]
    copies[0].wait()
    dz_ref[...] = (dot(dpre, w_wr[...], ((1,), (1,))) / cnt_ref[pl.ds(0, 256), pl.ds(0, 1)]).astype(BF)
    copies[1].wait()
    dx_ref[...] = dot(dpre, w_sp[...], ((1,), (1,)))


def edge_back(pack, cnt, w_write, w_self):
    return pl.pallas_call(
        edge_back_kernel,
        out_shape=[shape((256, 768), BF), shape((256, 768), F32)],
        in_specs=[IN_VMEM, IN_VMEM, ANYWHERE, ANYWHERE],
        out_specs=[IN_VMEM] * 2,
        scratch_shapes=[pltpu.VMEM((768, 1024), BF)] * 2 + [pltpu.SemaphoreType.DMA((2,))],
        compiler_params=params(16),
        cost_estimate=pl.CostEstimate(flops=10**9, bytes_accessed=5 * 10**6, transcendentals=0),
        name="edge_back",
    )(pack, cnt, w_write, w_self)


def weight_kernel(lefts, right, place_ref, *refs):
    ins, outs, turned = refs[:-5], refs[-5:-1], refs[-1]
    core, y = place_ref[1], place_ref[2]
    own, other, lane = right
    dpre = jnp.concatenate([ins[own][:, pl.ds(lane, 1024)], ins[other][:, pl.ds(lane, 1024)]], axis=0)
    for i, (own, other, lane) in enumerate(lefts):
        for k, ref in enumerate((ins[own], ins[other])):
            turned[i, :, pl.ds(256 * k, 256)] = ref[:, pl.ds(lane, 768)].T
        rows = []
        for d in range(4):
            start = pl.multiple_of((2 * ((y + d) & 3) + core) * 96, 32)
            rows.append(turned[i, pl.ds(start, 96), :])
        product = dot(jnp.concatenate(rows, axis=0), dpre).astype(BF)
        for d in range(4):
            outs[d][i] = product[96 * d : 96 * d + 96]


def weight_parts(place, arrays, lefts, right):
    n = len(lefts)
    return pl.pallas_call(
        functools.partial(weight_kernel, lefts, right),
        out_shape=[shape((n, 96, 1024), BF)] * 4,
        in_specs=[IN_SMEM] + [IN_VMEM] * len(arrays),
        out_specs=[IN_VMEM] * 4,
        scratch_shapes=[pltpu.VMEM((n, 768, 512), BF)],
        compiler_params=params(32),
        cost_estimate=pl.CostEstimate(flops=2 * 10**9, bytes_accessed=8 * 10**6, transcendentals=0),
        name="weight_parts",
    )(place, *arrays)


def y_sum_kernel(*refs):
    papers, authors, out_ref, stack = refs[:4], refs[4:8], refs[8], refs[9]
    for m in range(5):
        group, i = (papers, m) if m < 3 else (authors, m - 3)
        total = group[0][i].astype(F32)
        for y in range(1, 4):
            total = total + group[y][i].astype(F32)
        stack[pl.ds(96 * m, 96), :] = total
    stack[pl.ds(480, 32), :] = jnp.zeros((32, 1024), F32)
    for j in range(0, 16, 2):
        turned = stack[:, pl.ds(64 * j, 128)].T.astype(BF)
        out_ref[j] = turned[:64]
        out_ref[j + 1] = turned[64:]


def y_sum(paper, author):
    return pl.pallas_call(
        y_sum_kernel,
        out_shape=shape((16, 64, 512), BF),
        in_specs=[IN_VMEM] * 8,
        out_specs=IN_VMEM,
        scratch_shapes=[pltpu.VMEM((512, 1024), F32)],
        compiler_params=params(20),
        name="y_sum",
    )(*paper, *author)


def last_sum_kernel(got_ref, out_ref):
    total = got_ref[0].astype(F32)
    for j in range(1, 16):
        total = total + got_ref[j].astype(F32)
    total = total * (32768.0 ** -0.5)
    for m in range(5):
        out_ref[m] = total[:, 96 * m : 96 * m + 96]


def last_sum(got):
    return pl.pallas_call(
        last_sum_kernel,
        out_shape=shape((5, 64, 96), F32),
        in_specs=[IN_VMEM],
        out_specs=IN_VMEM,
        compiler_params=params(8),
        name="last_sum",
    )(got)


def per_device(
    x_paper, x_author, cite_nbr, write_src, write_dst,
    w_self_paper, w_cite, w_write, w_self_author, w_written, grad_paper, grad_author,
):
    row = lax.axis_index("row")
    place = jnp.stack([lax.axis_index("col"), row & 1, row >> 1]).astype(I32)

    parts = [x_paper[:128], x_paper[128:], cite_nbr.T.reshape(1, 16, 256)]
    parts = join(travel(parts, 0))

    pick, into_paper, into_author = edge_lists(write_src[0], write_dst[0])
    picker = (pick[:, None] == lax.iota(I32, 512)[None, :]).astype(BF)
    rows = dot(picker, jnp.concatenate([x_author, x_paper], axis=0)).astype(BF)
    arrived = exchange(rows)

    table = cite_table(place, cite_nbr, parts[0])
    parts = join(travel(parts, 1), (table,))
    parts = join(travel(parts, 2))
    pairs = travel(parts, 3)
    cite_first = first_half(table, [pair[0] for pair in pairs[:2]])

    out_author, pack_a, dz_written, dx_author_own, pre_paper, adder, cnt = author_step(
        arrived, into_paper, into_author, x_author, x_paper, grad_author,
        w_self_author, w_written, w_self_paper, w_write,
    )
    pack_a_other = other_core(pack_a)
    parts_author = weight_parts(place, [pack_a, pack_a_other], [(0, 1, 0), (0, 1, 768)], (0, 1, 3072))
    got_author = over_y(parts_author)

    out_paper, pack_p, dz_cite = paper_step(
        table, [pair[1] for pair in pairs[:2]], cite_first, cite_nbr, pre_paper, grad_paper, w_cite, parts_author[0]
    )
    pack_p_other = other_core(pack_p)
    back_pairs = travel([dz_cite[:128], dz_cite[128:]], 0)
    dz_write, dx_paper_own = edge_back(pack_p, cnt, w_write, w_self_paper)
    parts_paper = weight_parts(
        place, [pack_a, pack_a_other, pack_p, pack_p_other],
        [(0, 1, 1536), (2, 3, 0), (0, 1, 2304)], (2, 3, 768),
    )
    parts = join(back_pairs, (parts_paper[0],))
    got_paper = over_y(parts_paper)
    rows = dot(picker, jnp.concatenate([dz_written, dz_write], axis=0)).astype(BF)
    parts = join(travel(parts, 1), (rows,))
    back = exchange(rows)
    back_table = cited_by_table(place, pairs[2][0], pairs[2][1], parts[0])
    parts = join(travel(parts, 2), (back_table,))
    back_pairs = travel(parts, 3)
    back_first = first_half(back_table, [pair[0] for pair in back_pairs])

    got = lax.all_to_all(y_sum(got_paper, got_author), "col", split_axis=0, concat_axis=0, tiled=True)
    dweights = last_sum(got).transpose(0, 2, 1)

    dx_author, dx_paper_own = edge_add(adder, back, dx_author_own, dx_paper_own)
    dx_paper = last_half(back_table, [pair[1] for pair in back_pairs], back_first, dx_paper_own)
    return (out_paper, out_author, dx_paper, dx_author, dweights)


def solution(mesh):
    part = P(("row", "col"), None)
    part3 = P(("row", "col"), None, None)
    return jax.shard_map(
        per_device,
        mesh=mesh,
        in_specs=(part, part, part, part3, part3, P(), P(), P(), P(), P(), part, part),
        out_specs=(part, part, part, part, P(None, "row", "col")),
        check_vma=False,
    )
```

```python
import functools

import jax
import jax.numpy as jnp
from jax import lax
from jax.experimental import pallas as pl
from jax.experimental.pallas import tpu as pltpu
from jax.sharding import PartitionSpec as P

BF = jnp.bfloat16
F32 = jnp.float32
I32 = jnp.int32
MIB = 1024 * 1024
I16 = jnp.int16
CYCLE = (4, 1, 12, 3)
IN_VMEM = pl.BlockSpec(memory_space=pltpu.VMEM)
ANYWHERE = pl.BlockSpec(memory_space=pl.ANY)
IN_HBM = pl.BlockSpec(memory_space=pltpu.HBM)
IN_SMEM = pl.BlockSpec(memory_space=pltpu.SMEM)


def dot(a, b, dims=((1,), (0,))):
    return lax.dot_general(a, b, (dims, ((), ())), preferred_element_type=F32)


def shape(dims, kind):
    return jax.ShapeDtypeStruct(dims, kind)


def params(mib):
    return pltpu.CompilerParams(vmem_limit_bytes=mib * MIB)


def join_kernel(n, *refs):
    outs = refs[len(refs) - n :]
    for i in range(n):
        a, b, out = refs[2 * i], refs[2 * i + 1], outs[i]
        rows = a.shape[0]
        out[pl.ds(0, rows)] = a[...]
        out[pl.ds(rows, rows)] = b[...]


def join(pairs, tokens=()):
    n = len(pairs)
    flat = [v for pair in pairs for v in pair]
    outs = [shape((2 * a.shape[0],) + a.shape[1:], a.dtype) for a, _ in pairs]
    return pl.pallas_call(
        functools.partial(join_kernel, n),
        out_shape=outs,
        in_specs=[IN_VMEM] * (2 * n) + [ANYWHERE] * len(tokens),
        out_specs=[IN_VMEM] * n,
        compiler_params=params(16),
        name="join",
    )(*flat, *tokens)


def travel(parts, k):
    pairs = []
    for h, part in enumerate(parts):
        masks = [CYCLE[(k + 2 * (h & 1) + c) % 4] for c in range(2)]
        perm = [(r * 16 + c, r * 16 + (c ^ masks[r & 1])) for r in range(8) for c in range(16)]
        pairs.append((part, lax.ppermute(part, ("row", "col"), perm)))
    return pairs


def column_of(entries, col, core):
    diff = (entries >> 8) ^ col
    bits = {}
    for axis, (near, far) in enumerate(((4, 12), (1, 3))):
        d = ((diff >> 2) & 3) if axis == 0 else (diff & 3)
        bits[far] = d >> 1
        bits[near] = (d & 1) ^ (d >> 1)
    half = (entries >> 7) & 1
    turn = (2 * half + core) & 3
    place = jnp.zeros_like(entries)
    for s in range(4):
        m = jnp.zeros_like(entries)
        for k in range(4):
            m = m + (bits[CYCLE[(k + s) % 4]] << k)
        place = jnp.where(turn == s, m, place)
    return half * 2048 + place * 128 + (entries & 127)


def table_kernel(place_ref, nbr_ref, token_ref, out_ref, wide):
    nbr = nbr_ref[...]
    places = column_of(jnp.maximum(nbr, 0), place_ref[0], place_ref[1])
    live = nbr >= 0
    high = jnp.where(live, places & 4032, -64).astype(F32).astype(BF)
    low = jnp.where(live, places & 63, 0).astype(F32).astype(BF)
    slot = lax.broadcasted_iota(I32, (32, 2048), 0) & 15
    spread = jnp.where(slot == (lax.broadcasted_iota(I32, (32, 2048), 1) >> 7), 1.0, 0.0).astype(BF)
    wide[...] = dot(jnp.concatenate([high, low], axis=1), spread).astype(I32).astype(I16)
    base = lax.broadcasted_iota(I32, (256, 128), 1)
    one, zero = jnp.ones((), BF), jnp.zeros((), BF)

    @pl.loop(0, 32)
    def _(t):
        lanes = (base + t * 128).astype(I16)
        acc = jnp.zeros((256, 128), BF)
        for slot in range(16):
            acc = acc + jnp.where(wide[:, pl.ds(slot * 128, 128)] == lanes, one, zero)
        out_ref[:, pl.ds(pl.multiple_of(t * 128, 128), 128)] = acc


def cite_table(place, nbr, token):
    return pl.pallas_call(
        table_kernel,
        out_shape=shape((256, 4096), BF),
        in_specs=[IN_SMEM, IN_VMEM, ANYWHERE],
        out_specs=IN_VMEM,
        scratch_shapes=[pltpu.VMEM((256, 2048), I16)],
        compiler_params=params(16),
        cost_estimate=pl.CostEstimate(flops=10**9, bytes_accessed=3 * 10**6, transcendentals=0),
        name="cite_table",
    )(place, nbr, token)


def back_table_kernel(place_ref, a_ref, b_ref, token_ref, out_ref):
    own = (lax.broadcasted_iota(I32, (256, 128), 0) + place_ref[0] * 256).astype(I16)
    one, zero = jnp.ones((), BF), jnp.zeros((), BF)
    for m in range(16):
        lists = (a_ref if m < 8 else b_ref)[m % 8].astype(I16)
        for h in range(2):
            acc = jnp.zeros((256, 128), BF)
            for slot in range(16):
                acc = acc + jnp.where(lists[slot : slot + 1, 128 * h : 128 * h + 128] == own, one, zero)
            place = m if h == 0 else (m >> 2) | ((m & 3) << 2)
            out_ref[:, pl.ds(h * 2048 + place * 128, 128)] = acc


def cited_by_table(place, a, b, token):
    return pl.pallas_call(
        back_table_kernel,
        out_shape=shape((256, 4096), BF),
        in_specs=[IN_SMEM, IN_VMEM, IN_VMEM, ANYWHERE],
        out_specs=IN_VMEM,
        compiler_params=params(16),
        cost_estimate=pl.CostEstimate(flops=10**9, bytes_accessed=3 * 10**6, transcendentals=0),
        name="cited_by_table",
    )(place, a, b, token)


def edge_lists(write_src, write_dst):
    none = jnp.full_like(write_src, -1)
    pick = jnp.concatenate([write_src, jnp.where(write_dst >= 0, write_dst + 256, -1)], axis=1)
    into_paper = jnp.concatenate([write_dst, none], axis=1)
    into_author = jnp.concatenate([none, write_src], axis=1)
    return pick.reshape(1, -1), into_paper.reshape(1, -1), into_author.reshape(1, -1)


def exchange(rows):
    sent = rows.reshape(128, 8, rows.shape[-1])
    got = lax.all_to_all(sent, ("row", "col"), split_axis=0, concat_axis=0, tiled=True)
    return got.reshape(1024, rows.shape[-1])


def pick_kernel(pick_ref, a_ref, b_ref, token_ref, out_ref):
    hit = jnp.where(lax.broadcasted_iota(I32, (512, 1024), 0) == pick_ref[...], 1.0, 0.0).astype(BF)
    rows = dot(hit[:256], a_ref[...], ((0,), (0,))) + dot(hit[256:], b_ref[...], ((0,), (0,)))
    out_ref[...] = rows.astype(BF)


def pick_rows(pick, authors, papers, token):
    return pl.pallas_call(
        pick_kernel,
        out_shape=shape((1024, 768), BF),
        in_specs=[IN_VMEM] * 3 + [ANYWHERE],
        out_specs=IN_VMEM,
        compiler_params=params(16),
        cost_estimate=pl.CostEstimate(flops=10**9, bytes_accessed=3 * 10**6, transcendentals=0),
        name="pick_rows",
    )(pick, authors, papers, token)


def other_core(value):
    return lax.ppermute(value, "row", [(i, i ^ 1) for i in range(8)])


def over_y(parts):
    got = [parts[0]]
    for d in range(1, 4):
        perm = [(2 * y + c, 2 * ((y + d) % 4) + c) for y in range(4) for c in range(2)]
        got.append(lax.ppermute(parts[d], "row", perm))
    return got


def silu_and_slope(value):
    sigma = 1.0 / (1.0 + jnp.exp(-value))
    return (value * sigma).astype(BF), sigma * (1.0 + value * (1.0 - sigma))


def author_kernel(
    arrived_ref, into_paper_ref, into_author_ref, *refs
):
    sources, outs, held, sems = refs[:7], refs[7:14], refs[14:21], refs[21]
    out_ref, pack_ref, dz_ref, dx_ref, pre_ref, adder_ref, cnt_ref = outs
    x_author_ref, x_paper_ref, grad_ref, w_sa, w_wn, w_sp, w_wr = held
    copies = [pltpu.make_async_copy(a, b, sems.at[i]) for i, (a, b) in enumerate(zip(sources, held))]
    for i in (0, 3, 4, 2, 1, 5, 6):
        copies[i].start()
    ids = lax.broadcasted_iota(I32, (256, 1024), 0)
    means = []
    for i, ref in enumerate((into_paper_ref, into_author_ref)):
        hit = jnp.where(ref[...] == ids, 1.0, 0.0)
        cnt = jnp.maximum(jnp.sum(hit, axis=1, keepdims=True), 1.0)
        cnt_ref[pl.ds(256 * i, 256), :] = jnp.broadcast_to(cnt, (256, 128))
        hit = hit.astype(BF)
        adder_ref[pl.ds(256 * i, 256), :] = hit
        means.append((dot(hit, arrived_ref[...]) / cnt).astype(BF))
    written, authored = means
    for i in (0, 3, 4):
        copies[i].wait()
    x_author = x_author_ref[...]
    pre = dot(x_author, w_sa[...]) + dot(authored, w_wn[...])
    out, slope = silu_and_slope(pre)
    out_ref[...] = out
    copies[2].wait()
    copies[1].wait()
    x_paper = x_paper_ref[...]
    dpre = (grad_ref[...].astype(F32) * slope).astype(BF)
    pack_ref[:, pl.ds(0, 768)] = x_author
    pack_ref[:, pl.ds(768, 768)] = authored
    pack_ref[:, pl.ds(1536, 768)] = x_paper
    pack_ref[:, pl.ds(2304, 768)] = written
    pack_ref[:, pl.ds(3072, 1024)] = dpre
    dz_ref[...] = (dot(dpre, w_wn[...], ((1,), (1,))) / cnt_ref[pl.ds(256, 256), pl.ds(0, 1)]).astype(BF)
    dx_ref[...] = dot(dpre, w_sa[...], ((1,), (1,)))
    copies[5].wait()
    copies[6].wait()
    pre_ref[...] = dot(x_paper, w_sp[...]) + dot(written, w_wr[...])


def author_step(arrived, into_paper, into_author, x_author, x_paper, grad, w_sa, w_wn, w_sp, w_wr):
    weight = pltpu.VMEM((768, 1024), BF)
    return pl.pallas_call(
        author_kernel,
        out_shape=[
            shape((256, 1024), BF), shape((256, 4096), BF), shape((256, 768), BF), shape((256, 768), F32),
            shape((256, 1024), F32), shape((512, 1024), BF), shape((512, 128), F32),
        ],
        in_specs=[IN_VMEM] * 3 + [IN_HBM] * 7,
        out_specs=[IN_VMEM] * 7,
        scratch_shapes=[pltpu.VMEM((256, 768), BF)] * 2 + [pltpu.VMEM((256, 1024), BF)] + [weight] * 4
        + [pltpu.SemaphoreType.DMA((7,))],
        compiler_params=params(40),
        cost_estimate=pl.CostEstimate(flops=4 * 10**9, bytes_accessed=15 * 10**6, transcendentals=0),
        name="author_step",
    )(arrived, into_paper, into_author, x_author, x_paper, grad, w_sa, w_wn, w_sp, w_wr)


def first_kernel(table_ref, b0, b1, out_ref):
    acc = dot(table_ref[:, pl.ds(0, 1024)], b0[...]) + dot(table_ref[:, pl.ds(2048, 1024)], b1[...])
    out_ref[...] = acc


def first_half(table, blocks):
    return pl.pallas_call(
        first_kernel,
        out_shape=shape((256, 768), F32),
        in_specs=[IN_VMEM] * 3,
        out_specs=IN_VMEM,
        compiler_params=params(24),
        cost_estimate=pl.CostEstimate(flops=2 * 10**9, bytes_accessed=5 * 10**6, transcendentals=0),
        name="first_half",
    )(table, *blocks)


def last_kernel(table_ref, b0, b1, first_ref, own_ref, out_ref):
    acc = dot(table_ref[:, pl.ds(1024, 1024)], b0[...]) + dot(table_ref[:, pl.ds(3072, 1024)], b1[...])
    out_ref[...] = (acc + (first_ref[...] + own_ref[...])).astype(BF)


def last_half(table, blocks, first, own):
    return pl.pallas_call(
        last_kernel,
        out_shape=shape((256, 768), BF),
        in_specs=[IN_VMEM] * 5,
        out_specs=IN_VMEM,
        compiler_params=params(24),
        cost_estimate=pl.CostEstimate(flops=2 * 10**9, bytes_accessed=5 * 10**6, transcendentals=0),
        name="last_half",
    )(table, *blocks, first, own)


def edge_add_kernel(adder_ref, back_ref, author_ref, paper_ref, out_ref, sum_ref):
    back = back_ref[...]
    sum_ref[...] = paper_ref[...] + dot(adder_ref[pl.ds(0, 256), :], back)
    out_ref[...] = (author_ref[...] + dot(adder_ref[pl.ds(256, 256), :], back)).astype(BF)


def edge_add(adder, back, author, paper):
    return pl.pallas_call(
        edge_add_kernel,
        out_shape=[shape((256, 768), BF), shape((256, 768), F32)],
        in_specs=[IN_VMEM] * 4,
        out_specs=[IN_VMEM] * 2,
        compiler_params=params(16),
        cost_estimate=pl.CostEstimate(flops=10**9, bytes_accessed=5 * 10**6, transcendentals=0),
        name="edge_add",
    )(adder, back, author, paper)


def paper_kernel(
    table_ref, b0, b1, first_ref, nbr_ref, pre_ref, grad_hbm, w_hbm, token_ref,
    out_ref, pack_ref, dz_ref, grad_ref, w_ref, sems,
):
    copies = [pltpu.make_async_copy(w_hbm, w_ref, sems.at[0]), pltpu.make_async_copy(grad_hbm, grad_ref, sems.at[1])]
    for copy in copies:
        copy.start()
    total = first_ref[...]
    for h, block in enumerate((b0, b1)):
        total = total + dot(table_ref[:, pl.ds(h * 2048 + 1024, 1024)], block[...])
    cnt = jnp.sum(jnp.where(nbr_ref[...] >= 0, 1.0, 0.0), axis=1, keepdims=True)
    cnt = jnp.maximum(cnt, 1.0)
    cited = (total / cnt).astype(BF)
    pack_ref[:, pl.ds(0, 768)] = cited
    copies[0].wait()
    out, slope = silu_and_slope(pre_ref[...] + dot(cited, w_ref[...]))
    out_ref[...] = out
    copies[1].wait()
    dpre = (grad_ref[...].astype(F32) * slope).astype(BF)
    pack_ref[:, pl.ds(768, 1024)] = dpre
    dz_ref[...] = (dot(dpre, w_ref[...], ((1,), (1,))) / cnt).astype(BF)


def paper_step(table, blocks, first, nbr, pre, grad, w_cite, token):
    return pl.pallas_call(
        paper_kernel,
        out_shape=[shape((256, 1024), BF), shape((256, 1792), BF), shape((256, 768), BF)],
        in_specs=[IN_VMEM] * 6 + [IN_HBM] * 2 + [ANYWHERE],
        out_specs=[IN_VMEM] * 3,
        scratch_shapes=[pltpu.VMEM((256, 1024), BF), pltpu.VMEM((768, 1024), BF), pltpu.SemaphoreType.DMA((2,))],
        compiler_params=params(32),
        cost_estimate=pl.CostEstimate(flops=3 * 10**9, bytes_accessed=10 * 10**6, transcendentals=0),
        name="paper_step",
    )(table, *blocks, first, nbr, pre, grad, w_cite, token)


def edge_back_kernel(pack_ref, cnt_ref, w_wr_hbm, w_sp_hbm, dz_ref, dx_ref, w_wr, w_sp, sems):
    copies = [pltpu.make_async_copy(w_wr_hbm, w_wr, sems.at[0]), pltpu.make_async_copy(w_sp_hbm, w_sp, sems.at[1])]
    for copy in copies:
        copy.start()
    dpre = pack_ref[:, pl.ds(768, 1024)]
    copies[0].wait()
    dz_ref[...] = (dot(dpre, w_wr[...], ((1,), (1,))) / cnt_ref[pl.ds(0, 256), pl.ds(0, 1)]).astype(BF)
    copies[1].wait()
    dx_ref[...] = dot(dpre, w_sp[...], ((1,), (1,)))


def edge_back(pack, cnt, w_write, w_self):
    return pl.pallas_call(
        edge_back_kernel,
        out_shape=[shape((256, 768), BF), shape((256, 768), F32)],
        in_specs=[IN_VMEM, IN_VMEM, IN_HBM, IN_HBM],
        out_specs=[IN_VMEM] * 2,
        scratch_shapes=[pltpu.VMEM((768, 1024), BF)] * 2 + [pltpu.SemaphoreType.DMA((2,))],
        compiler_params=params(16),
        cost_estimate=pl.CostEstimate(flops=10**9, bytes_accessed=5 * 10**6, transcendentals=0),
        name="edge_back",
    )(pack, cnt, w_write, w_self)


def weight_kernel(lefts, right, place_ref, *refs):
    ins, outs, turned = refs[:-5], refs[-5:-1], refs[-1]
    core, y = place_ref[1], place_ref[2]
    own, other, lane = right
    dpre = jnp.concatenate([ins[own][:, pl.ds(lane, 1024)], ins[other][:, pl.ds(lane, 1024)]], axis=0)
    for i, (own, other, lane) in enumerate(lefts):
        for k, ref in enumerate((ins[own], ins[other])):
            turned[i, :, pl.ds(256 * k, 256)] = ref[:, pl.ds(lane, 768)].T
        rows = []
        for d in range(4):
            start = pl.multiple_of((2 * ((y + d) & 3) + core) * 96, 32)
            rows.append(turned[i, pl.ds(start, 96), :])
        product = dot(jnp.concatenate(rows, axis=0), dpre).astype(BF)
        for d in range(4):
            outs[d][i] = product[96 * d : 96 * d + 96]


def weight_parts(place, arrays, lefts, right):
    n = len(lefts)
    return pl.pallas_call(
        functools.partial(weight_kernel, lefts, right),
        out_shape=[shape((n, 96, 1024), BF)] * 4,
        in_specs=[IN_SMEM] + [IN_VMEM] * len(arrays),
        out_specs=[IN_VMEM] * 4,
        scratch_shapes=[pltpu.VMEM((n, 768, 512), BF)],
        compiler_params=params(32),
        cost_estimate=pl.CostEstimate(flops=2 * 10**9, bytes_accessed=8 * 10**6, transcendentals=0),
        name="weight_parts",
    )(place, *arrays)


def y_sum_kernel(*refs):
    papers, authors, out_ref, stack = refs[:4], refs[4:8], refs[8], refs[9]
    for m in range(5):
        group, i = (papers, m) if m < 3 else (authors, m - 3)
        total = group[0][i].astype(F32)
        for y in range(1, 4):
            total = total + group[y][i].astype(F32)
        stack[pl.ds(96 * m, 96), :] = total
    stack[pl.ds(480, 32), :] = jnp.zeros((32, 1024), F32)
    for j in range(0, 16, 2):
        turned = stack[:, pl.ds(64 * j, 128)].T.astype(BF)
        out_ref[j] = turned[:64]
        out_ref[j + 1] = turned[64:]


def y_sum(paper, author):
    return pl.pallas_call(
        y_sum_kernel,
        out_shape=shape((16, 64, 512), BF),
        in_specs=[IN_VMEM] * 8,
        out_specs=IN_VMEM,
        scratch_shapes=[pltpu.VMEM((512, 1024), F32)],
        compiler_params=params(20),
        name="y_sum",
    )(*paper, *author)


def last_sum_kernel(got_ref, token_ref, out_ref):
    total = got_ref[0].astype(F32)
    for j in range(1, 16):
        total = total + got_ref[j].astype(F32)
    total = total * (32768.0 ** -0.5)
    for m in range(5):
        out_ref[m] = total[:, 96 * m : 96 * m + 96]


def last_sum(got, token):
    return pl.pallas_call(
        last_sum_kernel,
        out_shape=shape((5, 64, 96), F32),
        in_specs=[IN_VMEM, ANYWHERE],
        out_specs=IN_VMEM,
        compiler_params=params(8),
        name="last_sum",
    )(got, token)


def per_device(
    x_paper, x_author, cite_nbr, write_src, write_dst,
    w_self_paper, w_cite, w_write, w_self_author, w_written, grad_paper, grad_author,
):
    row = lax.axis_index("row")
    place = jnp.stack([lax.axis_index("col"), row & 1, row >> 1]).astype(I32)

    parts = [x_paper[:128], x_paper[128:], cite_nbr.T.reshape(1, 16, 256)]
    parts = join(travel(parts, 0))

    pick, into_paper, into_author = edge_lists(write_src[0], write_dst[0])
    arrived = exchange(pick_rows(pick, x_author, x_paper, parts[0]))
    parts = join(travel(parts, 1))

    table = cite_table(place, cite_nbr, parts[0])
    parts = join(travel(parts, 2), (table,))
    pairs = travel(parts, 3)
    cite_first = first_half(table, [pair[0] for pair in pairs[:2]])

    out_author, pack_a, dz_written, dx_author_own, pre_paper, adder, cnt = author_step(
        arrived, into_paper, into_author, x_author, x_paper, grad_author,
        w_self_author, w_written, w_self_paper, w_write,
    )
    pack_a_other = other_core(pack_a)
    parts_author = weight_parts(place, [pack_a, pack_a_other], [(0, 1, 0), (0, 1, 768)], (0, 1, 3072))
    got_author = over_y(parts_author)

    out_paper, pack_p, dz_cite = paper_step(
        table, [pair[1] for pair in pairs[:2]], cite_first, cite_nbr, pre_paper, grad_paper, w_cite, parts_author[0]
    )
    pack_p_other = other_core(pack_p)
    back_pairs = travel([dz_cite[:128], dz_cite[128:]], 0)
    dz_write, dx_paper_own = edge_back(pack_p, cnt, w_write, w_self_paper)
    parts_paper = weight_parts(
        place, [pack_a, pack_a_other, pack_p, pack_p_other],
        [(0, 1, 1536), (2, 3, 0), (0, 1, 2304)], (2, 3, 768),
    )
    rows = pick_rows(pick, dz_written, dz_write, dz_cite)
    parts = join(back_pairs, (parts_paper[0], rows, pairs[2][1], *got_author[1:]))
    got_paper = over_y(parts_paper)
    back = exchange(rows)
    parts = join(travel(parts, 1))
    back_table = cited_by_table(place, pairs[2][0], pairs[2][1], parts[0])
    parts = join(travel(parts, 2), (back_table, *got_paper[1:]))
    back_pairs = travel(parts, 3)
    back_first = first_half(back_table, [pair[0] for pair in back_pairs])

    got = lax.all_to_all(y_sum(got_paper, got_author), "col", split_axis=0, concat_axis=0, tiled=True)

    dx_author, dx_paper_own = edge_add(adder, back, dx_author_own, dx_paper_own)
    dx_paper = last_half(back_table, [pair[1] for pair in back_pairs], back_first, dx_paper_own)
    dweights = last_sum(got, dx_paper).transpose(0, 2, 1)
    return (out_paper, out_author, dx_paper, dx_author, dweights)


def solution(mesh):
    part = P(("row", "col"), None)
    part3 = P(("row", "col"), None, None)
    return jax.shard_map(
        per_device,
        mesh=mesh,
        in_specs=(part, part, part, part3, part3, P(), P(), P(), P(), P(), part, part),
        out_specs=(part, part, part, part, P(None, "row", "col")),
        check_vma=False,
    )
```

```python
import functools

import jax
import jax.numpy as jnp
from jax import lax
from jax.experimental import pallas as pl
from jax.experimental.pallas import tpu as pltpu
from jax.sharding import PartitionSpec as P

BF = jnp.bfloat16
F32 = jnp.float32
I32 = jnp.int32
MIB = 1024 * 1024
I16 = jnp.int16
CYCLE = (4, 1, 12, 3)
IN_VMEM = pl.BlockSpec(memory_space=pltpu.VMEM)
ANYWHERE = pl.BlockSpec(memory_space=pl.ANY)
IN_HBM = pl.BlockSpec(memory_space=pltpu.HBM)
IN_SMEM = pl.BlockSpec(memory_space=pltpu.SMEM)


def dot(a, b, dims=((1,), (0,))):
    return lax.dot_general(a, b, (dims, ((), ())), preferred_element_type=F32)


def shape(dims, kind):
    return jax.ShapeDtypeStruct(dims, kind)


def params(mib):
    return pltpu.CompilerParams(vmem_limit_bytes=mib * MIB)


def join_kernel(n, *refs):
    outs = refs[len(refs) - n :]
    for i in range(n):
        a, b, out = refs[2 * i], refs[2 * i + 1], outs[i]
        rows = a.shape[0]
        out[pl.ds(0, rows)] = a[...]
        out[pl.ds(rows, rows)] = b[...]


def join(pairs, tokens=()):
    n = len(pairs)
    flat = [v for pair in pairs for v in pair]
    outs = [shape((2 * a.shape[0],) + a.shape[1:], a.dtype) for a, _ in pairs]
    return pl.pallas_call(
        functools.partial(join_kernel, n),
        out_shape=outs,
        in_specs=[IN_VMEM] * (2 * n) + [ANYWHERE] * len(tokens),
        out_specs=[IN_VMEM] * n,
        compiler_params=params(16),
        name="join",
    )(*flat, *tokens)


def travel(parts, k):
    pairs = []
    for h, part in enumerate(parts):
        masks = [CYCLE[(k + 2 * (h & 1) + c) % 4] for c in range(2)]
        perm = [(r * 16 + c, r * 16 + (c ^ masks[r & 1])) for r in range(8) for c in range(16)]
        pairs.append((part, lax.ppermute(part, ("row", "col"), perm)))
    return pairs


def column_of(entries, col, core):
    diff = (entries >> 8) ^ col
    bits = {}
    for axis, (near, far) in enumerate(((4, 12), (1, 3))):
        d = ((diff >> 2) & 3) if axis == 0 else (diff & 3)
        bits[far] = d >> 1
        bits[near] = (d & 1) ^ (d >> 1)
    half = (entries >> 7) & 1
    turn = (2 * half + core) & 3
    place = jnp.zeros_like(entries)
    for s in range(4):
        m = jnp.zeros_like(entries)
        for k in range(4):
            m = m + (bits[CYCLE[(k + s) % 4]] << k)
        place = jnp.where(turn == s, m, place)
    return half * 2048 + place * 128 + (entries & 127)


def table_kernel(place_ref, nbr_ref, token_ref, out_ref, wide):
    nbr = nbr_ref[...]
    places = column_of(jnp.maximum(nbr, 0), place_ref[0], place_ref[1])
    live = nbr >= 0
    high = jnp.where(live, places & 4032, -64).astype(F32).astype(BF)
    low = jnp.where(live, places & 63, 0).astype(F32).astype(BF)
    slot = lax.broadcasted_iota(I32, (32, 2048), 0) & 15
    spread = jnp.where(slot == (lax.broadcasted_iota(I32, (32, 2048), 1) >> 7), 1.0, 0.0).astype(BF)
    wide[...] = dot(jnp.concatenate([high, low], axis=1), spread).astype(I32).astype(I16)
    base = lax.broadcasted_iota(I32, (256, 128), 1)
    one, zero = jnp.ones((), BF), jnp.zeros((), BF)

    @pl.loop(0, 32)
    def _(t):
        lanes = (base + t * 128).astype(I16)
        acc = jnp.zeros((256, 128), BF)
        for slot in range(16):
            acc = acc + jnp.where(wide[:, pl.ds(slot * 128, 128)] == lanes, one, zero)
        out_ref[:, pl.ds(pl.multiple_of(t * 128, 128), 128)] = acc


def cite_table(place, nbr, token):
    return pl.pallas_call(
        table_kernel,
        out_shape=shape((256, 4096), BF),
        in_specs=[IN_SMEM, IN_VMEM, ANYWHERE],
        out_specs=IN_VMEM,
        scratch_shapes=[pltpu.VMEM((256, 2048), I16)],
        compiler_params=params(16),
        cost_estimate=pl.CostEstimate(flops=1, bytes_accessed=1, transcendentals=0),
        name="cite_table",
    )(place, nbr, token)


def back_table_kernel(place_ref, a_ref, b_ref, token_ref, out_ref):
    own = (lax.broadcasted_iota(I32, (256, 128), 0) + place_ref[0] * 256).astype(I16)
    one, zero = jnp.ones((), BF), jnp.zeros((), BF)
    for m in range(16):
        lists = (a_ref if m < 8 else b_ref)[m % 8].astype(I16)
        for h in range(2):
            acc = jnp.zeros((256, 128), BF)
            for slot in range(16):
                acc = acc + jnp.where(lists[slot : slot + 1, 128 * h : 128 * h + 128] == own, one, zero)
            place = m if h == 0 else (m >> 2) | ((m & 3) << 2)
            out_ref[:, pl.ds(h * 2048 + place * 128, 128)] = acc


def cited_by_table(place, a, b, token):
    return pl.pallas_call(
        back_table_kernel,
        out_shape=shape((256, 4096), BF),
        in_specs=[IN_SMEM, IN_VMEM, IN_VMEM, ANYWHERE],
        out_specs=IN_VMEM,
        compiler_params=params(16),
        cost_estimate=pl.CostEstimate(flops=1, bytes_accessed=1, transcendentals=0),
        name="cited_by_table",
    )(place, a, b, token)


def edge_lists(write_src, write_dst):
    none = jnp.full_like(write_src, -1)
    pick = jnp.concatenate([write_src, jnp.where(write_dst >= 0, write_dst + 256, -1)], axis=1)
    into_paper = jnp.concatenate([write_dst, none], axis=1)
    into_author = jnp.concatenate([none, write_src], axis=1)
    return pick.reshape(1, -1), into_paper.reshape(1, -1), into_author.reshape(1, -1)


def exchange(rows):
    sent = rows.reshape(128, 8, rows.shape[-1])
    got = lax.all_to_all(sent, ("row", "col"), split_axis=0, concat_axis=0, tiled=True)
    return got.reshape(1024, rows.shape[-1])


def pick_kernel(pick_ref, a_ref, b_ref, token_ref, out_ref):
    hit = jnp.where(lax.broadcasted_iota(I32, (512, 1024), 0) == pick_ref[...], 1.0, 0.0).astype(BF)
    rows = dot(hit[:256], a_ref[...], ((0,), (0,))) + dot(hit[256:], b_ref[...], ((0,), (0,)))
    out_ref[...] = rows.astype(BF)


def pick_rows(pick, authors, papers, token):
    return pl.pallas_call(
        pick_kernel,
        out_shape=shape((1024, 768), BF),
        in_specs=[IN_VMEM] * 3 + [ANYWHERE],
        out_specs=IN_VMEM,
        compiler_params=params(16),
        cost_estimate=pl.CostEstimate(flops=1, bytes_accessed=1, transcendentals=0),
        name="pick_rows",
    )(pick, authors, papers, token)


def other_core(value):
    return lax.ppermute(value, "row", [(i, i ^ 1) for i in range(8)])


def over_y(parts):
    got = [parts[0]]
    for d in range(1, 4):
        perm = [(2 * y + c, 2 * ((y + d) % 4) + c) for y in range(4) for c in range(2)]
        got.append(lax.ppermute(parts[d], "row", perm))
    return got


def silu_and_slope(value):
    sigma = 1.0 / (1.0 + jnp.exp(-value))
    return (value * sigma).astype(BF), sigma * (1.0 + value * (1.0 - sigma))


def author_kernel(
    arrived_ref, into_paper_ref, into_author_ref, *refs
):
    sources, outs, held, sems = refs[:7], refs[8:17], refs[17:24], refs[24]
    out_ref, authored_ref, written_ref, dpre_ref, dz_ref, dx_ref, pre_ref, adder_ref, cnt_ref = outs
    x_author_ref, x_paper_ref, grad_ref, w_sa, w_wn, w_sp, w_wr = held
    copies = [pltpu.make_async_copy(a, b, sems.at[i]) for i, (a, b) in enumerate(zip(sources, held))]
    for i in (0, 3, 4, 2, 1, 5, 6):
        copies[i].start()
    ids = lax.broadcasted_iota(I32, (256, 1024), 0)
    means = []
    for i, ref in enumerate((into_paper_ref, into_author_ref)):
        hit = jnp.where(ref[...] == ids, 1.0, 0.0)
        cnt = jnp.maximum(jnp.sum(hit, axis=1, keepdims=True), 1.0)
        cnt_ref[pl.ds(256 * i, 256), :] = jnp.broadcast_to(cnt, (256, 128))
        hit = hit.astype(BF)
        adder_ref[pl.ds(256 * i, 256), :] = hit
        means.append((dot(hit, arrived_ref[...]) / cnt).astype(BF))
    written, authored = means
    for i in (0, 3, 4):
        copies[i].wait()
    x_author = x_author_ref[...]
    pre = dot(x_author, w_sa[...]) + dot(authored, w_wn[...])
    out, slope = silu_and_slope(pre)
    out_ref[...] = out
    copies[2].wait()
    copies[1].wait()
    x_paper = x_paper_ref[...]
    dpre = (grad_ref[...].astype(F32) * slope).astype(BF)
    authored_ref[...] = authored
    written_ref[...] = written
    dpre_ref[...] = dpre
    dz_ref[...] = (dot(dpre, w_wn[...], ((1,), (1,))) / cnt_ref[pl.ds(256, 256), pl.ds(0, 1)]).astype(BF)
    dx_ref[...] = dot(dpre, w_sa[...], ((1,), (1,)))
    copies[5].wait()
    copies[6].wait()
    pre_ref[...] = dot(x_paper, w_sp[...]) + dot(written, w_wr[...])


def author_step(arrived, into_paper, into_author, x_author, x_paper, grad, w_sa, w_wn, w_sp, w_wr, token):
    weight = pltpu.VMEM((768, 1024), BF)
    return pl.pallas_call(
        author_kernel,
        out_shape=[
            shape((256, 1024), BF), shape((256, 768), BF), shape((256, 768), BF), shape((256, 1024), BF),
            shape((256, 768), BF), shape((256, 768), F32),
            shape((256, 1024), F32), shape((512, 1024), BF), shape((512, 128), F32),
        ],
        in_specs=[IN_VMEM] * 3 + [IN_HBM] * 7 + [ANYWHERE],
        out_specs=[IN_VMEM] * 9,
        scratch_shapes=[pltpu.VMEM((256, 768), BF)] * 2 + [pltpu.VMEM((256, 1024), BF)] + [weight] * 4
        + [pltpu.SemaphoreType.DMA((7,))],
        compiler_params=params(58),
        cost_estimate=pl.CostEstimate(flops=1, bytes_accessed=1, transcendentals=0),
        name="author_step",
    )(arrived, into_paper, into_author, x_author, x_paper, grad, w_sa, w_wn, w_sp, w_wr, token)


def first_kernel(table_ref, b0, b1, out_ref):
    acc = dot(table_ref[:, pl.ds(0, 1024)], b0[...]) + dot(table_ref[:, pl.ds(2048, 1024)], b1[...])
    out_ref[...] = acc


def first_half(table, blocks):
    return pl.pallas_call(
        first_kernel,
        out_shape=shape((256, 768), F32),
        in_specs=[IN_VMEM] * 3,
        out_specs=IN_VMEM,
        compiler_params=params(24),
        cost_estimate=pl.CostEstimate(flops=1, bytes_accessed=1, transcendentals=0),
        name="first_half",
    )(table, *blocks)


def last_kernel(table_ref, b0, b1, first_ref, own_ref, out_ref):
    acc = dot(table_ref[:, pl.ds(1024, 1024)], b0[...]) + dot(table_ref[:, pl.ds(3072, 1024)], b1[...])
    out_ref[...] = (acc + (first_ref[...] + own_ref[...])).astype(BF)


def last_half(table, blocks, first, own):
    return pl.pallas_call(
        last_kernel,
        out_shape=shape((256, 768), BF),
        in_specs=[IN_VMEM] * 5,
        out_specs=IN_VMEM,
        compiler_params=params(24),
        cost_estimate=pl.CostEstimate(flops=1, bytes_accessed=1, transcendentals=0),
        name="last_half",
    )(table, *blocks, first, own)


def edge_add_kernel(adder_ref, back_ref, author_ref, paper_ref, out_ref, sum_ref):
    back = back_ref[...]
    sum_ref[...] = paper_ref[...] + dot(adder_ref[pl.ds(0, 256), :], back)
    out_ref[...] = (author_ref[...] + dot(adder_ref[pl.ds(256, 256), :], back)).astype(BF)


def edge_add(adder, back, author, paper):
    return pl.pallas_call(
        edge_add_kernel,
        out_shape=[shape((256, 768), BF), shape((256, 768), F32)],
        in_specs=[IN_VMEM] * 4,
        out_specs=[IN_VMEM] * 2,
        compiler_params=params(16),
        cost_estimate=pl.CostEstimate(flops=1, bytes_accessed=1, transcendentals=0),
        name="edge_add",
    )(adder, back, author, paper)


def paper_kernel(
    table_ref, b0, b1, first_ref, nbr_ref, pre_ref, grad_hbm, w_hbm, token_a, token_b, token_c,
    out_ref, pack_ref, dz_ref, grad_ref, w_ref, sems,
):
    copies = [pltpu.make_async_copy(w_hbm, w_ref, sems.at[0]), pltpu.make_async_copy(grad_hbm, grad_ref, sems.at[1])]
    for copy in copies:
        copy.start()
    total = first_ref[...]
    for h, block in enumerate((b0, b1)):
        total = total + dot(table_ref[:, pl.ds(h * 2048 + 1024, 1024)], block[...])
    cnt = jnp.sum(jnp.where(nbr_ref[...] >= 0, 1.0, 0.0), axis=1, keepdims=True)
    cnt = jnp.maximum(cnt, 1.0)
    cited = (total / cnt).astype(BF)
    pack_ref[:, pl.ds(0, 768)] = cited
    copies[0].wait()
    out, slope = silu_and_slope(pre_ref[...] + dot(cited, w_ref[...]))
    out_ref[...] = out
    copies[1].wait()
    dpre = (grad_ref[...].astype(F32) * slope).astype(BF)
    pack_ref[:, pl.ds(768, 1024)] = dpre
    dz_ref[...] = (dot(dpre, w_ref[...], ((1,), (1,))) / cnt).astype(BF)


def paper_step(table, blocks, first, nbr, pre, grad, w_cite, *tokens):
    return pl.pallas_call(
        paper_kernel,
        out_shape=[shape((256, 1024), BF), shape((256, 1792), BF), shape((256, 768), BF)],
        in_specs=[IN_VMEM] * 6 + [IN_HBM] * 2 + [ANYWHERE] * 3,
        out_specs=[IN_VMEM] * 3,
        scratch_shapes=[pltpu.VMEM((256, 1024), BF), pltpu.VMEM((768, 1024), BF), pltpu.SemaphoreType.DMA((2,))],
        compiler_params=params(32),
        cost_estimate=pl.CostEstimate(flops=1, bytes_accessed=1, transcendentals=0),
        name="paper_step",
    )(table, *blocks, first, nbr, pre, grad, w_cite, *tokens)


def edge_back_kernel(pack_ref, cnt_ref, w_wr_hbm, w_sp_hbm, dz_ref, dx_ref, w_wr, w_sp, sems):
    copies = [pltpu.make_async_copy(w_wr_hbm, w_wr, sems.at[0]), pltpu.make_async_copy(w_sp_hbm, w_sp, sems.at[1])]
    for copy in copies:
        copy.start()
    dpre = pack_ref[:, pl.ds(768, 1024)]
    copies[0].wait()
    dz_ref[...] = (dot(dpre, w_wr[...], ((1,), (1,))) / cnt_ref[pl.ds(0, 256), pl.ds(0, 1)]).astype(BF)
    copies[1].wait()
    dx_ref[...] = dot(dpre, w_sp[...], ((1,), (1,)))


def edge_back(dpre, cnt, w_write, w_self):
    return pl.pallas_call(
        edge_back_kernel,
        out_shape=[shape((256, 768), BF), shape((256, 768), F32)],
        in_specs=[IN_VMEM, IN_VMEM, IN_HBM, IN_HBM],
        out_specs=[IN_VMEM] * 2,
        scratch_shapes=[pltpu.VMEM((768, 1024), BF)] * 2 + [pltpu.SemaphoreType.DMA((2,))],
        compiler_params=params(16),
        cost_estimate=pl.CostEstimate(flops=1, bytes_accessed=1, transcendentals=0),
        name="edge_back",
    )(dpre, cnt, w_write, w_self)


def weight_kernel(n, cuts, place_ref, *refs):
    outs, turned = refs[-4 * cuts - 1 : -1] if cuts else refs[-2:-1], refs[-1]
    core, y = place_ref[1], place_ref[2]
    dpre = jnp.concatenate([ref[:, pl.ds(ref.shape[1] - 1024, 1024)] for ref in refs[:2]], axis=0)
    wide = 1024 // max(cuts, 1)
    for i in range(n):
        for k in range(2):
            turned[i, :, pl.ds(256 * k, 256)] = refs[2 + 2 * i + k][:, pl.ds(0, 768)].T
        rows = []
        for d in range(4):
            ahead = ((y + d) & 3) if cuts else d
            start = pl.multiple_of((2 * ahead + core) * 96, 32)
            rows.append(turned[i, pl.ds(start, 96), :])
        product = dot(jnp.concatenate(rows, axis=0), dpre).astype(BF)
        if not cuts:
            for d in range(4):
                outs[0][d, i] = product[96 * d : 96 * d + 96]
        for j in range(cuts):
            for d in range(4):
                outs[4 * j + d][i] = product[96 * d : 96 * d + 96, wide * j : wide * j + wide]


def weight_parts(place, dpre, lefts, token, cuts):
    n = len(lefts)
    outs = pl.pallas_call(
        functools.partial(weight_kernel, n, cuts),
        out_shape=[shape((n, 96, 1024 // cuts), BF)] * (4 * cuts) if cuts else [shape((4, n, 96, 1024), BF)],
        in_specs=[IN_SMEM] + [IN_VMEM] * (2 + 2 * n) + [ANYWHERE],
        out_specs=[IN_VMEM] * max(4 * cuts, 1),
        scratch_shapes=[pltpu.VMEM((n, 768, 512), BF)],
        compiler_params=params(24),
        cost_estimate=pl.CostEstimate(flops=1, bytes_accessed=1, transcendentals=0),
        name="weight_parts",
    )(place, *dpre, *[v for pair in lefts for v in pair], token)
    return [outs[4 * j : 4 * j + 4] for j in range(cuts)] if cuts else outs


def y_sum_kernel(place_ref, *refs):
    left, right, authors, outs, stack = refs[:4], refs[4:8], refs[8], refs[9:13], refs[13]
    for group, first, rows, lane, wide in ((left, 0, 3, 0, 512), (right, 0, 3, 512, 512), (authors, 3, 2, 0, 1024)):
        for i in range(rows):
            part = (lambda y: group[y, i]) if first else (lambda y: group[y][i])
            total = part(0).astype(F32)
            for y in range(1, 4):
                total = total + part(y).astype(F32)
            stack[pl.ds(96 * (first + i), 96), pl.ds(lane, wide)] = total
    stack[pl.ds(480, 32), :] = jnp.zeros((32, 1024), F32)
    x = place_ref[0] >> 2
    for d in range(4):
        start = pl.multiple_of(((x + d) & 3) * 256, 256)
        outs[d][...] = stack[:, pl.ds(start, 256)].T.astype(BF)


def y_sum(place, left, right, author):
    return pl.pallas_call(
        y_sum_kernel,
        out_shape=[shape((256, 512), BF)] * 4,
        in_specs=[IN_SMEM] + [IN_VMEM] * 9,
        out_specs=[IN_VMEM] * 4,
        scratch_shapes=[pltpu.VMEM((512, 1024), F32)],
        compiler_params=params(20),
        cost_estimate=pl.CostEstimate(flops=1, bytes_accessed=1, transcendentals=0),
        name="y_sum",
    )(place, *left, *right, author)


def x_sum_kernel(place_ref, token_a, token_b, *refs):
    total = refs[0][...].astype(F32)
    for ref in refs[1:4]:
        total = total + ref[...].astype(F32)
    refs[8][...] = total
    z = place_ref[0] & 3
    for d in range(4):
        refs[4 + d][...] = refs[8][pl.ds(pl.multiple_of(((z + d) & 3) * 64, 64), 64), :]


def x_sum(place, got, *tokens):
    return pl.pallas_call(
        x_sum_kernel,
        out_shape=[shape((64, 512), F32)] * 4,
        in_specs=[IN_SMEM, ANYWHERE, ANYWHERE] + [IN_VMEM] * 4,
        out_specs=[IN_VMEM] * 4,
        scratch_shapes=[pltpu.VMEM((256, 512), F32)],
        compiler_params=params(8),
        cost_estimate=pl.CostEstimate(flops=1, bytes_accessed=1, transcendentals=0),
        name="x_sum",
    )(place, *tokens, *got)


def over_col(parts, step):
    got = [parts[0]]
    for d in range(1, 4):
        perm = []
        for c in range(16):
            x, z = c >> 2, c & 3
            perm.append((c, ((x + d) % 4) * 4 + z if step == 4 else x * 4 + (z + d) % 4))
        got.append(lax.ppermute(parts[d], "col", perm))
    return got


def last_sum_kernel(*refs):
    total = refs[0][...]
    for ref in refs[1:4]:
        total = total + ref[...]
    total = total * (32768.0 ** -0.5)
    for m in range(5):
        refs[-1][m] = total[:, 96 * m : 96 * m + 96]


def last_sum(got):
    return pl.pallas_call(
        last_sum_kernel,
        out_shape=shape((5, 64, 96), F32),
        in_specs=[IN_VMEM] * 4,
        out_specs=IN_VMEM,
        compiler_params=params(8),
        cost_estimate=pl.CostEstimate(flops=1, bytes_accessed=1, transcendentals=0),
        name="last_sum",
    )(*got)


def per_device(
    x_paper, x_author, cite_nbr, write_src, write_dst,
    w_self_paper, w_cite, w_write, w_self_author, w_written, grad_paper, grad_author,
):
    row = lax.axis_index("row")
    place = jnp.stack([lax.axis_index("col"), row & 1, row >> 1]).astype(I32)

    lists = [cite_nbr.T.reshape(1, 16, 256)]
    pairs = travel([x_paper[:128], x_paper[128:]], 0)
    lists = travel(lists, 0)

    pick, into_paper, into_author = edge_lists(write_src[0], write_dst[0])
    arrived = exchange(pick_rows(pick, x_author, x_paper, lists[0][1]))
    parts = join(pairs)
    pairs = travel(parts, 1)
    lists = travel(join(lists), 1)
    x_author_pair = (x_author, other_core(x_author))
    x_paper_pair = (x_paper, other_core(x_paper))

    parts = join(pairs, (lists[0][1],))
    table = cite_table(place, cite_nbr, parts[0])
    parts = join(travel(parts, 2), (table,))
    pairs = travel(parts, 3)
    lists = travel(join(lists), 2)
    cite_first = first_half(table, [pair[0] for pair in pairs])

    out_author, authored, written, dpre_author, dz_written, dx_author_own, pre_paper, adder, cnt = author_step(
        arrived, into_paper, into_author, x_author, x_paper, grad_author,
        w_self_author, w_written, w_self_paper, w_write, parts[0],
    )
    (parts_author,) = weight_parts(
        place, (dpre_author, other_core(dpre_author)),
        [x_author_pair, (authored, other_core(authored))], table, 0,
    )
    got_author = lax.all_to_all(
        parts_author, "row", split_axis=0, concat_axis=0, tiled=True,
        axis_index_groups=[[0, 2, 4, 6], [1, 3, 5, 7]],
    )
    written_pair = (written, other_core(written))

    out_paper, pack, dz_cite = paper_step(
        table, [pair[1] for pair in pairs], cite_first, cite_nbr, pre_paper, grad_paper, w_cite,
        parts_author, lists[0][1], authored,
    )
    back_pairs = travel([dz_cite[:128], dz_cite[128:]], 0)
    dz_write, dx_paper_own = edge_back(pack, cnt, w_write, w_self_paper)
    pack_other = other_core(pack)
    left, right = weight_parts(
        place, (pack, pack_other), [x_paper_pair, (pack, pack_other), written_pair], dz_write, 2,
    )
    lists = travel(join(lists), 3)[0]
    parts = join(back_pairs, (left[0], lists[1], got_author))
    pairs = travel(parts, 1)
    left = over_y(left)
    rows = pick_rows(pick, dz_written, dz_write, parts[0])
    back = exchange(rows)
    parts = join(pairs, left[1:])
    right = over_y(right)
    back_table = cited_by_table(place, lists[0], lists[1], parts[0])
    parts = join(travel(parts, 2), (back_table, *right[1:]))
    dx_author, dx_paper_own = edge_add(adder, back, dx_author_own, dx_paper_own)
    back_pairs = travel(parts, 3)
    back_first = first_half(back_table, [pair[0] for pair in back_pairs])

    got = over_col(y_sum(place, left, right, got_author), 4)
    got = over_col(x_sum(place, got, back_first, dx_author), 1)
    dx_paper = last_half(back_table, [pair[1] for pair in back_pairs], back_first, dx_paper_own)
    dweights = last_sum(got).transpose(0, 2, 1)
    return (out_paper, out_author, dx_paper, dx_author, dweights)


def solution(mesh):
    part = P(("row", "col"), None)
    part3 = P(("row", "col"), None, None)
    return jax.shard_map(
        per_device,
        mesh=mesh,
        in_specs=(part, part, part, part3, part3, P(), P(), P(), P(), P(), part, part),
        out_specs=(part, part, part, part, P(None, "row", "col")),
        check_vma=False,
    )
```

```python
import functools

import jax
import jax.numpy as jnp
from jax import lax
from jax.experimental import pallas as pl
from jax.experimental.pallas import tpu as pltpu
from jax.sharding import PartitionSpec as P

BF = jnp.bfloat16
F32 = jnp.float32
I32 = jnp.int32
MIB = 1024 * 1024
I16 = jnp.int16
CYCLE = (4, 1, 12, 3)
IN_VMEM = pl.BlockSpec(memory_space=pltpu.VMEM)
ANYWHERE = pl.BlockSpec(memory_space=pl.ANY)
IN_HBM = pl.BlockSpec(memory_space=pltpu.HBM)
IN_SMEM = pl.BlockSpec(memory_space=pltpu.SMEM)


def dot(a, b, dims=((1,), (0,))):
    return lax.dot_general(a, b, (dims, ((), ())), preferred_element_type=F32)


def shape(dims, kind):
    return jax.ShapeDtypeStruct(dims, kind)


def params(mib):
    return pltpu.CompilerParams(vmem_limit_bytes=mib * MIB)


def join_kernel(n, *refs):
    outs = refs[len(refs) - n :]
    for i in range(n):
        a, b, out = refs[2 * i], refs[2 * i + 1], outs[i]
        rows = a.shape[0]
        out[pl.ds(0, rows)] = a[...]
        out[pl.ds(rows, rows)] = b[...]


def join(pairs, tokens=()):
    n = len(pairs)
    flat = [v for pair in pairs for v in pair]
    outs = [shape((2 * a.shape[0],) + a.shape[1:], a.dtype) for a, _ in pairs]
    return pl.pallas_call(
        functools.partial(join_kernel, n),
        out_shape=outs,
        in_specs=[IN_VMEM] * (2 * n) + [ANYWHERE] * len(tokens),
        out_specs=[IN_VMEM] * n,
        compiler_params=params(16),
        name="join",
    )(*flat, *tokens)


def travel(parts, k):
    pairs = []
    for h, part in enumerate(parts):
        masks = [CYCLE[(k + 2 * (h & 1) + c) % 4] for c in range(2)]
        perm = [(r * 16 + c, r * 16 + (c ^ masks[r & 1])) for r in range(8) for c in range(16)]
        pairs.append((part, lax.ppermute(part, ("row", "col"), perm)))
    return pairs


def column_of(entries, col, core):
    diff = (entries >> 8) ^ col
    bits = {}
    for axis, (near, far) in enumerate(((4, 12), (1, 3))):
        d = ((diff >> 2) & 3) if axis == 0 else (diff & 3)
        bits[far] = d >> 1
        bits[near] = (d & 1) ^ (d >> 1)
    half = (entries >> 7) & 1
    turn = (2 * half + core) & 3
    place = jnp.zeros_like(entries)
    for s in range(4):
        m = jnp.zeros_like(entries)
        for k in range(4):
            m = m + (bits[CYCLE[(k + s) % 4]] << k)
        place = jnp.where(turn == s, m, place)
    return half * 2048 + place * 128 + (entries & 127)


def table_kernel(place_ref, nbr_ref, token_ref, out_ref, wide):
    nbr = nbr_ref[...]
    places = column_of(jnp.maximum(nbr, 0), place_ref[0], place_ref[1])
    live = nbr >= 0
    high = jnp.where(live, places & 4032, -64).astype(F32).astype(BF)
    low = jnp.where(live, places & 63, 0).astype(F32).astype(BF)
    slot = lax.broadcasted_iota(I32, (32, 2048), 0) & 15
    spread = jnp.where(slot == (lax.broadcasted_iota(I32, (32, 2048), 1) >> 7), 1.0, 0.0).astype(BF)
    wide[...] = dot(jnp.concatenate([high, low], axis=1), spread).astype(I32).astype(I16)
    base = lax.broadcasted_iota(I32, (256, 128), 1)
    one, zero = jnp.ones((), BF), jnp.zeros((), BF)

    @pl.loop(0, 32)
    def _(t):
        lanes = (base + t * 128).astype(I16)
        acc = jnp.zeros((256, 128), BF)
        for slot in range(16):
            acc = acc + jnp.where(wide[:, pl.ds(slot * 128, 128)] == lanes, one, zero)
        out_ref[:, pl.ds(pl.multiple_of(t * 128, 128), 128)] = acc


def cite_table(place, nbr, token):
    return pl.pallas_call(
        table_kernel,
        out_shape=shape((256, 4096), BF),
        in_specs=[IN_SMEM, IN_VMEM, ANYWHERE],
        out_specs=IN_VMEM,
        scratch_shapes=[pltpu.VMEM((256, 2048), I16)],
        compiler_params=params(16),
        cost_estimate=pl.CostEstimate(flops=1, bytes_accessed=1, transcendentals=0),
        name="cite_table",
    )(place, nbr, token)


def back_table_kernel(place_ref, a_ref, b_ref, token_ref, out_ref):
    own = (lax.broadcasted_iota(I32, (256, 128), 0) + place_ref[0] * 256).astype(I16)
    one, zero = jnp.ones((), BF), jnp.zeros((), BF)
    for m in range(16):
        lists = (a_ref if m < 8 else b_ref)[m % 8].astype(I16)
        for h in range(2):
            acc = jnp.zeros((256, 128), BF)
            for slot in range(16):
                acc = acc + jnp.where(lists[slot : slot + 1, 128 * h : 128 * h + 128] == own, one, zero)
            place = m if h == 0 else (m >> 2) | ((m & 3) << 2)
            out_ref[:, pl.ds(h * 2048 + place * 128, 128)] = acc


def cited_by_table(place, a, b, token):
    return pl.pallas_call(
        back_table_kernel,
        out_shape=shape((256, 4096), BF),
        in_specs=[IN_SMEM, IN_VMEM, IN_VMEM, ANYWHERE],
        out_specs=IN_VMEM,
        compiler_params=params(16),
        cost_estimate=pl.CostEstimate(flops=1, bytes_accessed=1, transcendentals=0),
        name="cited_by_table",
    )(place, a, b, token)


def edge_lists(write_src, write_dst):
    none = jnp.full_like(write_src, -1)
    pick = jnp.concatenate([write_src, jnp.where(write_dst >= 0, write_dst + 256, -1)], axis=1)
    into_paper = jnp.concatenate([write_dst, none], axis=1)
    into_author = jnp.concatenate([none, write_src], axis=1)
    return pick.reshape(1, -1), into_paper.reshape(1, -1), into_author.reshape(1, -1)


def exchange(rows):
    sent = rows.reshape(128, 8, rows.shape[-1])
    got = lax.all_to_all(sent, ("row", "col"), split_axis=0, concat_axis=0, tiled=True)
    return got.reshape(1024, rows.shape[-1])


def pick_kernel(pick_ref, a_ref, b_ref, token_ref, out_ref):
    hit = jnp.where(lax.broadcasted_iota(I32, (512, 1024), 0) == pick_ref[...], 1.0, 0.0).astype(BF)
    rows = dot(hit[:256], a_ref[...], ((0,), (0,))) + dot(hit[256:], b_ref[...], ((0,), (0,)))
    out_ref[...] = rows.astype(BF)


def pick_rows(pick, authors, papers, token):
    return pl.pallas_call(
        pick_kernel,
        out_shape=shape((1024, 768), BF),
        in_specs=[IN_VMEM] * 3 + [ANYWHERE],
        out_specs=IN_VMEM,
        compiler_params=params(16),
        cost_estimate=pl.CostEstimate(flops=1, bytes_accessed=1, transcendentals=0),
        name="pick_rows",
    )(pick, authors, papers, token)


def other_core(value):
    return lax.ppermute(value, "row", [(i, i ^ 1) for i in range(8)])


def over_y(parts):
    got = [parts[0]]
    for d in range(1, 4):
        perm = [(2 * y + c, 2 * ((y + d) % 4) + c) for y in range(4) for c in range(2)]
        got.append(lax.ppermute(parts[d], "row", perm))
    return got


def silu_and_slope(value):
    sigma = 1.0 / (1.0 + jnp.exp(-value))
    return (value * sigma).astype(BF), sigma * (1.0 + value * (1.0 - sigma))


def author_kernel(
    arrived_ref, into_paper_ref, into_author_ref, *refs
):
    sources, outs, held, sems = refs[:7], refs[8:17], refs[17:24], refs[24]
    out_ref, authored_ref, written_ref, dpre_ref, dz_ref, dx_ref, pre_ref, adder_ref, cnt_ref = outs
    x_author_ref, x_paper_ref, grad_ref, w_sa, w_wn, w_sp, w_wr = held
    copies = [pltpu.make_async_copy(a, b, sems.at[i]) for i, (a, b) in enumerate(zip(sources, held))]
    for i in (0, 3, 4, 2, 1, 5, 6):
        copies[i].start()
    ids = lax.broadcasted_iota(I32, (256, 1024), 0)
    means = []
    for i, ref in enumerate((into_paper_ref, into_author_ref)):
        hit = jnp.where(ref[...] == ids, 1.0, 0.0)
        cnt = jnp.maximum(jnp.sum(hit, axis=1, keepdims=True), 1.0)
        cnt_ref[pl.ds(256 * i, 256), :] = jnp.broadcast_to(cnt, (256, 128))
        hit = hit.astype(BF)
        adder_ref[pl.ds(256 * i, 256), :] = hit
        means.append((dot(hit, arrived_ref[...]) / cnt).astype(BF))
    written, authored = means
    for i in (0, 3, 4):
        copies[i].wait()
    x_author = x_author_ref[...]
    pre = dot(x_author, w_sa[...]) + dot(authored, w_wn[...])
    out, slope = silu_and_slope(pre)
    out_ref[...] = out
    copies[2].wait()
    copies[1].wait()
    x_paper = x_paper_ref[...]
    dpre = (grad_ref[...].astype(F32) * slope).astype(BF)
    authored_ref[...] = authored
    written_ref[...] = written
    dpre_ref[...] = dpre
    dz_ref[...] = (dot(dpre, w_wn[...], ((1,), (1,))) / cnt_ref[pl.ds(256, 256), pl.ds(0, 1)]).astype(BF)
    dx_ref[...] = dot(dpre, w_sa[...], ((1,), (1,)))
    copies[5].wait()
    copies[6].wait()
    pre_ref[...] = dot(x_paper, w_sp[...]) + dot(written, w_wr[...])


def author_step(arrived, into_paper, into_author, x_author, x_paper, grad, w_sa, w_wn, w_sp, w_wr, token):
    weight = pltpu.VMEM((768, 1024), BF)
    return pl.pallas_call(
        author_kernel,
        out_shape=[
            shape((256, 1024), BF), shape((256, 768), BF), shape((256, 768), BF), shape((256, 1024), BF),
            shape((256, 768), BF), shape((256, 768), F32),
            shape((256, 1024), F32), shape((512, 1024), BF), shape((512, 128), F32),
        ],
        in_specs=[IN_VMEM] * 3 + [IN_HBM] * 7 + [ANYWHERE],
        out_specs=[IN_VMEM] * 9,
        scratch_shapes=[pltpu.VMEM((256, 768), BF)] * 2 + [pltpu.VMEM((256, 1024), BF)] + [weight] * 4
        + [pltpu.SemaphoreType.DMA((7,))],
        compiler_params=params(58),
        cost_estimate=pl.CostEstimate(flops=1, bytes_accessed=1, transcendentals=0),
        name="author_step",
    )(arrived, into_paper, into_author, x_author, x_paper, grad, w_sa, w_wn, w_sp, w_wr, token)


def first_kernel(table_ref, b0, b1, out_ref):
    acc = dot(table_ref[:, pl.ds(0, 1024)], b0[...]) + dot(table_ref[:, pl.ds(2048, 1024)], b1[...])
    out_ref[...] = acc


def first_half(table, blocks):
    return pl.pallas_call(
        first_kernel,
        out_shape=shape((256, 768), F32),
        in_specs=[IN_VMEM] * 3,
        out_specs=IN_VMEM,
        compiler_params=params(24),
        cost_estimate=pl.CostEstimate(flops=1, bytes_accessed=1, transcendentals=0),
        name="first_half",
    )(table, *blocks)


def last_kernel(table_ref, b0, b1, first_ref, own_ref, out_ref):
    acc = dot(table_ref[:, pl.ds(1024, 1024)], b0[...]) + dot(table_ref[:, pl.ds(3072, 1024)], b1[...])
    out_ref[...] = (acc + (first_ref[...] + own_ref[...])).astype(BF)


def last_half(table, blocks, first, own):
    return pl.pallas_call(
        last_kernel,
        out_shape=shape((256, 768), BF),
        in_specs=[IN_VMEM] * 5,
        out_specs=IN_VMEM,
        compiler_params=params(24),
        cost_estimate=pl.CostEstimate(flops=1, bytes_accessed=1, transcendentals=0),
        name="last_half",
    )(table, *blocks, first, own)


def edge_add_kernel(adder_ref, back_ref, author_ref, paper_ref, out_ref, sum_ref):
    back = back_ref[...]
    sum_ref[...] = paper_ref[...] + dot(adder_ref[pl.ds(0, 256), :], back)
    out_ref[...] = (author_ref[...] + dot(adder_ref[pl.ds(256, 256), :], back)).astype(BF)


def edge_add(adder, back, author, paper):
    return pl.pallas_call(
        edge_add_kernel,
        out_shape=[shape((256, 768), BF), shape((256, 768), F32)],
        in_specs=[IN_VMEM] * 4,
        out_specs=[IN_VMEM] * 2,
        compiler_params=params(16),
        cost_estimate=pl.CostEstimate(flops=1, bytes_accessed=1, transcendentals=0),
        name="edge_add",
    )(adder, back, author, paper)


def paper_kernel(
    table_ref, b0, b1, first_ref, nbr_ref, pre_ref, grad_hbm, w_hbm, token_a, token_b, token_c,
    out_ref, pack_ref, dz_ref, grad_ref, w_ref, sems,
):
    copies = [pltpu.make_async_copy(w_hbm, w_ref, sems.at[0]), pltpu.make_async_copy(grad_hbm, grad_ref, sems.at[1])]
    for copy in copies:
        copy.start()
    total = first_ref[...]
    for h, block in enumerate((b0, b1)):
        total = total + dot(table_ref[:, pl.ds(h * 2048 + 1024, 1024)], block[...])
    cnt = jnp.sum(jnp.where(nbr_ref[...] >= 0, 1.0, 0.0), axis=1, keepdims=True)
    cnt = jnp.maximum(cnt, 1.0)
    cited = (total / cnt).astype(BF)
    pack_ref[:, pl.ds(0, 768)] = cited
    copies[0].wait()
    out, slope = silu_and_slope(pre_ref[...] + dot(cited, w_ref[...]))
    out_ref[...] = out
    copies[1].wait()
    dpre = (grad_ref[...].astype(F32) * slope).astype(BF)
    pack_ref[:, pl.ds(768, 1024)] = dpre
    dz_ref[...] = (dot(dpre, w_ref[...], ((1,), (1,))) / cnt).astype(BF)


def paper_step(table, blocks, first, nbr, pre, grad, w_cite, *tokens):
    return pl.pallas_call(
        paper_kernel,
        out_shape=[shape((256, 1024), BF), shape((256, 1792), BF), shape((256, 768), BF)],
        in_specs=[IN_VMEM] * 6 + [IN_HBM] * 2 + [ANYWHERE] * 3,
        out_specs=[IN_VMEM] * 3,
        scratch_shapes=[pltpu.VMEM((256, 1024), BF), pltpu.VMEM((768, 1024), BF), pltpu.SemaphoreType.DMA((2,))],
        compiler_params=params(32),
        cost_estimate=pl.CostEstimate(flops=1, bytes_accessed=1, transcendentals=0),
        name="paper_step",
    )(table, *blocks, first, nbr, pre, grad, w_cite, *tokens)


def edge_back_kernel(pack_ref, cnt_ref, w_wr_hbm, w_sp_hbm, dz_ref, dx_ref, w_wr, w_sp, sems):
    copies = [pltpu.make_async_copy(w_wr_hbm, w_wr, sems.at[0]), pltpu.make_async_copy(w_sp_hbm, w_sp, sems.at[1])]
    for copy in copies:
        copy.start()
    dpre = pack_ref[:, pl.ds(768, 1024)]
    copies[0].wait()
    dz_ref[...] = (dot(dpre, w_wr[...], ((1,), (1,))) / cnt_ref[pl.ds(0, 256), pl.ds(0, 1)]).astype(BF)
    copies[1].wait()
    dx_ref[...] = dot(dpre, w_sp[...], ((1,), (1,)))


def edge_back(dpre, cnt, w_write, w_self):
    return pl.pallas_call(
        edge_back_kernel,
        out_shape=[shape((256, 768), BF), shape((256, 768), F32)],
        in_specs=[IN_VMEM, IN_VMEM, IN_HBM, IN_HBM],
        out_specs=[IN_VMEM] * 2,
        scratch_shapes=[pltpu.VMEM((768, 1024), BF)] * 2 + [pltpu.SemaphoreType.DMA((2,))],
        compiler_params=params(16),
        cost_estimate=pl.CostEstimate(flops=1, bytes_accessed=1, transcendentals=0),
        name="edge_back",
    )(dpre, cnt, w_write, w_self)


def weight_kernel(n, cuts, place_ref, *refs):
    outs, turned = refs[-4 * cuts - 1 : -1] if cuts else refs[-2:-1], refs[-1]
    core, y = place_ref[1], place_ref[2]
    dpre = jnp.concatenate([ref[:, pl.ds(ref.shape[1] - 1024, 1024)] for ref in refs[:2]], axis=0)
    wide = 1024 // max(cuts, 1)
    for i in range(n):
        for k in range(2):
            turned[i, :, pl.ds(256 * k, 256)] = refs[2 + 2 * i + k][:, pl.ds(0, 768)].T
        rows = []
        for d in range(4):
            ahead = ((y + d) & 3) if cuts else d
            start = pl.multiple_of((2 * ahead + core) * 96, 32)
            rows.append(turned[i, pl.ds(start, 96), :])
        product = dot(jnp.concatenate(rows, axis=0), dpre).astype(BF)
        if not cuts:
            for d in range(4):
                outs[0][d, i] = product[96 * d : 96 * d + 96]
        for j in range(cuts):
            for d in range(4):
                outs[4 * j + d][i] = product[96 * d : 96 * d + 96, wide * j : wide * j + wide]


def weight_parts(place, dpre, lefts, token, cuts):
    n = len(lefts)
    outs = pl.pallas_call(
        functools.partial(weight_kernel, n, cuts),
        out_shape=[shape((n, 96, 1024 // cuts), BF)] * (4 * cuts) if cuts else [shape((4, n, 96, 1024), BF)],
        in_specs=[IN_SMEM] + [IN_VMEM] * (2 + 2 * n) + [ANYWHERE],
        out_specs=[IN_VMEM] * max(4 * cuts, 1),
        scratch_shapes=[pltpu.VMEM((n, 768, 512), BF)],
        compiler_params=params(24),
        cost_estimate=pl.CostEstimate(flops=1, bytes_accessed=1, transcendentals=0),
        name="weight_parts",
    )(place, *dpre, *[v for pair in lefts for v in pair], token)
    return [outs[4 * j : 4 * j + 4] for j in range(cuts)] if cuts else outs


def y_sum_kernel(place_ref, *refs):
    left, right, authors, outs, stack, turned = refs[:4], refs[4:8], refs[8], refs[9:13], refs[13], refs[14]
    for group, first, rows, lane, wide in ((left, 0, 3, 0, 512), (right, 0, 3, 512, 512), (authors, 3, 2, 0, 1024)):
        for i in range(rows):
            part = (lambda y: group[y, i]) if first else (lambda y: group[y][i])
            total = part(0).astype(F32)
            for y in range(1, 4):
                total = total + part(y).astype(F32)
            stack[pl.ds(96 * (first + i), 96), pl.ds(lane, wide)] = total
    stack[pl.ds(480, 32), :] = jnp.zeros((32, 1024), F32)
    turned[...] = stack[...].T.astype(BF)
    core, x, z = place_ref[1], place_ref[0] >> 2, place_ref[0] & 3
    for d in range(4):
        for j in range(4):
            start = jnp.where(core == 0, ((x + d) & 3) * 256 + j * 64, j * 256 + ((z + d) & 3) * 64)
            outs[d][pl.ds(64 * j, 64), :] = turned[pl.ds(pl.multiple_of(start, 64), 64), :]


def y_sum(place, left, right, author):
    return pl.pallas_call(
        y_sum_kernel,
        out_shape=[shape((256, 512), BF)] * 4,
        in_specs=[IN_SMEM] + [IN_VMEM] * 9,
        out_specs=[IN_VMEM] * 4,
        scratch_shapes=[pltpu.VMEM((512, 1024), F32), pltpu.VMEM((1024, 512), BF)],
        compiler_params=params(20),
        cost_estimate=pl.CostEstimate(flops=1, bytes_accessed=1, transcendentals=0),
        name="y_sum",
    )(place, *left, *right, author)


def x_sum_kernel(place_ref, token_a, token_b, *refs):
    total = refs[0][...].astype(F32)
    for ref in refs[1:4]:
        total = total + ref[...].astype(F32)
    refs[8][...] = total
    at = jnp.where(place_ref[1] == 0, place_ref[0] & 3, place_ref[0] >> 2)
    for d in range(4):
        refs[4 + d][...] = refs[8][pl.ds(pl.multiple_of(((at + d) & 3) * 64, 64), 64), :]


def x_sum(place, got, *tokens):
    return pl.pallas_call(
        x_sum_kernel,
        out_shape=[shape((64, 512), F32)] * 4,
        in_specs=[IN_SMEM, ANYWHERE, ANYWHERE] + [IN_VMEM] * 4,
        out_specs=[IN_VMEM] * 4,
        scratch_shapes=[pltpu.VMEM((256, 512), F32)],
        compiler_params=params(8),
        cost_estimate=pl.CostEstimate(flops=1, bytes_accessed=1, transcendentals=0),
        name="x_sum",
    )(place, *tokens, *got)


def over_col(parts, stage):
    got = [parts[0]]
    for d in range(1, 4):
        perm = []
        for r in range(8):
            for c in range(16):
                x, z = c >> 2, c & 3
                to = ((x + d) % 4) * 4 + z if (r & 1) == stage else x * 4 + (z + d) % 4
                perm.append((r * 16 + c, r * 16 + to))
        got.append(lax.ppermute(parts[d], ("row", "col"), perm))
    return got


def last_sum_kernel(*refs):
    total = refs[0][...]
    for ref in refs[1:4]:
        total = total + ref[...]
    total = total * (32768.0 ** -0.5)
    for m in range(5):
        refs[-1][m] = total[:, 96 * m : 96 * m + 96]


def last_sum(got):
    return pl.pallas_call(
        last_sum_kernel,
        out_shape=shape((5, 64, 96), F32),
        in_specs=[IN_VMEM] * 4,
        out_specs=IN_VMEM,
        compiler_params=params(8),
        cost_estimate=pl.CostEstimate(flops=1, bytes_accessed=1, transcendentals=0),
        name="last_sum",
    )(*got)


def per_device(
    x_paper, x_author, cite_nbr, write_src, write_dst,
    w_self_paper, w_cite, w_write, w_self_author, w_written, grad_paper, grad_author,
):
    row = lax.axis_index("row")
    place = jnp.stack([lax.axis_index("col"), row & 1, row >> 1]).astype(I32)

    lists = [cite_nbr.T.reshape(1, 16, 256)]
    pairs = travel([x_paper[:128], x_paper[128:]], 0)
    lists = travel(lists, 0)

    pick, into_paper, into_author = edge_lists(write_src[0], write_dst[0])
    arrived = exchange(pick_rows(pick, x_author, x_paper, lists[0][1]))
    parts = join(pairs)
    pairs = travel(parts, 1)
    lists = travel(join(lists), 1)
    x_author_pair = (x_author, other_core(x_author))
    x_paper_pair = (x_paper, other_core(x_paper))

    parts = join(pairs, (lists[0][1],))
    table = cite_table(place, cite_nbr, parts[0])
    parts = join(travel(parts, 2), (table,))
    pairs = travel(parts, 3)
    lists = travel(join(lists), 2)
    cite_first = first_half(table, [pair[0] for pair in pairs])

    out_author, authored, written, dpre_author, dz_written, dx_author_own, pre_paper, adder, cnt = author_step(
        arrived, into_paper, into_author, x_author, x_paper, grad_author,
        w_self_author, w_written, w_self_paper, w_write, parts[0],
    )
    (parts_author,) = weight_parts(
        place, (dpre_author, other_core(dpre_author)),
        [x_author_pair, (authored, other_core(authored))], table, 0,
    )
    got_author = lax.all_to_all(
        parts_author, "row", split_axis=0, concat_axis=0, tiled=True,
        axis_index_groups=[[0, 2, 4, 6], [1, 3, 5, 7]],
    )
    written_pair = (written, other_core(written))

    out_paper, pack, dz_cite = paper_step(
        table, [pair[1] for pair in pairs], cite_first, cite_nbr, pre_paper, grad_paper, w_cite,
        parts_author, lists[0][1], authored,
    )
    back_pairs = travel([dz_cite[:128], dz_cite[128:]], 0)
    dz_write, dx_paper_own = edge_back(pack, cnt, w_write, w_self_paper)
    pack_other = other_core(pack)
    left, right = weight_parts(
        place, (pack, pack_other), [x_paper_pair, (pack, pack_other), written_pair], dz_write, 2,
    )
    lists = travel(join(lists), 3)[0]
    parts = join(back_pairs, (left[0], lists[1], got_author))
    pairs = travel(parts, 1)
    left = over_y(left)
    rows = pick_rows(pick, dz_written, dz_write, parts[0])
    back = exchange(rows)
    parts = join(pairs, left[1:])
    right = over_y(right)
    back_table = cited_by_table(place, lists[0], lists[1], parts[0])
    parts = join(travel(parts, 2), (back_table, *right[1:]))
    dx_author, dx_paper_own = edge_add(adder, back, dx_author_own, dx_paper_own)
    back_pairs = travel(parts, 3)
    back_first = first_half(back_table, [pair[0] for pair in back_pairs])

    got = over_col(y_sum(place, left, right, got_author), 0)
    got = over_col(x_sum(place, got, back_first, dx_author), 1)
    dx_paper = last_half(back_table, [pair[1] for pair in back_pairs], back_first, dx_paper_own)
    dweights = last_sum(got).transpose(0, 2, 1)
    return (out_paper, out_author, dx_paper, dx_author, dweights)


def solution(mesh):
    part = P(("row", "col"), None)
    part3 = P(("row", "col"), None, None)
    return jax.shard_map(
        per_device,
        mesh=mesh,
        in_specs=(part, part, part, part3, part3, P(), P(), P(), P(), P(), part, part),
        out_specs=(part, part, part, part, P(None, "row", "col")),
        check_vma=False,
    )
```

```python
import functools

import jax
import jax.numpy as jnp
from jax import lax
from jax.experimental import pallas as pl
from jax.experimental.pallas import tpu as pltpu
from jax.sharding import PartitionSpec as P

BF = jnp.bfloat16
F32 = jnp.float32
I32 = jnp.int32
MIB = 1024 * 1024
I16 = jnp.int16
CYCLE = (4, 1, 12, 3)
IN_VMEM = pl.BlockSpec(memory_space=pltpu.VMEM)
ANYWHERE = pl.BlockSpec(memory_space=pl.ANY)
IN_HBM = pl.BlockSpec(memory_space=pltpu.HBM)
IN_SMEM = pl.BlockSpec(memory_space=pltpu.SMEM)


def dot(a, b, dims=((1,), (0,))):
    return lax.dot_general(a, b, (dims, ((), ())), preferred_element_type=F32)


def shape(dims, kind):
    return jax.ShapeDtypeStruct(dims, kind)


def params(mib):
    return pltpu.CompilerParams(vmem_limit_bytes=mib * MIB)


def join_kernel(n, *refs):
    outs = refs[len(refs) - n :]
    for i in range(n):
        a, b, out = refs[2 * i], refs[2 * i + 1], outs[i]
        rows = a.shape[0]
        out[pl.ds(0, rows)] = a[...]
        out[pl.ds(rows, rows)] = b[...]


def join(pairs, tokens=()):
    n = len(pairs)
    flat = [v for pair in pairs for v in pair]
    outs = [shape((2 * a.shape[0],) + a.shape[1:], a.dtype) for a, _ in pairs]
    return pl.pallas_call(
        functools.partial(join_kernel, n),
        out_shape=outs,
        in_specs=[IN_VMEM] * (2 * n) + [ANYWHERE] * len(tokens),
        out_specs=[IN_VMEM] * n,
        compiler_params=params(16),
        name="join",
    )(*flat, *tokens)


def travel(parts, k):
    pairs = []
    for h, part in enumerate(parts):
        masks = [CYCLE[(k + 2 * (h & 1) + c) % 4] for c in range(2)]
        perm = [(r * 16 + c, r * 16 + (c ^ masks[r & 1])) for r in range(8) for c in range(16)]
        pairs.append((part, lax.ppermute(part, ("row", "col"), perm)))
    return pairs


def column_of(entries, col, core):
    diff = (entries >> 8) ^ col
    bits = {}
    for axis, (near, far) in enumerate(((4, 12), (1, 3))):
        d = ((diff >> 2) & 3) if axis == 0 else (diff & 3)
        bits[far] = d >> 1
        bits[near] = (d & 1) ^ (d >> 1)
    half = (entries >> 7) & 1
    turn = (2 * half + core) & 3
    place = jnp.zeros_like(entries)
    for s in range(4):
        m = jnp.zeros_like(entries)
        for k in range(4):
            m = m + (bits[CYCLE[(k + s) % 4]] << k)
        place = jnp.where(turn == s, m, place)
    return half * 2048 + place * 128 + (entries & 127)


def table_kernel(place_ref, nbr_ref, token_ref, out_ref, wide):
    nbr = nbr_ref[...]
    places = column_of(jnp.maximum(nbr, 0), place_ref[0], place_ref[1])
    live = nbr >= 0
    high = jnp.where(live, places & 4032, -64).astype(F32).astype(BF)
    low = jnp.where(live, places & 63, 0).astype(F32).astype(BF)
    slot = lax.broadcasted_iota(I32, (32, 2048), 0) & 15
    spread = jnp.where(slot == (lax.broadcasted_iota(I32, (32, 2048), 1) >> 7), 1.0, 0.0).astype(BF)
    wide[...] = dot(jnp.concatenate([high, low], axis=1), spread).astype(I32).astype(I16)
    base = lax.broadcasted_iota(I32, (256, 128), 1)
    one, zero = jnp.ones((), BF), jnp.zeros((), BF)

    @pl.loop(0, 32)
    def _(t):
        lanes = (base + t * 128).astype(I16)
        acc = jnp.zeros((256, 128), BF)
        for slot in range(16):
            acc = acc + jnp.where(wide[:, pl.ds(slot * 128, 128)] == lanes, one, zero)
        out_ref[:, pl.ds(pl.multiple_of(t * 128, 128), 128)] = acc


def cite_table(place, nbr, token):
    return pl.pallas_call(
        table_kernel,
        out_shape=shape((256, 4096), BF),
        in_specs=[IN_SMEM, IN_VMEM, ANYWHERE],
        out_specs=IN_VMEM,
        scratch_shapes=[pltpu.VMEM((256, 2048), I16)],
        compiler_params=params(16),
        cost_estimate=pl.CostEstimate(flops=1, bytes_accessed=1, transcendentals=0),
        name="cite_table",
    )(place, nbr, token)


def back_table_kernel(place_ref, a_ref, b_ref, token_ref, out_ref):
    own = (lax.broadcasted_iota(I32, (256, 128), 0) + place_ref[0] * 256).astype(I16)
    one, zero = jnp.ones((), BF), jnp.zeros((), BF)
    for m in range(16):
        lists = (a_ref if m < 8 else b_ref)[m % 8].astype(I16)
        for h in range(2):
            acc = jnp.zeros((256, 128), BF)
            for slot in range(16):
                acc = acc + jnp.where(lists[slot : slot + 1, 128 * h : 128 * h + 128] == own, one, zero)
            place = m if h == 0 else (m >> 2) | ((m & 3) << 2)
            out_ref[:, pl.ds(h * 2048 + place * 128, 128)] = acc


def cited_by_table(place, a, b, token):
    return pl.pallas_call(
        back_table_kernel,
        out_shape=shape((256, 4096), BF),
        in_specs=[IN_SMEM, IN_VMEM, IN_VMEM, ANYWHERE],
        out_specs=IN_VMEM,
        compiler_params=params(16),
        cost_estimate=pl.CostEstimate(flops=1, bytes_accessed=1, transcendentals=0),
        name="cited_by_table",
    )(place, a, b, token)


def edge_lists(write_src, write_dst):
    none = jnp.full_like(write_src, -1)
    pick = jnp.concatenate([write_src, jnp.where(write_dst >= 0, write_dst + 256, -1)], axis=1)
    into_paper = jnp.concatenate([write_dst, none], axis=1)
    into_author = jnp.concatenate([none, write_src], axis=1)
    return pick.reshape(1, -1), into_paper.reshape(1, -1), into_author.reshape(1, -1)


def exchange(rows):
    sent = rows.reshape(128, 8, rows.shape[-1])
    got = lax.all_to_all(sent, ("row", "col"), split_axis=0, concat_axis=0, tiled=True)
    return got.reshape(1024, rows.shape[-1])


def pick_kernel(pick_ref, a_ref, b_ref, token_ref, out_ref):
    hit = jnp.where(lax.broadcasted_iota(I32, (512, 1024), 0) == pick_ref[...], 1.0, 0.0).astype(BF)
    rows = dot(hit[:256], a_ref[...], ((0,), (0,))) + dot(hit[256:], b_ref[...], ((0,), (0,)))
    out_ref[...] = rows.astype(BF)


def pick_rows(pick, authors, papers, token):
    return pl.pallas_call(
        pick_kernel,
        out_shape=shape((1024, 768), BF),
        in_specs=[IN_VMEM] * 3 + [ANYWHERE],
        out_specs=IN_VMEM,
        compiler_params=params(16),
        cost_estimate=pl.CostEstimate(flops=1, bytes_accessed=1, transcendentals=0),
        name="pick_rows",
    )(pick, authors, papers, token)


def other_core(value):
    return lax.ppermute(value, "row", [(i, i ^ 1) for i in range(8)])


def over_y(parts):
    got = [parts[0]]
    for d in range(1, 4):
        perm = [(2 * y + c, 2 * ((y + d) % 4) + c) for y in range(4) for c in range(2)]
        got.append(lax.ppermute(parts[d], "row", perm))
    return got


def silu_and_slope(value):
    sigma = 1.0 / (1.0 + jnp.exp(-value))
    return (value * sigma).astype(BF), sigma * (1.0 + value * (1.0 - sigma))


def author_kernel(
    arrived_ref, into_paper_ref, into_author_ref, *refs
):
    sources, outs, held, sems = refs[:7], refs[8:17], refs[17:24], refs[24]
    out_ref, authored_ref, written_ref, dpre_ref, dz_ref, dx_ref, pre_ref, adder_ref, cnt_ref = outs
    x_author_ref, x_paper_ref, grad_ref, w_sa, w_wn, w_sp, w_wr = held
    copies = [pltpu.make_async_copy(a, b, sems.at[i]) for i, (a, b) in enumerate(zip(sources, held))]
    for i in (0, 3, 4, 2, 1, 5, 6):
        copies[i].start()
    ids = lax.broadcasted_iota(I32, (256, 1024), 0)
    means = []
    for i, ref in enumerate((into_paper_ref, into_author_ref)):
        hit = jnp.where(ref[...] == ids, 1.0, 0.0)
        cnt = jnp.maximum(jnp.sum(hit, axis=1, keepdims=True), 1.0)
        cnt_ref[pl.ds(256 * i, 256), :] = jnp.broadcast_to(cnt, (256, 128))
        hit = hit.astype(BF)
        adder_ref[pl.ds(256 * i, 256), :] = hit
        means.append((dot(hit, arrived_ref[...]) / cnt).astype(BF))
    written, authored = means
    for i in (0, 3, 4):
        copies[i].wait()
    x_author = x_author_ref[...]
    pre = dot(x_author, w_sa[...]) + dot(authored, w_wn[...])
    out, slope = silu_and_slope(pre)
    out_ref[...] = out
    copies[2].wait()
    copies[1].wait()
    x_paper = x_paper_ref[...]
    dpre = (grad_ref[...].astype(F32) * slope).astype(BF)
    authored_ref[...] = authored
    written_ref[...] = written
    dpre_ref[...] = dpre
    dz_ref[...] = (dot(dpre, w_wn[...], ((1,), (1,))) / cnt_ref[pl.ds(256, 256), pl.ds(0, 1)]).astype(BF)
    dx_ref[...] = dot(dpre, w_sa[...], ((1,), (1,)))
    copies[5].wait()
    copies[6].wait()
    pre_ref[...] = dot(x_paper, w_sp[...]) + dot(written, w_wr[...])


def author_step(arrived, into_paper, into_author, x_author, x_paper, grad, w_sa, w_wn, w_sp, w_wr, token):
    weight = pltpu.VMEM((768, 1024), BF)
    return pl.pallas_call(
        author_kernel,
        out_shape=[
            shape((256, 1024), BF), shape((256, 768), BF), shape((256, 768), BF), shape((256, 1024), BF),
            shape((256, 768), BF), shape((256, 768), F32),
            shape((256, 1024), F32), shape((512, 1024), BF), shape((512, 128), F32),
        ],
        in_specs=[IN_VMEM] * 3 + [IN_HBM] * 7 + [ANYWHERE],
        out_specs=[IN_VMEM] * 9,
        scratch_shapes=[pltpu.VMEM((256, 768), BF)] * 2 + [pltpu.VMEM((256, 1024), BF)] + [weight] * 4
        + [pltpu.SemaphoreType.DMA((7,))],
        compiler_params=params(58),
        cost_estimate=pl.CostEstimate(flops=1, bytes_accessed=1, transcendentals=0),
        name="author_step",
    )(arrived, into_paper, into_author, x_author, x_paper, grad, w_sa, w_wn, w_sp, w_wr, token)


def first_kernel(table_ref, b0, b1, out_ref):
    acc = dot(table_ref[:, pl.ds(0, 1024)], b0[...]) + dot(table_ref[:, pl.ds(2048, 1024)], b1[...])
    out_ref[...] = acc


def first_half(table, blocks):
    return pl.pallas_call(
        first_kernel,
        out_shape=shape((256, 768), F32),
        in_specs=[IN_VMEM] * 3,
        out_specs=IN_VMEM,
        compiler_params=params(24),
        cost_estimate=pl.CostEstimate(flops=1, bytes_accessed=1, transcendentals=0),
        name="first_half",
    )(table, *blocks)


def last_kernel(table_ref, b0, b1, first_ref, own_ref, out_ref):
    acc = dot(table_ref[:, pl.ds(1024, 1024)], b0[...]) + dot(table_ref[:, pl.ds(3072, 1024)], b1[...])
    out_ref[...] = (acc + (first_ref[...] + own_ref[...])).astype(BF)


def last_half(table, blocks, first, own):
    return pl.pallas_call(
        last_kernel,
        out_shape=shape((256, 768), BF),
        in_specs=[IN_VMEM] * 5,
        out_specs=IN_VMEM,
        compiler_params=params(24),
        cost_estimate=pl.CostEstimate(flops=1, bytes_accessed=1, transcendentals=0),
        name="last_half",
    )(table, *blocks, first, own)


def edge_add_kernel(adder_ref, back_ref, author_ref, paper_ref, out_ref, sum_ref):
    back = back_ref[...]
    sum_ref[...] = paper_ref[...] + dot(adder_ref[pl.ds(0, 256), :], back)
    out_ref[...] = (author_ref[...] + dot(adder_ref[pl.ds(256, 256), :], back)).astype(BF)


def edge_add(adder, back, author, paper):
    return pl.pallas_call(
        edge_add_kernel,
        out_shape=[shape((256, 768), BF), shape((256, 768), F32)],
        in_specs=[IN_VMEM] * 4,
        out_specs=[IN_VMEM] * 2,
        compiler_params=params(16),
        cost_estimate=pl.CostEstimate(flops=1, bytes_accessed=1, transcendentals=0),
        name="edge_add",
    )(adder, back, author, paper)


def paper_kernel(
    table_ref, b0, b1, first_ref, nbr_ref, pre_ref, grad_hbm, w_hbm, token_a, token_b, token_c,
    out_ref, pack_ref, dz_ref, grad_ref, w_ref, sems,
):
    copies = [pltpu.make_async_copy(w_hbm, w_ref, sems.at[0]), pltpu.make_async_copy(grad_hbm, grad_ref, sems.at[1])]
    for copy in copies:
        copy.start()
    total = first_ref[...]
    for h, block in enumerate((b0, b1)):
        total = total + dot(table_ref[:, pl.ds(h * 2048 + 1024, 1024)], block[...])
    cnt = jnp.sum(jnp.where(nbr_ref[...] >= 0, 1.0, 0.0), axis=1, keepdims=True)
    cnt = jnp.maximum(cnt, 1.0)
    cited = (total / cnt).astype(BF)
    pack_ref[:, pl.ds(0, 768)] = cited
    copies[0].wait()
    out, slope = silu_and_slope(pre_ref[...] + dot(cited, w_ref[...]))
    out_ref[...] = out
    copies[1].wait()
    dpre = (grad_ref[...].astype(F32) * slope).astype(BF)
    pack_ref[:, pl.ds(768, 1024)] = dpre
    dz_ref[...] = (dot(dpre, w_ref[...], ((1,), (1,))) / cnt).astype(BF)


def paper_step(table, blocks, first, nbr, pre, grad, w_cite, *tokens):
    return pl.pallas_call(
        paper_kernel,
        out_shape=[shape((256, 1024), BF), shape((256, 1792), BF), shape((256, 768), BF)],
        in_specs=[IN_VMEM] * 6 + [IN_HBM] * 2 + [ANYWHERE] * 3,
        out_specs=[IN_VMEM] * 3,
        scratch_shapes=[pltpu.VMEM((256, 1024), BF), pltpu.VMEM((768, 1024), BF), pltpu.SemaphoreType.DMA((2,))],
        compiler_params=params(32),
        cost_estimate=pl.CostEstimate(flops=1, bytes_accessed=1, transcendentals=0),
        name="paper_step",
    )(table, *blocks, first, nbr, pre, grad, w_cite, *tokens)


def edge_back_kernel(pack_ref, cnt_ref, w_wr_hbm, w_sp_hbm, dz_ref, dx_ref, w_wr, w_sp, sems):
    copies = [pltpu.make_async_copy(w_wr_hbm, w_wr, sems.at[0]), pltpu.make_async_copy(w_sp_hbm, w_sp, sems.at[1])]
    for copy in copies:
        copy.start()
    dpre = pack_ref[:, pl.ds(768, 1024)]
    copies[0].wait()
    dz_ref[...] = (dot(dpre, w_wr[...], ((1,), (1,))) / cnt_ref[pl.ds(0, 256), pl.ds(0, 1)]).astype(BF)
    copies[1].wait()
    dx_ref[...] = dot(dpre, w_sp[...], ((1,), (1,)))


def edge_back(dpre, cnt, w_write, w_self):
    return pl.pallas_call(
        edge_back_kernel,
        out_shape=[shape((256, 768), BF), shape((256, 768), F32)],
        in_specs=[IN_VMEM, IN_VMEM, IN_HBM, IN_HBM],
        out_specs=[IN_VMEM] * 2,
        scratch_shapes=[pltpu.VMEM((768, 1024), BF)] * 2 + [pltpu.SemaphoreType.DMA((2,))],
        compiler_params=params(16),
        cost_estimate=pl.CostEstimate(flops=1, bytes_accessed=1, transcendentals=0),
        name="edge_back",
    )(dpre, cnt, w_write, w_self)


def weight_kernel(n, cuts, place_ref, *refs):
    outs, turned = refs[-4 * cuts - 1 : -1] if cuts else refs[-2:-1], refs[-1]
    core, y = place_ref[1], place_ref[2]
    dpre = jnp.concatenate([ref[:, pl.ds(ref.shape[1] - 1024, 1024)] for ref in refs[:2]], axis=0)
    wide = 1024 // max(cuts, 1)
    for i in range(n):
        for k in range(2):
            turned[i, :, pl.ds(256 * k, 256)] = refs[2 + 2 * i + k][:, pl.ds(0, 768)].T
        rows = []
        for d in range(4):
            ahead = ((y + d) & 3) if cuts else d
            start = pl.multiple_of((2 * ahead + core) * 96, 32)
            rows.append(turned[i, pl.ds(start, 96), :])
        product = dot(jnp.concatenate(rows, axis=0), dpre).astype(BF)
        if not cuts:
            for d in range(4):
                outs[0][d, i] = product[96 * d : 96 * d + 96]
        for j in range(cuts):
            for d in range(4):
                outs[4 * j + d][i] = product[96 * d : 96 * d + 96, wide * j : wide * j + wide]


def weight_parts(place, dpre, lefts, token, cuts):
    n = len(lefts)
    outs = pl.pallas_call(
        functools.partial(weight_kernel, n, cuts),
        out_shape=[shape((n, 96, 1024 // cuts), BF)] * (4 * cuts) if cuts else [shape((4, n, 96, 1024), BF)],
        in_specs=[IN_SMEM] + [IN_VMEM] * (2 + 2 * n) + [ANYWHERE],
        out_specs=[IN_VMEM] * max(4 * cuts, 1),
        scratch_shapes=[pltpu.VMEM((n, 768, 512), BF)],
        compiler_params=params(24),
        cost_estimate=pl.CostEstimate(flops=1, bytes_accessed=1, transcendentals=0),
        name="weight_parts",
    )(place, *dpre, *[v for pair in lefts for v in pair], token)
    return [outs[4 * j : 4 * j + 4] for j in range(cuts)] if cuts else outs


def y_sum_kernel(place_ref, *refs):
    left, right, authors, outs, stack, turned = refs[:4], refs[4:8], refs[8], refs[9:13], refs[13], refs[14]
    for group, first, rows, lane, wide in ((left, 0, 3, 0, 512), (right, 0, 3, 512, 512), (authors, 3, 2, 0, 1024)):
        for i in range(rows):
            part = (lambda y: group[y, i]) if first else (lambda y: group[y][i])
            total = part(0).astype(F32)
            for y in range(1, 4):
                total = total + part(y).astype(F32)
            stack[pl.ds(96 * (first + i), 96), pl.ds(lane, wide)] = total
    stack[pl.ds(480, 32), :] = jnp.zeros((32, 1024), F32)
    turned[...] = stack[...].T.astype(BF)
    core, x, z = place_ref[1], place_ref[0] >> 2, place_ref[0] & 3
    for d in range(4):
        for j in range(4):
            start = jnp.where(core == 0, ((x + d) & 3) * 256 + j * 64, j * 256 + ((z + d) & 3) * 64)
            outs[d][pl.ds(64 * j, 64), :] = turned[pl.ds(pl.multiple_of(start, 64), 64), :]


def y_sum(place, left, right, author):
    return pl.pallas_call(
        y_sum_kernel,
        out_shape=[shape((256, 512), BF)] * 4,
        in_specs=[IN_SMEM] + [IN_VMEM] * 9,
        out_specs=[IN_VMEM] * 4,
        scratch_shapes=[pltpu.VMEM((512, 1024), F32), pltpu.VMEM((1024, 512), BF)],
        compiler_params=params(20),
        cost_estimate=pl.CostEstimate(flops=1, bytes_accessed=1, transcendentals=0),
        name="y_sum",
    )(place, *left, *right, author)


def x_sum_kernel(place_ref, token_a, token_b, *refs):
    total = refs[0][...].astype(F32)
    for ref in refs[1:4]:
        total = total + ref[...].astype(F32)
    refs[8][...] = total
    at = jnp.where(place_ref[1] == 0, place_ref[0] & 3, place_ref[0] >> 2)
    for d in range(4):
        refs[4 + d][...] = refs[8][pl.ds(pl.multiple_of(((at + d) & 3) * 64, 64), 64), :]


def x_sum(place, got, *tokens):
    return pl.pallas_call(
        x_sum_kernel,
        out_shape=[shape((64, 512), F32)] * 4,
        in_specs=[IN_SMEM, ANYWHERE, ANYWHERE] + [IN_VMEM] * 4,
        out_specs=[IN_VMEM] * 4,
        scratch_shapes=[pltpu.VMEM((256, 512), F32)],
        compiler_params=params(8),
        cost_estimate=pl.CostEstimate(flops=1, bytes_accessed=1, transcendentals=0),
        name="x_sum",
    )(place, *tokens, *got)


def over_col(parts, stage):
    got = [parts[0]]
    for d in range(1, 4):
        perm = []
        for r in range(8):
            for c in range(16):
                x, z = c >> 2, c & 3
                to = ((x + d) % 4) * 4 + z if (r & 1) == stage else x * 4 + (z + d) % 4
                perm.append((r * 16 + c, r * 16 + to))
        got.append(lax.ppermute(parts[d], ("row", "col"), perm))
    return got


def last_sum_kernel(token_ref, *refs):
    total = refs[0][...]
    for ref in refs[1:4]:
        total = total + ref[...]
    total = total * (32768.0 ** -0.5)
    for m in range(5):
        refs[-1][m] = total[:, 96 * m : 96 * m + 96]


def last_sum(got, token):
    return pl.pallas_call(
        last_sum_kernel,
        out_shape=shape((5, 64, 96), F32),
        in_specs=[ANYWHERE] + [IN_VMEM] * 4,
        out_specs=IN_VMEM,
        compiler_params=params(8),
        cost_estimate=pl.CostEstimate(flops=1, bytes_accessed=1, transcendentals=0),
        name="last_sum",
    )(token, *got)


def per_device(
    x_paper, x_author, cite_nbr, write_src, write_dst,
    w_self_paper, w_cite, w_write, w_self_author, w_written, grad_paper, grad_author,
):
    row = lax.axis_index("row")
    place = jnp.stack([lax.axis_index("col"), row & 1, row >> 1]).astype(I32)

    lists = [cite_nbr.T.reshape(1, 16, 256)]
    pairs = travel([x_paper[:128], x_paper[128:]], 0)
    lists = travel(lists, 0)

    pick, into_paper, into_author = edge_lists(write_src[0], write_dst[0])
    arrived = exchange(pick_rows(pick, x_author, x_paper, lists[0][1]))
    parts = join(pairs)
    pairs = travel(parts, 1)
    lists = travel(join(lists), 1)
    x_author_pair = (x_author, other_core(x_author))
    x_paper_pair = (x_paper, other_core(x_paper))

    parts = join(pairs, (lists[0][1],))
    table = cite_table(place, cite_nbr, parts[0])
    parts = join(travel(parts, 2), (table,))
    pairs = travel(parts, 3)
    lists = travel(join(lists), 2)
    cite_first = first_half(table, [pair[0] for pair in pairs])

    out_author, authored, written, dpre_author, dz_written, dx_author_own, pre_paper, adder, cnt = author_step(
        arrived, into_paper, into_author, x_author, x_paper, grad_author,
        w_self_author, w_written, w_self_paper, w_write, parts[0],
    )
    (parts_author,) = weight_parts(
        place, (dpre_author, other_core(dpre_author)),
        [x_author_pair, (authored, other_core(authored))], table, 0,
    )
    got_author = lax.all_to_all(
        parts_author, "row", split_axis=0, concat_axis=0, tiled=True,
        axis_index_groups=[[0, 2, 4, 6], [1, 3, 5, 7]],
    )
    written_pair = (written, other_core(written))

    out_paper, pack, dz_cite = paper_step(
        table, [pair[1] for pair in pairs], cite_first, cite_nbr, pre_paper, grad_paper, w_cite,
        parts_author, lists[0][1], authored,
    )
    back_pairs = travel([dz_cite[:128], dz_cite[128:]], 0)
    dz_write, dx_paper_own = edge_back(pack, cnt, w_write, w_self_paper)
    pack_other = other_core(pack)
    left, right = weight_parts(
        place, (pack, pack_other), [x_paper_pair, (pack, pack_other), written_pair], dz_write, 2,
    )
    lists = travel(join(lists), 3)[0]
    parts = join(back_pairs, (left[0], lists[1], got_author))
    pairs = travel(parts, 1)
    left = over_y(left)
    rows = pick_rows(pick, dz_written, dz_write, parts[0])
    back = exchange(rows)
    back_table = cited_by_table(place, lists[0], lists[1], parts[0])
    parts = join(pairs, (back_table, *left[1:]))
    right = over_y(right)
    parts = join(travel(parts, 2), (back_table, *right[1:]))
    dx_author, dx_paper_own = edge_add(adder, back, dx_author_own, dx_paper_own)
    back_pairs = travel(parts, 3)
    back_first = first_half(back_table, [pair[0] for pair in back_pairs])

    got = over_col(y_sum(place, left, right, got_author), 0)
    got = over_col(x_sum(place, got, back_first, dx_author), 1)
    dx_paper = last_half(back_table, [pair[1] for pair in back_pairs], back_first, dx_paper_own)
    dweights = last_sum(got, dx_paper).transpose(0, 2, 1)
    return (out_paper, out_author, dx_paper, dx_author, dweights)


def solution(mesh):
    part = P(("row", "col"), None)
    part3 = P(("row", "col"), None, None)
    return jax.shard_map(
        per_device,
        mesh=mesh,
        in_specs=(part, part, part, part3, part3, P(), P(), P(), P(), P(), part, part),
        out_specs=(part, part, part, part, P(None, "row", "col")),
        check_vma=False,
    )
```

```python
import functools

import jax
import jax.numpy as jnp
from jax import lax
from jax.experimental import pallas as pl
from jax.experimental.pallas import tpu as pltpu
from jax.sharding import PartitionSpec as P

BF = jnp.bfloat16
F32 = jnp.float32
I32 = jnp.int32
MIB = 1024 * 1024
I16 = jnp.int16
CYCLE = (4, 1, 12, 3)
IN_VMEM = pl.BlockSpec(memory_space=pltpu.VMEM)
ANYWHERE = pl.BlockSpec(memory_space=pl.ANY)
IN_HBM = pl.BlockSpec(memory_space=pltpu.HBM)
IN_SMEM = pl.BlockSpec(memory_space=pltpu.SMEM)


def dot(a, b, dims=((1,), (0,))):
    return lax.dot_general(a, b, (dims, ((), ())), preferred_element_type=F32)


def shape(dims, kind):
    return jax.ShapeDtypeStruct(dims, kind)


def params(mib):
    return pltpu.CompilerParams(vmem_limit_bytes=mib * MIB)


def join_kernel(n, *refs):
    outs = refs[len(refs) - n :]
    for i in range(n):
        a, b, out = refs[2 * i], refs[2 * i + 1], outs[i]
        rows = a.shape[0]
        out[pl.ds(0, rows)] = a[...]
        out[pl.ds(rows, rows)] = b[...]


def join(pairs, tokens=()):
    n = len(pairs)
    flat = [v for pair in pairs for v in pair]
    outs = [shape((2 * a.shape[0],) + a.shape[1:], a.dtype) for a, _ in pairs]
    return pl.pallas_call(
        functools.partial(join_kernel, n),
        out_shape=outs,
        in_specs=[IN_VMEM] * (2 * n) + [ANYWHERE] * len(tokens),
        out_specs=[IN_VMEM] * n,
        compiler_params=params(16),
        name="join",
    )(*flat, *tokens)


def travel(parts, k):
    pairs = []
    for h, part in enumerate(parts):
        masks = [CYCLE[(k + 2 * (h & 1) + c) % 4] for c in range(2)]
        perm = [(r * 16 + c, r * 16 + (c ^ masks[r & 1])) for r in range(8) for c in range(16)]
        pairs.append((part, lax.ppermute(part, ("row", "col"), perm)))
    return pairs


def column_of(entries, col, core):
    diff = (entries >> 8) ^ col
    bits = {}
    for axis, (near, far) in enumerate(((4, 12), (1, 3))):
        d = ((diff >> 2) & 3) if axis == 0 else (diff & 3)
        bits[far] = d >> 1
        bits[near] = (d & 1) ^ (d >> 1)
    half = (entries >> 7) & 1
    turn = (2 * half + core) & 3
    place = jnp.zeros_like(entries)
    for s in range(4):
        m = jnp.zeros_like(entries)
        for k in range(4):
            m = m + (bits[CYCLE[(k + s) % 4]] << k)
        place = jnp.where(turn == s, m, place)
    return half * 2048 + place * 128 + (entries & 127)


def table_kernel(place_ref, nbr_ref, token_ref, out_ref, wide):
    nbr = nbr_ref[...]
    places = column_of(jnp.maximum(nbr, 0), place_ref[0], place_ref[1])
    live = nbr >= 0
    high = jnp.where(live, places & 4032, -64).astype(F32).astype(BF)
    low = jnp.where(live, places & 63, 0).astype(F32).astype(BF)
    slot = lax.broadcasted_iota(I32, (32, 2048), 0) & 15
    spread = jnp.where(slot == (lax.broadcasted_iota(I32, (32, 2048), 1) >> 7), 1.0, 0.0).astype(BF)
    wide[...] = dot(jnp.concatenate([high, low], axis=1), spread).astype(I32).astype(I16)
    base = lax.broadcasted_iota(I32, (256, 128), 1)
    one, zero = jnp.ones((), BF), jnp.zeros((), BF)

    @pl.loop(0, 32)
    def _(t):
        lanes = (base + t * 128).astype(I16)
        acc = jnp.zeros((256, 128), BF)
        for slot in range(16):
            acc = acc + jnp.where(wide[:, pl.ds(slot * 128, 128)] == lanes, one, zero)
        out_ref[:, pl.ds(pl.multiple_of(t * 128, 128), 128)] = acc


def cite_table(place, nbr, token):
    return pl.pallas_call(
        table_kernel,
        out_shape=shape((256, 4096), BF),
        in_specs=[IN_SMEM, IN_VMEM, ANYWHERE],
        out_specs=IN_VMEM,
        scratch_shapes=[pltpu.VMEM((256, 2048), I16)],
        compiler_params=params(16),
        cost_estimate=pl.CostEstimate(flops=1, bytes_accessed=1, transcendentals=0),
        name="cite_table",
    )(place, nbr, token)


def back_table_kernel(place_ref, a_ref, b_ref, token_ref, out_ref):
    own = (lax.broadcasted_iota(I32, (256, 128), 0) + place_ref[0] * 256).astype(I16)
    one, zero = jnp.ones((), BF), jnp.zeros((), BF)
    for m in range(16):
        lists = (a_ref if m < 8 else b_ref)[m % 8].astype(I16)
        for h in range(2):
            acc = jnp.zeros((256, 128), BF)
            for slot in range(16):
                acc = acc + jnp.where(lists[slot : slot + 1, 128 * h : 128 * h + 128] == own, one, zero)
            place = m if h == 0 else (m >> 2) | ((m & 3) << 2)
            out_ref[:, pl.ds(h * 2048 + place * 128, 128)] = acc


def cited_by_table(place, a, b, token):
    return pl.pallas_call(
        back_table_kernel,
        out_shape=shape((256, 4096), BF),
        in_specs=[IN_SMEM, IN_VMEM, IN_VMEM, ANYWHERE],
        out_specs=IN_VMEM,
        compiler_params=params(16),
        cost_estimate=pl.CostEstimate(flops=1, bytes_accessed=1, transcendentals=0),
        name="cited_by_table",
    )(place, a, b, token)


def edge_lists(write_src, write_dst):
    none = jnp.full_like(write_src, -1)
    pick = jnp.concatenate([write_src, jnp.where(write_dst >= 0, write_dst + 256, -1)], axis=1)
    into_paper = jnp.concatenate([write_dst, none], axis=1)
    into_author = jnp.concatenate([none, write_src], axis=1)
    return pick.reshape(1, -1), into_paper.reshape(1, -1), into_author.reshape(1, -1)


def exchange(rows):
    sent = rows.reshape(128, 8, rows.shape[-1])
    got = lax.all_to_all(sent, ("row", "col"), split_axis=0, concat_axis=0, tiled=True)
    return got.reshape(1024, rows.shape[-1])


def pick_kernel(pick_ref, a_ref, b_ref, token_ref, out_ref):
    hit = jnp.where(lax.broadcasted_iota(I32, (512, 1024), 0) == pick_ref[...], 1.0, 0.0).astype(BF)
    rows = dot(hit[:256], a_ref[...], ((0,), (0,))) + dot(hit[256:], b_ref[...], ((0,), (0,)))
    out_ref[...] = rows.astype(BF)


def pick_rows(pick, authors, papers, token):
    return pl.pallas_call(
        pick_kernel,
        out_shape=shape((1024, 768), BF),
        in_specs=[IN_VMEM] * 3 + [ANYWHERE],
        out_specs=IN_VMEM,
        compiler_params=params(16),
        cost_estimate=pl.CostEstimate(flops=1, bytes_accessed=1, transcendentals=0),
        name="pick_rows",
    )(pick, authors, papers, token)


def other_core(value):
    return lax.ppermute(value, "row", [(i, i ^ 1) for i in range(8)])


def over_y(parts):
    got = [parts[0]]
    for d in range(1, 4):
        perm = [(2 * y + c, 2 * ((y + d) % 4) + c) for y in range(4) for c in range(2)]
        got.append(lax.ppermute(parts[d], "row", perm))
    return got


def silu_and_slope(value):
    sigma = 1.0 / (1.0 + jnp.exp(-value))
    return (value * sigma).astype(BF), sigma * (1.0 + value * (1.0 - sigma))


def author_kernel(
    arrived_ref, into_paper_ref, into_author_ref, *refs
):
    sources, outs, held, sems = refs[:7], refs[8:17], refs[17:24], refs[24]
    out_ref, authored_ref, written_ref, dpre_ref, dz_ref, dx_ref, pre_ref, adder_ref, cnt_ref = outs
    x_author_ref, x_paper_ref, grad_ref, w_sa, w_wn, w_sp, w_wr = held
    copies = [pltpu.make_async_copy(a, b, sems.at[i]) for i, (a, b) in enumerate(zip(sources, held))]
    for i in (0, 3, 4, 2, 1, 5, 6):
        copies[i].start()
    ids = lax.broadcasted_iota(I32, (256, 1024), 0)
    means = []
    for i, ref in enumerate((into_paper_ref, into_author_ref)):
        hit = jnp.where(ref[...] == ids, 1.0, 0.0)
        cnt = jnp.maximum(jnp.sum(hit, axis=1, keepdims=True), 1.0)
        cnt_ref[pl.ds(256 * i, 256), :] = jnp.broadcast_to(cnt, (256, 128))
        hit = hit.astype(BF)
        adder_ref[pl.ds(256 * i, 256), :] = hit
        means.append((dot(hit, arrived_ref[...]) / cnt).astype(BF))
    written, authored = means
    for i in (0, 3, 4):
        copies[i].wait()
    x_author = x_author_ref[...]
    pre = dot(x_author, w_sa[...]) + dot(authored, w_wn[...])
    out, slope = silu_and_slope(pre)
    out_ref[...] = out
    copies[2].wait()
    copies[1].wait()
    x_paper = x_paper_ref[...]
    dpre = (grad_ref[...].astype(F32) * slope).astype(BF)
    authored_ref[...] = authored
    written_ref[...] = written
    dpre_ref[...] = dpre
    dz_ref[...] = (dot(dpre, w_wn[...], ((1,), (1,))) / cnt_ref[pl.ds(256, 256), pl.ds(0, 1)]).astype(BF)
    dx_ref[...] = dot(dpre, w_sa[...], ((1,), (1,)))
    copies[5].wait()
    copies[6].wait()
    pre_ref[...] = dot(x_paper, w_sp[...]) + dot(written, w_wr[...])


def author_step(arrived, into_paper, into_author, x_author, x_paper, grad, w_sa, w_wn, w_sp, w_wr, token):
    weight = pltpu.VMEM((768, 1024), BF)
    return pl.pallas_call(
        author_kernel,
        out_shape=[
            shape((256, 1024), BF), shape((256, 768), BF), shape((256, 768), BF), shape((256, 1024), BF),
            shape((256, 768), BF), shape((256, 768), F32),
            shape((256, 1024), F32), shape((512, 1024), BF), shape((512, 128), F32),
        ],
        in_specs=[IN_VMEM] * 3 + [IN_HBM] * 7 + [ANYWHERE],
        out_specs=[IN_VMEM] * 9,
        scratch_shapes=[pltpu.VMEM((256, 768), BF)] * 2 + [pltpu.VMEM((256, 1024), BF)] + [weight] * 4
        + [pltpu.SemaphoreType.DMA((7,))],
        compiler_params=params(58),
        cost_estimate=pl.CostEstimate(flops=1, bytes_accessed=1, transcendentals=0),
        name="author_step",
    )(arrived, into_paper, into_author, x_author, x_paper, grad, w_sa, w_wn, w_sp, w_wr, token)


def first_kernel(table_ref, b0, b1, out_ref):
    acc = dot(table_ref[:, pl.ds(0, 1024)], b0[...]) + dot(table_ref[:, pl.ds(2048, 1024)], b1[...])
    out_ref[...] = acc


def first_half(table, blocks):
    return pl.pallas_call(
        first_kernel,
        out_shape=shape((256, 768), F32),
        in_specs=[IN_VMEM] * 3,
        out_specs=IN_VMEM,
        compiler_params=params(24),
        cost_estimate=pl.CostEstimate(flops=1, bytes_accessed=1, transcendentals=0),
        name="first_half",
    )(table, *blocks)


def last_kernel(table_ref, b0, b1, first_ref, own_ref, out_ref):
    acc = dot(table_ref[:, pl.ds(1024, 1024)], b0[...]) + dot(table_ref[:, pl.ds(3072, 1024)], b1[...])
    out_ref[...] = (acc + (first_ref[...] + own_ref[...])).astype(BF)


def last_half(table, blocks, first, own):
    return pl.pallas_call(
        last_kernel,
        out_shape=shape((256, 768), BF),
        in_specs=[IN_VMEM] * 5,
        out_specs=IN_VMEM,
        compiler_params=params(24),
        cost_estimate=pl.CostEstimate(flops=1, bytes_accessed=1, transcendentals=0),
        name="last_half",
    )(table, *blocks, first, own)


def edge_add_kernel(adder_ref, back_ref, author_ref, paper_ref, out_ref, sum_ref):
    back = back_ref[...]
    sum_ref[...] = paper_ref[...] + dot(adder_ref[pl.ds(0, 256), :], back)
    out_ref[...] = (author_ref[...] + dot(adder_ref[pl.ds(256, 256), :], back)).astype(BF)


def edge_add(adder, back, author, paper):
    return pl.pallas_call(
        edge_add_kernel,
        out_shape=[shape((256, 768), BF), shape((256, 768), F32)],
        in_specs=[IN_VMEM] * 4,
        out_specs=[IN_VMEM] * 2,
        compiler_params=params(16),
        cost_estimate=pl.CostEstimate(flops=1, bytes_accessed=1, transcendentals=0),
        name="edge_add",
    )(adder, back, author, paper)


def paper_kernel(
    table_ref, b0, b1, first_ref, nbr_ref, pre_ref, grad_hbm, w_hbm, token_a, token_b, token_c,
    out_ref, pack_ref, dz_ref, grad_ref, w_ref, sems,
):
    copies = [pltpu.make_async_copy(w_hbm, w_ref, sems.at[0]), pltpu.make_async_copy(grad_hbm, grad_ref, sems.at[1])]
    for copy in copies:
        copy.start()
    total = first_ref[...]
    for h, block in enumerate((b0, b1)):
        total = total + dot(table_ref[:, pl.ds(h * 2048 + 1024, 1024)], block[...])
    cnt = jnp.sum(jnp.where(nbr_ref[...] >= 0, 1.0, 0.0), axis=1, keepdims=True)
    cnt = jnp.maximum(cnt, 1.0)
    cited = (total / cnt).astype(BF)
    pack_ref[:, pl.ds(0, 768)] = cited
    copies[0].wait()
    out, slope = silu_and_slope(pre_ref[...] + dot(cited, w_ref[...]))
    out_ref[...] = out
    copies[1].wait()
    dpre = (grad_ref[...].astype(F32) * slope).astype(BF)
    pack_ref[:, pl.ds(768, 1024)] = dpre
    dz_ref[...] = (dot(dpre, w_ref[...], ((1,), (1,))) / cnt).astype(BF)


def paper_step(table, blocks, first, nbr, pre, grad, w_cite, *tokens):
    return pl.pallas_call(
        paper_kernel,
        out_shape=[shape((256, 1024), BF), shape((256, 1792), BF), shape((256, 768), BF)],
        in_specs=[IN_VMEM] * 6 + [IN_HBM] * 2 + [ANYWHERE] * 3,
        out_specs=[IN_VMEM] * 3,
        scratch_shapes=[pltpu.VMEM((256, 1024), BF), pltpu.VMEM((768, 1024), BF), pltpu.SemaphoreType.DMA((2,))],
        compiler_params=params(32),
        cost_estimate=pl.CostEstimate(flops=1, bytes_accessed=1, transcendentals=0),
        name="paper_step",
    )(table, *blocks, first, nbr, pre, grad, w_cite, *tokens)


def edge_back_kernel(pack_ref, cnt_ref, w_wr_hbm, w_sp_hbm, dz_ref, dx_ref, w_wr, w_sp, sems):
    copies = [pltpu.make_async_copy(w_wr_hbm, w_wr, sems.at[0]), pltpu.make_async_copy(w_sp_hbm, w_sp, sems.at[1])]
    for copy in copies:
        copy.start()
    dpre = pack_ref[:, pl.ds(768, 1024)]
    copies[0].wait()
    dz_ref[...] = (dot(dpre, w_wr[...], ((1,), (1,))) / cnt_ref[pl.ds(0, 256), pl.ds(0, 1)]).astype(BF)
    copies[1].wait()
    dx_ref[...] = dot(dpre, w_sp[...], ((1,), (1,)))


def edge_back(dpre, cnt, w_write, w_self):
    return pl.pallas_call(
        edge_back_kernel,
        out_shape=[shape((256, 768), BF), shape((256, 768), F32)],
        in_specs=[IN_VMEM, IN_VMEM, IN_HBM, IN_HBM],
        out_specs=[IN_VMEM] * 2,
        scratch_shapes=[pltpu.VMEM((768, 1024), BF)] * 2 + [pltpu.SemaphoreType.DMA((2,))],
        compiler_params=params(16),
        cost_estimate=pl.CostEstimate(flops=1, bytes_accessed=1, transcendentals=0),
        name="edge_back",
    )(dpre, cnt, w_write, w_self)


def weight_kernel(n, cuts, place_ref, *refs):
    outs, turned = refs[-4 * cuts - 1 : -1] if cuts else refs[-2:-1], refs[-1]
    core, y = place_ref[1], place_ref[2]
    dpre = jnp.concatenate([ref[:, pl.ds(ref.shape[1] - 1024, 1024)] for ref in refs[:2]], axis=0)
    wide = 1024 // max(cuts, 1)
    for i in range(n):
        for k in range(2):
            turned[i, :, pl.ds(256 * k, 256)] = refs[2 + 2 * i + k][:, pl.ds(0, 768)].T
        rows = []
        for d in range(4):
            ahead = ((y + d) & 3) if cuts else d
            start = pl.multiple_of((2 * ahead + core) * 96, 32)
            rows.append(turned[i, pl.ds(start, 96), :])
        product = dot(jnp.concatenate(rows, axis=0), dpre).astype(BF)
        if not cuts:
            for d in range(4):
                outs[0][d, i] = product[96 * d : 96 * d + 96]
        for j in range(cuts):
            for d in range(4):
                outs[4 * j + d][i] = product[96 * d : 96 * d + 96, wide * j : wide * j + wide]


def weight_parts(place, dpre, lefts, token, cuts):
    n = len(lefts)
    outs = pl.pallas_call(
        functools.partial(weight_kernel, n, cuts),
        out_shape=[shape((n, 96, 1024 // cuts), BF)] * (4 * cuts) if cuts else [shape((4, n, 96, 1024), BF)],
        in_specs=[IN_SMEM] + [IN_VMEM] * (2 + 2 * n) + [ANYWHERE],
        out_specs=[IN_VMEM] * max(4 * cuts, 1),
        scratch_shapes=[pltpu.VMEM((n, 768, 512), BF)],
        compiler_params=params(24),
        cost_estimate=pl.CostEstimate(flops=1, bytes_accessed=1, transcendentals=0),
        name="weight_parts",
    )(place, *dpre, *[v for pair in lefts for v in pair], token)
    return [outs[4 * j : 4 * j + 4] for j in range(cuts)] if cuts else outs


def y_sum_kernel(place_ref, *refs):
    left, right, authors, outs, stack, turned = refs[:4], refs[4:8], refs[8], refs[9:13], refs[13], refs[14]
    for group, first, rows, lane, wide in ((left, 0, 3, 0, 512), (right, 0, 3, 512, 512), (authors, 3, 2, 0, 1024)):
        for i in range(rows):
            part = (lambda y: group[y, i]) if first else (lambda y: group[y][i])
            total = part(0).astype(F32)
            for y in range(1, 4):
                total = total + part(y).astype(F32)
            stack[pl.ds(96 * (first + i), 96), pl.ds(lane, wide)] = total
    stack[pl.ds(480, 32), :] = jnp.zeros((32, 1024), F32)
    turned[...] = stack[...].T.astype(BF)
    core, x, z = place_ref[1], place_ref[0] >> 2, place_ref[0] & 3
    for d in range(4):
        for j in range(4):
            start = jnp.where(core == 0, ((x + d) & 3) * 256 + j * 64, j * 256 + ((z + d) & 3) * 64)
            outs[d][pl.ds(64 * j, 64), :] = turned[pl.ds(pl.multiple_of(start, 64), 64), :]


def y_sum(place, left, right, author):
    return pl.pallas_call(
        y_sum_kernel,
        out_shape=[shape((256, 512), BF)] * 4,
        in_specs=[IN_SMEM] + [IN_VMEM] * 9,
        out_specs=[IN_VMEM] * 4,
        scratch_shapes=[pltpu.VMEM((512, 1024), F32), pltpu.VMEM((1024, 512), BF)],
        compiler_params=params(20),
        cost_estimate=pl.CostEstimate(flops=1, bytes_accessed=1, transcendentals=0),
        name="y_sum",
    )(place, *left, *right, author)


def x_sum_kernel(place_ref, token_a, token_b, *refs):
    total = refs[0][...].astype(F32)
    for ref in refs[1:4]:
        total = total + ref[...].astype(F32)
    refs[8][...] = total
    at = jnp.where(place_ref[1] == 0, place_ref[0] & 3, place_ref[0] >> 2)
    for d in range(4):
        refs[4 + d][...] = refs[8][pl.ds(pl.multiple_of(((at + d) & 3) * 64, 64), 64), :]


def x_sum(place, got, *tokens):
    return pl.pallas_call(
        x_sum_kernel,
        out_shape=[shape((64, 512), F32)] * 4,
        in_specs=[IN_SMEM, ANYWHERE, ANYWHERE] + [IN_VMEM] * 4,
        out_specs=[IN_VMEM] * 4,
        scratch_shapes=[pltpu.VMEM((256, 512), F32)],
        compiler_params=params(8),
        cost_estimate=pl.CostEstimate(flops=1, bytes_accessed=1, transcendentals=0),
        name="x_sum",
    )(place, *tokens, *got)


def over_col(parts, stage):
    got = [parts[0]]
    for d in range(1, 4):
        perm = []
        for r in range(8):
            for c in range(16):
                x, z = c >> 2, c & 3
                to = ((x + d) % 4) * 4 + z if (r & 1) == stage else x * 4 + (z + d) % 4
                perm.append((r * 16 + c, r * 16 + to))
        got.append(lax.ppermute(parts[d], ("row", "col"), perm))
    return got


def last_sum_kernel(token_ref, *refs):
    total = refs[0][...]
    for ref in refs[1:4]:
        total = total + ref[...]
    total = total * (32768.0 ** -0.5)
    for m in range(5):
        refs[-1][m] = total[:, 96 * m : 96 * m + 96]


def last_sum(got, token):
    return pl.pallas_call(
        last_sum_kernel,
        out_shape=shape((5, 64, 96), F32),
        in_specs=[ANYWHERE] + [IN_VMEM] * 4,
        out_specs=IN_VMEM,
        compiler_params=params(8),
        cost_estimate=pl.CostEstimate(flops=1, bytes_accessed=1, transcendentals=0),
        name="last_sum",
    )(token, *got)


def per_device(
    x_paper, x_author, cite_nbr, write_src, write_dst,
    w_self_paper, w_cite, w_write, w_self_author, w_written, grad_paper, grad_author,
):
    row = lax.axis_index("row")
    place = jnp.stack([lax.axis_index("col"), row & 1, row >> 1]).astype(I32)

    lists = [cite_nbr.T.reshape(1, 16, 256)]
    pairs = travel([x_paper[:128], x_paper[128:]], 0)
    lists = travel(lists, 0)

    pick, into_paper, into_author = edge_lists(write_src[0], write_dst[0])
    arrived = exchange(pick_rows(pick, x_author, x_paper, lists[0][1]))
    parts = join(pairs)
    pairs = travel(parts, 1)
    lists = travel(join(lists), 1)
    x_author_pair = (x_author, other_core(x_author))
    x_paper_pair = (x_paper, other_core(x_paper))

    parts = join(pairs, (lists[0][1],))
    table = cite_table(place, cite_nbr, parts[0])
    parts = join(travel(parts, 2), (table,))
    pairs = travel(parts, 3)
    lists = travel(join(lists), 2)
    cite_first = first_half(table, [pair[0] for pair in pairs])

    out_author, authored, written, dpre_author, dz_written, dx_author_own, pre_paper, adder, cnt = author_step(
        arrived, into_paper, into_author, x_author, x_paper, grad_author,
        w_self_author, w_written, w_self_paper, w_write, parts[0],
    )
    (parts_author,) = weight_parts(
        place, (dpre_author, other_core(dpre_author)),
        [x_author_pair, (authored, other_core(authored))], table, 0,
    )
    got_author = lax.all_to_all(
        parts_author, "row", split_axis=0, concat_axis=0, tiled=True,
        axis_index_groups=[[0, 2, 4, 6], [1, 3, 5, 7]],
    )
    written_pair = (written, other_core(written))

    out_paper, pack, dz_cite = paper_step(
        table, [pair[1] for pair in pairs], cite_first, cite_nbr, pre_paper, grad_paper, w_cite,
        parts_author, written_pair[1], authored,
    )
    back_pairs = travel([dz_cite[:128], dz_cite[128:]], 0)
    dz_write, dx_paper_own = edge_back(pack, cnt, w_write, w_self_paper)
    pack_other = other_core(pack)
    left, right = weight_parts(
        place, (pack, pack_other), [x_paper_pair, (pack, pack_other), written_pair], dz_write, 2,
    )
    parts = join(back_pairs, (left[0], lists[0][1]))
    lists = travel(join(lists), 3)[0]
    pairs = travel(parts, 1)
    left = over_y(left)
    rows = pick_rows(pick, dz_written, dz_write, parts[0])
    back = exchange(rows)
    back_table = cited_by_table(place, lists[0], lists[1], parts[0])
    parts = join(pairs, (back_table, *left[1:]))
    right = over_y(right)
    parts = join(travel(parts, 2), (back_table, *right[1:]))
    dx_author, dx_paper_own = edge_add(adder, back, dx_author_own, dx_paper_own)
    back_pairs = travel(parts, 3)
    back_first = first_half(back_table, [pair[0] for pair in back_pairs])

    got = over_col(y_sum(place, left, right, got_author), 0)
    got = over_col(x_sum(place, got, back_first, dx_author), 1)
    dx_paper = last_half(back_table, [pair[1] for pair in back_pairs], back_first, dx_paper_own)
    dweights = last_sum(got, dx_paper).transpose(0, 2, 1)
    return (out_paper, out_author, dx_paper, dx_author, dweights)


def solution(mesh):
    part = P(("row", "col"), None)
    part3 = P(("row", "col"), None, None)
    return jax.shard_map(
        per_device,
        mesh=mesh,
        in_specs=(part, part, part, part3, part3, P(), P(), P(), P(), P(), part, part),
        out_specs=(part, part, part, part, P(None, "row", "col")),
        check_vma=False,
    )
```
